32 devices in a mesh: grp: 2 (over y), tm: 4 (over z), mod: 4 (over x, core).
Axes of the slice: x: 2, y: 2, z: 4, core: 2. Of those that a mesh axis runs over, the one named last changes fastest.
Arguments:
- phase: float32 [16, 512, 128], P(('grp', 'tm'), 'mod'), parts along dimension 0, may hold values from -4 to 4
- direction: float32 [16, 512, 128], P(('grp', 'tm'), 'mod'), parts along dimension 0, may hold values from -16 to 16
- pupil_mask: int32 [512, 128], replicated, may hold values 0 or 1
- mod_tilts: int32 [4], P('mod'), may hold values from -8 to 8
- wind_codes: int32 [1024, 128], P('grp'), parts along dimension 0, may hold values from 0 to 15
- noise_weight: float32 [16, 1024, 128], P(('grp', 'tm')), parts along dimension 0, may hold values from 0.075 to 0.75
Outputs:
- hess_vec: float32 [16, 512, 128], P(('grp', 'tm'), 'mod'), parts along dimension 0
- curvature: float32 [2], P('grp'), parts along dimension 0
The draws below stay inside these ranges and needn't reach their ends.
There are 2 independent parts, one for each index of `grp`. The reference program is written for one: setup_inputs(seed, part) draws one part's arguments, and reference() takes and returns one part's arrays. A program takes and returns all parts, laid end to end along the dimension named above; an argument that names none is the same for every part. Nothing has to cross between parts.
All inputs are finite; a program needn't handle non-finite values.
Results may differ from the reference program's by a relative error of at most 0.0003.
Values sent between devices are 32-bit elements; how exact they have to be, the bound alone decides.
No kernel may reach another device: no remote copies, remote signals or barrier semaphores. Data moves between devices by JAX's collectives and lax.ppermute only.
A program may use at most 64 MiB of HBM per device.

```python
import math
import jax
import jax.numpy as jnp
from jax import lax

PUPIL = 512
NPIX = 1024
ROWS = 128
FRAMES = 8
MODS = 4
MODR = 8


def draw_direction(key, part):
    shape = (FRAMES, PUPIL, ROWS)
    frame_pos = lax.broadcasted_iota(jnp.float32, shape, 0) / (FRAMES - 1)
    pixel_pos = lax.broadcasted_iota(jnp.float32, shape, 1) / (PUPIL - 1)
    base = jax.random.truncated_normal(key, -4.0, 4.0, shape, jnp.float32)
    ramp = jnp.exp(0.5 * jnp.log(3.0) * (frame_pos + pixel_pos))
    return base * ramp


def touch_ends(drawn, rng, low, top_value):
    longest = drawn.shape.index(max(drawn.shape))
    spots = []
    for shift in (0, 1):
        where = [jax.random.randint(jax.random.fold_in(rng, axis), (), 0, length) for axis, length in enumerate(drawn.shape)]
        where[longest] = (where[longest] + shift) % drawn.shape[longest]
        spots.append(tuple(where))
    return drawn.at[spots[0]].set(low).at[spots[1]].set(top_value)


def level_of(stream_key, dims, shards, least, top_value):
    level = 1.0
    for position, parts in shards:
        draws = jax.random.uniform(jax.random.fold_in(jax.random.fold_in(stream_key, 6), position), (parts,), jnp.float32, least / len(shards), top_value / len(shards))
        level = level * jnp.repeat(jnp.exp(draws), dims[position] // parts).reshape((-1,) + (1,) * (len(dims) - 1 - position))
    return level


def scatter_about(rng, dims, scale, most, shards=(), held_as=jnp.bfloat16):
    drawn = jax.random.normal(rng, dims, jnp.float32) * scale
    if len(shards) > 0:
        drawn = level_of(rng, dims, shards, -0.22, 0.18) * drawn
    return jnp.clip(drawn, min=-most, max=most).astype(held_as)


def setup_inputs(seed: int = 0, part: int = 0) -> dict:
    keys = jax.random.split(jax.random.key(seed), 7)
    own_keys = jax.random.split(jax.random.fold_in(keys[6], part), 7)
    return {
        "phase": scatter_about(own_keys[0], (FRAMES, PUPIL, ROWS), 1.0, 4.0, ((0, 4), (1, 4)), jnp.float32),
        "direction": draw_direction(jax.random.fold_in(jax.random.fold_in(keys[6], part), 71), part),
        "pupil_mask": touch_ends((jax.random.randint(keys[2], (PUPIL, ROWS), 0, 8) < 7).astype(jnp.int32), jax.random.fold_in(keys[2], 1), 0, 1),
        "mod_tilts": touch_ends(jax.random.randint(keys[3], (MODS,), -MODR, MODR + 1), jax.random.fold_in(keys[3], 1), -MODR, MODR).astype(jnp.int32),
        "wind_codes": touch_ends(jax.random.randint(own_keys[4], (PUPIL, ROWS), 0, 16), jax.random.fold_in(own_keys[4], 1), 0, 15).astype(jnp.int32),
        "noise_weight": jnp.clip(jnp.exp(math.log(0.75) - 2.3025851 * jax.random.uniform(own_keys[5], (FRAMES, NPIX, ROWS), jnp.float32) ** level_of(own_keys[5], (FRAMES, NPIX, ROWS), ((0, 4),), -0.2, 0.2)), 0.075, 0.75),
    }


def roof_mask(length, shift_bins):
    freq_index = jnp.arange(length, dtype=jnp.int32)
    signed_freq = jnp.where(freq_index < length // 2, freq_index, freq_index - length)
    turn_counts = (shift_bins * jnp.abs(signed_freq)) % length
    angles = (-2.0 * jnp.pi / length) * turn_counts.astype(jnp.float32)
    return jnp.cos(angles), jnp.sin(angles)


def apply_pyramid(field_real, field_imag, gain_real, gain_imag):
    field = lax.complex(field_real, field_imag)
    spectrum = jnp.fft.fft(field, axis=1)
    gain = lax.complex(gain_real, gain_imag)[None, :, None]
    result = jnp.fft.ifft(spectrum * gain, axis=1)
    return jnp.real(result), jnp.imag(result)


def reference(phase, direction, pupil_mask, mod_tilts, wind_codes, noise_weight):
    frames, pupil_width, row_count = phase.shape
    line_length = 2 * pupil_width
    quarter = pupil_width // 2
    amplitude = pupil_mask.astype(jnp.float32)
    positions = quarter + jnp.arange(pupil_width, dtype=jnp.int32)
    gain_real, gain_imag = roof_mask(line_length, quarter)
    margins = ((0, 0), (quarter, quarter), (0, 0))

    def fields(tilt):
        turn_counts = (tilt * positions) % line_length
        angles = phase + ((2.0 * jnp.pi / line_length) * turn_counts.astype(jnp.float32))[None, :, None]
        return amplitude * jnp.cos(angles), amplitude * jnp.sin(angles)

    def forward(carry, tilt):
        field_real, field_imag = fields(tilt)
        image_real, image_imag = apply_pyramid(jnp.pad(field_real, margins), jnp.pad(field_imag, margins), gain_real, gain_imag)
        push_real, push_imag = apply_pyramid(jnp.pad(-field_imag * direction, margins), jnp.pad(field_real * direction, margins), gain_real, gain_imag)
        return carry + 2.0 * (image_real * push_real + image_imag * push_imag), None

    signal, _ = lax.scan(forward, jnp.zeros((frames, line_length, row_count), jnp.float32), mod_tilts)
    weighted = noise_weight * signal

    def backward(carry, tilt):
        field_real, field_imag = fields(tilt)
        image_real, image_imag = apply_pyramid(jnp.pad(field_real, margins), jnp.pad(field_imag, margins), gain_real, gain_imag)
        back_real, back_imag = apply_pyramid(weighted * image_real, weighted * image_imag, gain_real, -gain_imag)
        back_real = back_real[:, quarter:quarter + pupil_width]
        back_imag = back_imag[:, quarter:quarter + pupil_width]
        return carry - 2.0 * (field_imag * back_real - field_real * back_imag), None

    data_grad, _ = lax.scan(backward, jnp.zeros((frames, pupil_width, row_count), jnp.float32), mod_tilts)

    frac_x = ((wind_codes % 4).astype(jnp.float32) + 0.5) / 4.0
    frac_r = ((wind_codes // 4).astype(jnp.float32) + 0.5) / 4.0
    stay_stay = (1.0 - frac_x) * (1.0 - frac_r)
    ahead_stay = frac_x * (1.0 - frac_r)
    stay_ahead = (1.0 - frac_x) * frac_r
    ahead_ahead = frac_x * frac_r

    def advect(field):
        next_x = jnp.pad(field[:, 1:, :], ((0, 0), (0, 1), (0, 0)))
        next_r = jnp.pad(field[:, :, 1:], ((0, 0), (0, 0), (0, 1)))
        next_both = jnp.pad(field[:, 1:, 1:], ((0, 0), (0, 1), (0, 1)))
        return stay_stay * field + ahead_stay * next_x + stay_ahead * next_r + ahead_ahead * next_both

    def advect_adjoint(field):
        part_one = stay_stay * field
        part_two = jnp.pad((ahead_stay * field)[:, :-1, :], ((0, 0), (1, 0), (0, 0)))
        part_three = jnp.pad((stay_ahead * field)[:, :, :-1], ((0, 0), (0, 0), (1, 0)))
        part_four = jnp.pad((ahead_ahead * field)[:, :-1, :-1], ((0, 0), (1, 0), (1, 0)))
        return part_one + part_two + part_three + part_four

    flow = direction[1:] - advect(direction[:-1])
    prior = jnp.pad(flow, ((1, 0), (0, 0), (0, 0))) - jnp.pad(advect_adjoint(flow), ((0, 1), (0, 0), (0, 0)))
    hess_vec = data_grad + prior
    curvature = (jnp.sum(direction * hess_vec) / float(frames * pupil_width * row_count)).reshape(1)
    return hess_vec, curvature
```

```python
import functools

import jax
import jax.numpy as jnp
import ml_dtypes
import numpy as np
from jax import lax
from jax.experimental import pallas as pl
from jax.experimental.pallas import tpu as pltpu
from jax.sharding import PartitionSpec as P

LANES = 128
SUB = 8
CHUNK = 32
VMEM = pl.BlockSpec(memory_space=pltpu.VMEM)
SMEM = pl.BlockSpec(memory_space=pltpu.SMEM)


def params():
    return pltpu.CompilerParams(vmem_limit_bytes=48 * 1024 * 1024)


class Plan:
    def __init__(self, frames, shard, rows, points, mods):
        self.frames, self.shard, self.rows, self.mods = frames, shard, rows, mods
        self.points = points
        self.pupil = shard * mods
        self.length = 2 * self.pupil
        assert rows == LANES and mods % frames == 0
        self.groups = mods // frames
        self.width = rows // self.groups
        assert 2 * self.width <= LANES
        self.copies = LANES // self.width
        self.total_points = points * mods
        assert self.total_points % self.copies == 0
        self.tiles = self.total_points // self.copies
        self.half = shard // 2
        self.cells = self.pupil // 2
        self.extra = -(-(points + 2 * frames) // SUB) * SUB


def roof_tables(plan):
    cells, length = plan.cells, plan.length
    index = np.arange(cells)
    turned = (index + cells // 2) % cells

    def kernel(gap):
        return 2.0 / length / np.cos(2.0 * np.pi * gap / length)

    even = kernel(2 * turned[:, None] - (2 * index[None, :] + 1))
    odd = kernel(2 * turned[:, None] + 1 - 2 * index[None, :])

    def split(table):
        high = table.astype(ml_dtypes.bfloat16)
        low = (table - high.astype(np.float64)).astype(ml_dtypes.bfloat16)
        return np.concatenate([high, high, low], axis=1)

    return split(even), split(odd), split(even.T), split(odd.T)


def spread(cells, plan, first):
    lane = lax.broadcasted_iota(jnp.int32, cells.shape, 1)
    width = plan.width
    if 2 * width == LANES:
        other = pltpu.roll(cells, width, 1)
        keep = (lane < width) if first == 0 else (lane >= width)
        return jnp.where(keep, cells, other)
    if first:
        cells = pltpu.roll(cells, LANES - first, 1)
    cells = jnp.where(lane < width, cells, 0.0)
    step = width
    while step < LANES:
        cells = cells + pltpu.roll(cells, step, 1)
        step *= 2
    return cells


def lane_sum(cells, plan):
    step = plan.width
    while step < LANES:
        cells = cells + pltpu.roll(cells, step, 1)
        step *= 2
    return cells


def pack_kernel(plan, me_ref, tilt_ref, phase_ref, direction_ref, *outs):
    me = me_ref[0]
    width, half, shard = plan.width, plan.half, plan.shard
    lane = lax.broadcasted_iota(jnp.int32, (half, LANES), 1)
    for k, out in enumerate(outs):
        dest = me ^ k
        frame, group = dest // plan.groups, dest % plan.groups
        back = (LANES - group * width) % LANES
        ahead = (LANES + width - group * width) % LANES
        for parity in range(2):
            own = pl.ds(parity, half, stride=2)
            one = pltpu.roll(phase_ref[frame, own, :], back, 1)
            two = pltpu.roll(direction_ref[frame, own, :], ahead, 1)
            out[parity * half : (parity + 1) * half, :] = jnp.where(lane < width, one, two)
        rows = [jnp.full((1, LANES), tilt_ref[p], jnp.int32).astype(jnp.float32) for p in range(plan.points)]
        for f in range(plan.frames):
            rows += [direction_ref[f, 0:1, :], direction_ref[f, shard - 1 : shard, :]]
        rows += [jnp.zeros((1, LANES), jnp.float32)] * (plan.extra - len(rows))
        out[shard : shard + plan.extra, :] = jnp.concatenate(rows, axis=0)


def wave(turns):
    quarters = jnp.round(turns * 4.0)
    angle = (turns - quarters * 0.25) * (2.0 * np.pi)
    square = angle * angle
    sin_part = ((-1.9515295891e-4 * square + 8.3321608736e-3) * square - 1.6666654611e-1) * square * angle + angle
    cos_part = (
        (2.443315711809948e-5 * square - 1.388731625493765e-3) * square + 4.166664568298827e-2
    ) * (square * square) + (1.0 - 0.5 * square)
    count = quarters.astype(jnp.int32)
    odd = (count & 1) != 0
    cosine = jnp.where(odd, sin_part, cos_part)
    sine = jnp.where(odd, cos_part, sin_part)
    cosine = jnp.where(((count + 1) & 2) != 0, -cosine, cosine)
    sine = jnp.where((count & 2) != 0, -sine, sine)
    return cosine, sine


def put_split(ref, parity, row, rows, cells, column, value):
    high = value.astype(jnp.bfloat16)
    low = (value - high.astype(jnp.float32)).astype(jnp.bfloat16)
    where = slice(column, column + LANES)
    ref[parity, row : row + rows, where] = high
    ref[parity, cells + row : cells + row + rows, where] = low
    ref[parity, 2 * cells + row : 2 * cells + row + rows, where] = high


def main_kernel(plan, me_ref, *refs):
    mods, half, cells, width = plan.mods, plan.half, plan.cells, plan.width
    tiles, wide = plan.tiles, plan.tiles * LANES
    pieces = refs[:mods]
    mask_ref, noise_ref, even_ref, odd_ref, even_back_ref, odd_back_ref, prev_ref, next_ref, flow_ref = refs[mods : mods + 9]
    outs = refs[mods + 9 : 2 * mods + 9]
    turn_ref, dir_ref, cos_ref, sin_ref, in_ref, image_ref, fold_ref, grad_ref = refs[2 * mods + 9 :]
    me = me_ref[0]
    frame, group = me // plan.groups, me % plan.groups
    group_back = (LANES - group * width) % LANES
    lane_row = lax.broadcasted_iota(jnp.int32, (1, LANES), 1)

    for k, piece in enumerate(pieces):
        place = pl.ds(pl.multiple_of((me ^ k) * half, SUB), half)
        for parity in range(2):
            cells_in = piece[parity * half : (parity + 1) * half, :]
            turn_ref[parity, place, :] = spread(cells_in, plan, 0) * (0.5 / np.pi)
            dir_ref[parity, place, :] = spread(cells_in, plan, width)

    tilt_rows = [jnp.zeros((1, LANES), jnp.float32)] * tiles
    for k, piece in enumerate(pieces):
        for p in range(plan.points):
            tile, slot = divmod(k * plan.points + p, plan.copies)
            row = piece[plan.shard + p : plan.shard + p + 1, :]
            tilt_rows[tile] = jnp.where(lane_row // width == slot, row, tilt_rows[tile])

    for parity in range(2):
        for row in range(0, cells, CHUNK):
            here = slice(row, row + CHUNK)
            turns = turn_ref[parity, here, :]
            push = dir_ref[parity, here, :]
            picked = mask_ref[pl.ds(2 * row + parity, CHUNK, stride=2), :].astype(jnp.float32)
            mask = spread(pltpu.roll(picked, group_back, 1), plan, 0)
            spots = lax.broadcasted_iota(jnp.int32, (CHUNK, LANES), 0)
            spots = (2 * (spots + row) + (parity + plan.pupil // 2)).astype(jnp.float32) / plan.length
            for tile in range(tiles):
                tilt = spots * tilt_rows[tile]
                cosine, sine = wave(turns + (tilt - jnp.round(tilt)))
                cosine, sine = cosine * mask, sine * mask
                at = tile * LANES
                cos_ref[parity, here, at : at + LANES] = cosine
                sin_ref[parity, here, at : at + LANES] = sine
                put_split(in_ref, parity, row, CHUNK, cells, at, cosine)
                put_split(in_ref, parity, row, CHUNK, cells, wide + at, sine)
                put_split(in_ref, parity, row, CHUNK, cells, 2 * wide + at, -sine * push)
                put_split(in_ref, parity, row, CHUNK, cells, 3 * wide + at, cosine * push)

    for parity, table in enumerate((even_ref, odd_ref)):
        image_ref[parity] = jnp.dot(table[...], in_ref[1 - parity], preferred_element_type=jnp.float32)

    total = jnp.zeros((SUB, LANES), jnp.float32)
    quarter = cells // 2
    for parity in range(2):
        for row in range(0, cells, CHUNK):
            here = slice(row, row + CHUNK)
            push = dir_ref[parity, here, :]
            even_sum = odd_sum = shift = 0.0
            for tile in range(tiles):
                at = tile * LANES
                cosine = cos_ref[parity, here, at : at + LANES]
                sine = sin_ref[parity, here, at : at + LANES]
                image_cos, image_sin, push_real, push_imag = [
                    image_ref[parity, here, q * wide + at : q * wide + at + LANES] for q in range(4)
                ]
                even_sum += image_sin * push_imag + image_cos * push_real
                odd_sum += cosine * (push_imag - push * image_cos) - sine * (push_real + push * image_sin)
                shift += cosine * image_cos + sine * image_sin
            even_sum = lane_sum(even_sum, plan) * 2.0
            odd_sum = lane_sum(odd_sum, plan)
            signal_after, signal_before = even_sum + odd_sum, even_sum - odd_sum
            inner = row % quarter
            low_half = row < quarter
            after_at = (2 if low_half else 1) * (plan.pupil // 2) + 2 * inner + parity
            before_at = (0 if low_half else 3) * (plan.pupil // 2) + 2 * inner + parity
            noise_after, noise_before = [
                spread(pltpu.roll(noise_ref[frame, pl.ds(first, CHUNK, stride=2), :], group_back, 1), plan, 0)
                for first in (after_at, before_at)
            ]
            weighted_after, weighted_before = noise_after * signal_after, noise_before * signal_before
            squares = weighted_after * signal_after + weighted_before * signal_before
            for r in range(0, CHUNK, SUB):
                total += squares[r : r + SUB]
            both = weighted_after + weighted_before
            gap = (weighted_after - weighted_before) * 0.5
            grad_ref[parity, here, :] = -gap * shift
            for tile in range(tiles):
                at = tile * LANES
                cosine = cos_ref[parity, here, at : at + LANES]
                sine = sin_ref[parity, here, at : at + LANES]
                image_cos = image_ref[parity, here, at : at + LANES]
                image_sin = image_ref[parity, here, wide + at : wide + at + LANES]
                put_split(fold_ref, parity, row, CHUNK, cells, at, gap * cosine + both * image_sin)
                put_split(fold_ref, parity, row, CHUNK, cells, wide + at, gap * sine - both * image_cos)

    for parity, table in enumerate((odd_back_ref, even_back_ref)):
        image_ref[parity, :, : 2 * wide] = jnp.dot(table[...], fold_ref[1 - parity], preferred_element_type=jnp.float32)

    for row in range(0, cells, CHUNK):
        here = slice(row, row + CHUNK)
        grads = []
        for parity in range(2):
            grad = grad_ref[parity, here, :]
            for tile in range(tiles):
                at = tile * LANES
                grad += cos_ref[parity, here, at : at + LANES] * image_ref[parity, here, at : at + LANES]
                grad += sin_ref[parity, here, at : at + LANES] * image_ref[parity, here, wide + at : wide + at + LANES]
            grads.append(lane_sum(grad, plan) * 2.0)
        lane = lax.broadcasted_iota(jnp.int32, (CHUNK, LANES), 1)
        grad_ref[0, here, :] = jnp.where(lane < width, grads[0], grads[1])

    total = jnp.sum(total, axis=0, keepdims=True) / plan.copies + jnp.sum(flow_ref[...], axis=0, keepdims=True)
    rows = [total, prev_ref[0:1, :], next_ref[plan.shard - 1 : plan.shard, :]]
    rows += [jnp.zeros((1, LANES), jnp.float32)] * (SUB - len(rows))
    tail = jnp.concatenate(rows, axis=0)
    for k, out in enumerate(outs):
        place = pl.ds(pl.multiple_of((me ^ k) * half, SUB), half)
        out[0:half, :] = grad_ref[0, place, :]
        out[half : half + SUB, :] = tail


def row_ahead(cells):
    lane = lax.broadcasted_iota(jnp.int32, cells.shape, 1)
    return jnp.where(lane == LANES - 1, 0.0, pltpu.roll(cells, LANES - 1, 1))


def row_behind(cells):
    lane = lax.broadcasted_iota(jnp.int32, cells.shape, 1)
    return jnp.where(lane == 0, 0.0, pltpu.roll(cells, 1, 1))


def shares(codes):
    ahead_x = ((codes % 4).astype(jnp.float32) + 0.5) / 4.0
    ahead_r = ((codes // 4).astype(jnp.float32) + 0.5) / 4.0
    return (1.0 - ahead_x) * (1.0 - ahead_r), ahead_x * (1.0 - ahead_r), (1.0 - ahead_x) * ahead_r, ahead_x * ahead_r


def prior_kernel(plan, total_frames, place_ref, *refs):
    mods, shard, frames = plan.mods, plan.shard, plan.frames
    pieces = refs[: mods - 1]
    direction_ref, prev_ref, next_ref, codes_ref, prior_ref, flow_ref, coef_ref = refs[mods - 1 :]
    me, first_frame = place_ref[0], place_ref[1]
    zero_row = jnp.zeros((1, LANES), jnp.float32)

    below = [zero_row] * (frames + 2)
    above = [zero_row] * (frames + 2)
    for k in range(1, mods):
        source = me ^ k
        for f in range(frames):
            at = shard + plan.points + 2 * f
            above[f + 1] = jnp.where(source == me + 1, pieces[k - 1][at : at + 1, :], above[f + 1])
            below[f + 1] = jnp.where(source == me - 1, pieces[k - 1][at + 1 : at + 2, :], below[f + 1])

    cells = [prev_ref[...]] + [direction_ref[f] for f in range(frames)] + [next_ref[...]]
    row_id = lax.broadcasted_iota(jnp.int32, (shard, LANES), 0)

    def from_next(body, last):
        return jnp.where(row_id == shard - 1, last, pltpu.roll(body, shard - 1, 0))

    def from_last(body, first):
        return jnp.where(row_id == 0, first, pltpu.roll(body, 1, 0))

    begin = pl.multiple_of(me * shard, SUB)
    coef = shares(codes_ref[pl.ds(begin, shard), :])
    before = pl.multiple_of(jnp.maximum(begin - SUB, 0), SUB)
    edge = [jnp.where(me > 0, c[SUB - 1 : SUB], 0.0) for c in shares(codes_ref[pl.ds(before, SUB), :])]

    def moved(share, base, ahead):
        return share[0] * base + share[1] * ahead + share[2] * row_ahead(base) + share[3] * row_ahead(ahead)

    flow, flow_edge = [], []
    for t in range(frames + 1):
        frame = first_frame + t - 1
        valid = (frame >= 0) & (frame <= total_frames - 2)
        ahead = from_next(cells[t], above[t])
        flow.append(jnp.where(valid, cells[t + 1] - moved(coef, cells[t], ahead), 0.0))
        if t > 0:
            value = below[t + 1] - moved(edge, below[t], cells[t][0:1])
            flow_edge.append(jnp.where(valid & (me > 0), value, 0.0))
    total = jnp.zeros((SUB, LANES), jnp.float32)
    for t in range(frames):
        square = flow[t + 1] * flow[t + 1]
        for r in range(0, shard, SUB):
            total += square[r : r + SUB]
        base, side = flow[t + 1], flow_edge[t]
        spread_to = (
            coef[0] * base
            + from_last(coef[1] * base, edge[1] * side)
            + row_behind(coef[2] * base + from_last(coef[3] * base, edge[3] * side))
        )
        prior_ref[t] = flow[t] - spread_to
    flow_ref[...] = total
    rows = [coef[1][shard - 1 : shard], coef[3][shard - 1 : shard], edge[1], edge[3]]
    rows += [zero_row] * (SUB - len(rows))
    coef_ref[...] = jnp.concatenate(rows, axis=0)


def final_kernel(plan, me_ref, *refs):
    mods, half, width, shard = plan.mods, plan.half, plan.width, plan.shard
    pieces = refs[:mods]
    prior_ref, coef_ref, hess_ref, sum_ref = refs[mods : mods + 4]
    me = me_ref[0]
    lane = lax.broadcasted_iota(jnp.int32, (half, LANES), 1)
    for parity in range(2):
        own = pl.ds(parity, half, stride=2)
        for f in range(plan.frames):
            hess_ref[f, own, :] = prior_ref[f, own, :]
        for k, piece in enumerate(pieces):
            source = me ^ k
            frame, group = source // plan.groups, source % plan.groups
            turn = (group * width - parity * width + LANES) % LANES
            moved = pltpu.roll(piece[0:half, :], turn, 1)
            hess_ref[frame, own, :] += jnp.where(lane // width == group, moved, 0.0)
    zero_row = jnp.zeros((1, LANES), jnp.float32)
    total, above, below = zero_row, zero_row, zero_row
    for k, piece in enumerate(pieces):
        source = me ^ k
        total += piece[half : half + 1, :]
        above = jnp.where(source == me + 1, piece[half + 1 : half + 2, :], above)
        below = jnp.where(source == me - 1, piece[half + 2 : half + 3, :], below)
    hess_ref[0, shard - 1 : shard, :] -= coef_ref[0:1, :] * above + coef_ref[1:2, :] * row_ahead(above)
    hess_ref[plan.frames - 1, 0:1, :] -= coef_ref[2:3, :] * below + row_behind(coef_ref[3:4, :] * below)
    sum_ref[...] = jnp.broadcast_to(total, (SUB, LANES))


def exchange(arrays, axis):
    count = lax.axis_size(axis)
    return [arrays[0]] + [
        lax.ppermute(arrays[k], axis, [(i, i ^ k) for i in range(count)]) for k in range(1, count)
    ]


def per_device(phase, direction, pupil_mask, mod_tilts, wind_codes, noise_weight):
    frames, shard, rows = phase.shape
    mods, steps = lax.axis_size("mod"), lax.axis_size("tm")
    plan = Plan(frames, shard, rows, mod_tilts.shape[0], mods)
    f32 = jnp.float32
    me = lax.axis_index("mod").astype(jnp.int32).reshape(1)
    place = jnp.stack([lax.axis_index("mod"), lax.axis_index("tm") * frames]).astype(jnp.int32)
    total_frames = frames * steps

    packed = pl.pallas_call(
        functools.partial(pack_kernel, plan),
        out_shape=[jax.ShapeDtypeStruct((shard + plan.extra, LANES), f32)] * mods,
        in_specs=[SMEM, SMEM, VMEM, VMEM],
        out_specs=[VMEM] * mods,
        compiler_params=params(),
        name="pack",
    )(me, mod_tilts, phase, direction)
    pieces = exchange(packed, "mod")
    prev_frame = lax.ppermute(direction[-1], "tm", [(i, i + 1) for i in range(steps - 1)])
    next_frame = lax.ppermute(direction[0], "tm", [(i + 1, i) for i in range(steps - 1)])

    prior, flow_total, coef = pl.pallas_call(
        functools.partial(prior_kernel, plan, total_frames),
        out_shape=[
            jax.ShapeDtypeStruct(phase.shape, f32),
            jax.ShapeDtypeStruct((SUB, LANES), f32),
            jax.ShapeDtypeStruct((SUB, LANES), f32),
        ],
        in_specs=[SMEM] + [VMEM] * (mods + 3),
        out_specs=[VMEM] * 3,
        compiler_params=params(),
        name="prior",
    )(place, *pieces[1:], direction, prev_frame, next_frame, wind_codes)

    tables = [jnp.asarray(t) for t in roof_tables(plan)]
    cells, wide = plan.cells, plan.tiles * LANES
    grads = pl.pallas_call(
        functools.partial(main_kernel, plan),
        out_shape=[jax.ShapeDtypeStruct((plan.half + SUB, LANES), f32)] * mods,
        in_specs=[SMEM] + [VMEM] * (mods + 9),
        out_specs=[VMEM] * mods,
        scratch_shapes=[
            pltpu.VMEM((2, cells, LANES), f32),
            pltpu.VMEM((2, cells, LANES), f32),
            pltpu.VMEM((2, cells, wide), f32),
            pltpu.VMEM((2, cells, wide), f32),
            pltpu.VMEM((2, 3 * cells, 4 * wide), jnp.bfloat16),
            pltpu.VMEM((2, cells, 4 * wide), f32),
            pltpu.VMEM((2, 3 * cells, 2 * wide), jnp.bfloat16),
            pltpu.VMEM((2, cells, LANES), f32),
        ],
        compiler_params=params(),
        name="data_term",
    )(me, *pieces, pupil_mask, noise_weight, *tables, prev_frame, next_frame, flow_total)
    returned = exchange(grads, "mod")

    hess_vec, mod_total = pl.pallas_call(
        functools.partial(final_kernel, plan),
        out_shape=[jax.ShapeDtypeStruct(phase.shape, f32), jax.ShapeDtypeStruct((SUB, LANES), f32)],
        in_specs=[SMEM] + [VMEM] * (mods + 2),
        out_specs=[VMEM] * 2,
        compiler_params=params(),
        name="join",
    )(me, *returned, prior, coef)
    group_total = sum(exchange([mod_total] * steps, "tm"))
    curvature = (jnp.sum(group_total[0]) / float(total_frames * plan.pupil * rows)).reshape(1)
    return hess_vec, curvature


def solution(mesh):
    return jax.shard_map(
        per_device,
        mesh=mesh,
        in_specs=(
            P(("grp", "tm"), "mod", None),
            P(("grp", "tm"), "mod", None),
            P(),
            P("mod"),
            P("grp", None),
            P(("grp", "tm"), None, None),
        ),
        out_specs=(P(("grp", "tm"), "mod", None), P("grp")),
        check_vma=False,
    )
```

```python
import functools

import jax
import jax.numpy as jnp
import ml_dtypes
import numpy as np
from jax import lax
from jax.experimental import pallas as pl
from jax.experimental.pallas import tpu as pltpu
from jax.sharding import PartitionSpec as P

LANES = 128
SUB = 8
CHUNK = 32
VMEM = pl.BlockSpec(memory_space=pltpu.VMEM)
SMEM = pl.BlockSpec(memory_space=pltpu.SMEM)
HBM = pl.BlockSpec(memory_space=pltpu.HBM)


def params():
    return pltpu.CompilerParams(vmem_limit_bytes=48 * 1024 * 1024)


class Plan:
    def __init__(self, frames, shard, rows, points, mods):
        self.frames, self.shard, self.rows, self.mods = frames, shard, rows, mods
        self.points = points
        self.pupil = shard * mods
        self.length = 2 * self.pupil
        assert rows == LANES and mods % frames == 0
        self.groups = mods // frames
        self.width = rows // self.groups
        assert 2 * self.width <= LANES
        self.copies = LANES // self.width
        self.total_points = points * mods
        assert self.total_points % self.copies == 0
        self.tiles = self.total_points // self.copies
        self.half = shard // 2
        self.cells = self.pupil // 2
        self.extra = -(-(points + 2 * frames) // SUB) * SUB


def roof_tables(plan):
    cells, length = plan.cells, plan.length
    index = np.arange(cells)
    turned = (index + cells // 2) % cells

    def kernel(gap):
        return 2.0 / length / np.cos(2.0 * np.pi * gap / length)

    even = kernel(2 * turned[:, None] - (2 * index[None, :] + 1))
    odd = kernel(2 * turned[:, None] + 1 - 2 * index[None, :])

    def split(table):
        high = table.astype(ml_dtypes.bfloat16)
        low = (table - high.astype(np.float64)).astype(ml_dtypes.bfloat16)
        return np.concatenate([high, high, low], axis=1)

    return split(even), split(odd), split(even.T), split(odd.T)


def spread(cells, plan, first):
    lane = lax.broadcasted_iota(jnp.int32, cells.shape, 1)
    width = plan.width
    if 2 * width == LANES:
        other = pltpu.roll(cells, width, 1)
        keep = (lane < width) if first == 0 else (lane >= width)
        return jnp.where(keep, cells, other)
    if first:
        cells = pltpu.roll(cells, LANES - first, 1)
    cells = jnp.where(lane < width, cells, 0.0)
    step = width
    while step < LANES:
        cells = cells + pltpu.roll(cells, step, 1)
        step *= 2
    return cells


def lane_sum(cells, plan):
    step = plan.width
    while step < LANES:
        cells = cells + pltpu.roll(cells, step, 1)
        step *= 2
    return cells


def place_on(axis):
    return lax.axis_index(axis)


def pack_kernel(plan, tilt_hbm, phase_hbm, direction_hbm, *refs):
    mods = plan.mods
    outs = refs[:mods]
    direction_ref, first_ref, second_ref, phase_ref, tilt_ref, sems = refs[mods:]
    loads = [
        pltpu.make_async_copy(source, target, sems.at[i])
        for i, (source, target) in enumerate(
            ((direction_hbm, direction_ref), (phase_hbm, phase_ref), (tilt_hbm, tilt_ref))
        )
    ]
    for load in loads:
        load.start()
    me, step = place_on("mod"), place_on("tm")
    width, half, shard, frames = plan.width, plan.half, plan.shard, plan.frames
    lane = lax.broadcasted_iota(jnp.int32, (half, LANES), 1)
    for load in loads:
        load.wait()
    for k, out in enumerate(outs):
        dest = me ^ k
        frame, group = dest // plan.groups, dest % plan.groups
        back = (LANES - group * width) % LANES
        ahead = (LANES + width - group * width) % LANES
        for parity in range(2):
            own = pl.ds(parity, half, stride=2)
            one = pltpu.roll(phase_ref[frame, own, :], back, 1)
            two = pltpu.roll(direction_ref[frame, own, :], ahead, 1)
            out[parity * half : (parity + 1) * half, :] = jnp.where(lane < width, one, two)
        rows = [jnp.full((1, LANES), tilt_ref[p], jnp.int32).astype(jnp.float32) for p in range(plan.points)]
        for f in range(frames):
            rows += [direction_ref[f, 0:1, :], direction_ref[f, shard - 1 : shard, :]]
        rows += [jnp.zeros((1, LANES), jnp.float32)] * (plan.extra - len(rows))
        out[shard : shard + plan.extra, :] = jnp.concatenate(rows, axis=0)
    even = step % 2 == 0
    first_ref[...] = direction_ref[jnp.where(even, frames - 1, 0)]
    second_ref[...] = direction_ref[jnp.where(even, 0, frames - 1)]


def prep_kernel(plan, seed_ref, mask_hbm, noise_hbm, codes_hbm, *refs):
    tables_hbm, refs = refs[:4], refs[4:]
    tables, (mask_out, noise_out, coef_out, edge_out), refs = refs[:4], refs[4:8], refs[8:]
    mask_ref, noise_ref, codes_ref, sems = refs
    me = place_on("mod")
    shard, cells, quarter_line = plan.shard, plan.cells, plan.pupil // 2
    frame, group = me // plan.groups, me % plan.groups
    group_back = (LANES - group * plan.width) % LANES
    begin = pl.multiple_of(me * shard, SUB)
    before = pl.multiple_of(jnp.maximum(begin - SUB, 0), SUB)
    pairs = [
        (mask_hbm, mask_ref),
        (noise_hbm.at[frame], noise_ref),
        (codes_hbm.at[pl.ds(before, SUB)], codes_ref.at[0:SUB]),
        (codes_hbm.at[pl.ds(begin, shard)], codes_ref.at[SUB : SUB + shard]),
    ] + list(zip(tables_hbm, tables))
    loads = [pltpu.make_async_copy(source, target, sems.at[i]) for i, (source, target) in enumerate(pairs)]
    for load in loads:
        load.start()

    def own_rows(cells_in):
        return spread(pltpu.roll(cells_in, group_back, 1), plan, 0)

    loads[0].wait()
    for parity in range(2):
        for row in range(0, cells, CHUNK):
            picked = mask_ref[pl.ds(2 * row + parity, CHUNK, stride=2), :].astype(jnp.float32)
            mask_out[parity, row : row + CHUNK, :] = own_rows(picked)
    loads[1].wait()
    for parity in range(2):
        for row in range(0, cells, CHUNK):
            low_half = row < cells // 2
            inner = 2 * (row % (cells // 2)) + parity
            for side, block in enumerate((2, 0) if low_half else (1, 3)):
                picked = noise_ref[pl.ds(block * quarter_line + inner, CHUNK, stride=2), :]
                noise_out[side, parity, row : row + CHUNK, :] = own_rows(picked)
    loads[2].wait()
    loads[3].wait()
    for i, share in enumerate(shares(codes_ref[SUB : SUB + shard, :])):
        coef_out[i] = share
    for i, share in enumerate(shares(codes_ref[0:SUB, :])):
        edge_out[i] = jnp.where(me > 0, share, 0.0)
    for load in loads[4:]:
        load.wait()


def wave(turns):
    quarters = jnp.round(turns * 4.0)
    angle = (turns - quarters * 0.25) * (2.0 * np.pi)
    square = angle * angle
    sin_part = ((-1.9515295891e-4 * square + 8.3321608736e-3) * square - 1.6666654611e-1) * square * angle + angle
    cos_part = (
        (2.443315711809948e-5 * square - 1.388731625493765e-3) * square + 4.166664568298827e-2
    ) * (square * square) + (1.0 - 0.5 * square)
    count = quarters.astype(jnp.int32)
    odd = (count & 1) != 0
    cosine = jnp.where(odd, sin_part, cos_part)
    sine = jnp.where(odd, cos_part, sin_part)
    cosine = jnp.where(((count + 1) & 2) != 0, -cosine, cosine)
    sine = jnp.where((count & 2) != 0, -sine, sine)
    return cosine, sine


def put_split(ref, parity, row, rows, cells, column, value):
    high = value.astype(jnp.bfloat16)
    low = (value - high.astype(jnp.float32)).astype(jnp.bfloat16)
    where = slice(column, column + LANES)
    ref[parity, row : row + rows, where] = high
    ref[parity, cells + row : cells + row + rows, where] = low
    ref[parity, 2 * cells + row : 2 * cells + row + rows, where] = high


def forward_kernel(plan, *refs):
    mods, half, cells = plan.mods, plan.half, plan.cells
    tiles, wide = plan.tiles, plan.tiles * LANES
    pieces = refs[:mods]
    mask_ref, noise_ref, even_ref, odd_ref, flow_ref = refs[mods : mods + 5]
    cos_ref, sin_ref, fold_ref, grad_ref, total_ref = refs[mods + 5 : mods + 10]
    turn_ref, dir_ref, in_ref, image_ref = refs[mods + 10 :]
    me = place_on("mod")
    lane_row = lax.broadcasted_iota(jnp.int32, (1, LANES), 1)

    for k, piece in enumerate(pieces):
        place = pl.ds(pl.multiple_of((me ^ k) * half, SUB), half)
        for parity in range(2):
            cells_in = piece[parity * half : (parity + 1) * half, :]
            turn_ref[parity, place, :] = spread(cells_in, plan, 0) * (0.5 / np.pi)
            dir_ref[parity, place, :] = spread(cells_in, plan, plan.width)

    tilt_rows = [jnp.zeros((1, LANES), jnp.float32)] * tiles
    for k, piece in enumerate(pieces):
        for p in range(plan.points):
            tile, slot = divmod(k * plan.points + p, plan.copies)
            row = piece[plan.shard + p : plan.shard + p + 1, :]
            tilt_rows[tile] = jnp.where(lane_row // plan.width == slot, row, tilt_rows[tile])

    for parity in range(2):
        for row in range(0, cells, CHUNK):
            here = slice(row, row + CHUNK)
            turns = turn_ref[parity, here, :]
            push = dir_ref[parity, here, :]
            mask = mask_ref[parity, here, :]
            spots = lax.broadcasted_iota(jnp.int32, (CHUNK, LANES), 0)
            spots = (2 * (spots + row) + (parity + plan.pupil // 2)).astype(jnp.float32) / plan.length
            for tile in range(tiles):
                tilt = spots * tilt_rows[tile]
                cosine, sine = wave(turns + (tilt - jnp.round(tilt)))
                cosine, sine = cosine * mask, sine * mask
                at = tile * LANES
                cos_ref[parity, here, at : at + LANES] = cosine
                sin_ref[parity, here, at : at + LANES] = sine
                put_split(in_ref, parity, row, CHUNK, cells, at, cosine)
                put_split(in_ref, parity, row, CHUNK, cells, wide + at, sine)
                put_split(in_ref, parity, row, CHUNK, cells, 2 * wide + at, -sine * push)
                put_split(in_ref, parity, row, CHUNK, cells, 3 * wide + at, cosine * push)

    for parity, table in enumerate((even_ref, odd_ref)):
        image_ref[parity] = jnp.dot(table[...], in_ref[1 - parity], preferred_element_type=jnp.float32)

    total = jnp.zeros((SUB, LANES), jnp.float32)
    for parity in range(2):
        for row in range(0, cells, CHUNK):
            here = slice(row, row + CHUNK)
            push = dir_ref[parity, here, :]
            even_sum = odd_sum = shift = 0.0
            for tile in range(tiles):
                at = tile * LANES
                cosine = cos_ref[parity, here, at : at + LANES]
                sine = sin_ref[parity, here, at : at + LANES]
                image_cos, image_sin, push_real, push_imag = [
                    image_ref[parity, here, q * wide + at : q * wide + at + LANES] for q in range(4)
                ]
                even_sum += image_sin * push_imag + image_cos * push_real
                odd_sum += cosine * (push_imag - push * image_cos) - sine * (push_real + push * image_sin)
                shift += cosine * image_cos + sine * image_sin
            even_sum = lane_sum(even_sum, plan) * 2.0
            odd_sum = lane_sum(odd_sum, plan)
            signal_after, signal_before = even_sum + odd_sum, even_sum - odd_sum
            weighted_after = noise_ref[0, parity, here, :] * signal_after
            weighted_before = noise_ref[1, parity, here, :] * signal_before
            squares = weighted_after * signal_after + weighted_before * signal_before
            for r in range(0, CHUNK, SUB):
                total += squares[r : r + SUB]
            both = weighted_after + weighted_before
            gap = (weighted_after - weighted_before) * 0.5
            grad_ref[parity, here, :] = -gap * shift
            for tile in range(tiles):
                at = tile * LANES
                cosine = cos_ref[parity, here, at : at + LANES]
                sine = sin_ref[parity, here, at : at + LANES]
                image_cos = image_ref[parity, here, at : at + LANES]
                image_sin = image_ref[parity, here, wide + at : wide + at + LANES]
                put_split(fold_ref, parity, row, CHUNK, cells, at, gap * cosine + both * image_sin)
                put_split(fold_ref, parity, row, CHUNK, cells, wide + at, gap * sine - both * image_cos)
    total_ref[...] = total / plan.copies + flow_ref[...]


def backward_kernel(plan, cos_ref, sin_ref, fold_ref, start_ref, even_ref, odd_ref, grad_ref, image_ref):
    cells, tiles, wide = plan.cells, plan.tiles, plan.tiles * LANES
    for parity, table in enumerate((odd_ref, even_ref)):
        image_ref[parity] = jnp.dot(table[...], fold_ref[1 - parity], preferred_element_type=jnp.float32)
    lane = lax.broadcasted_iota(jnp.int32, (CHUNK, LANES), 1)
    for row in range(0, cells, CHUNK):
        here = slice(row, row + CHUNK)
        grads = []
        for parity in range(2):
            grad = start_ref[parity, here, :]
            for tile in range(tiles):
                at = tile * LANES
                grad += cos_ref[parity, here, at : at + LANES] * image_ref[parity, here, at : at + LANES]
                grad += sin_ref[parity, here, at : at + LANES] * image_ref[parity, here, wide + at : wide + at + LANES]
            grads.append(lane_sum(grad, plan) * 2.0)
        grad_ref[here, :] = jnp.where(lane < plan.width, grads[0], grads[1])


def send_kernel(plan, steps, *refs):
    half = plan.half
    totals, (grad_ref, prev_ref, next_ref), outs = refs[:steps], refs[steps : steps + 3], refs[steps + 3 :]
    me = place_on("mod")
    total = totals[0][...]
    for other in totals[1:]:
        total += other[...]
    rows = [jnp.sum(total, axis=0, keepdims=True), prev_ref[0:1, :], next_ref[plan.shard - 1 : plan.shard, :]]
    rows += [jnp.zeros((1, LANES), jnp.float32)] * (SUB - len(rows))
    tail = jnp.concatenate(rows, axis=0)
    for k, out in enumerate(outs):
        place = pl.ds(pl.multiple_of((me ^ k) * half, SUB), half)
        out[0:half, :] = grad_ref[place, :]
        out[half : half + SUB, :] = tail


def row_ahead(cells):
    lane = lax.broadcasted_iota(jnp.int32, cells.shape, 1)
    return jnp.where(lane == LANES - 1, 0.0, pltpu.roll(cells, LANES - 1, 1))


def row_behind(cells):
    lane = lax.broadcasted_iota(jnp.int32, cells.shape, 1)
    return jnp.where(lane == 0, 0.0, pltpu.roll(cells, 1, 1))


def shares(codes):
    ahead_x = ((codes % 4).astype(jnp.float32) + 0.5) / 4.0
    ahead_r = ((codes // 4).astype(jnp.float32) + 0.5) / 4.0
    return (1.0 - ahead_x) * (1.0 - ahead_r), ahead_x * (1.0 - ahead_r), (1.0 - ahead_x) * ahead_r, ahead_x * ahead_r


def prior_kernel(plan, steps, *refs):
    mods, shard, frames = plan.mods, plan.shard, plan.frames
    pieces, refs = refs[: mods - 1], refs[mods - 1 :]
    direction_ref, first_ref, second_ref, coef_ref, edge_ref, prior_ref, flow_ref, prev_ref, next_ref = refs
    me, step = place_on("mod"), place_on("tm")
    first_frame, total_frames = step * frames, steps * frames
    zero_row = jnp.zeros((1, LANES), jnp.float32)

    below = [zero_row] * (frames + 2)
    above = [zero_row] * (frames + 2)
    for k in range(1, mods):
        source = me ^ k
        for f in range(frames):
            at = shard + plan.points + 2 * f
            above[f + 1] = jnp.where(source == me + 1, pieces[k - 1][at : at + 1, :], above[f + 1])
            below[f + 1] = jnp.where(source == me - 1, pieces[k - 1][at + 1 : at + 2, :], below[f + 1])

    even = step % 2 == 0
    prev_ref[...] = jnp.where(even, second_ref[...], first_ref[...])
    next_ref[...] = jnp.where(even, first_ref[...], second_ref[...])
    cells = [prev_ref[...]] + [direction_ref[f] for f in range(frames)] + [next_ref[...]]
    row_id = lax.broadcasted_iota(jnp.int32, (shard, LANES), 0)

    def from_next(body, last):
        return jnp.where(row_id == shard - 1, last, pltpu.roll(body, shard - 1, 0))

    def from_last(body, first):
        return jnp.where(row_id == 0, first, pltpu.roll(body, 1, 0))

    coef = [coef_ref[i] for i in range(4)]
    edge = [edge_ref[i, SUB - 1 : SUB, :] for i in range(4)]

    def moved(share, base, ahead):
        return share[0] * base + share[1] * ahead + row_ahead_sum(share, base, ahead)

    def row_ahead_sum(share, base, ahead):
        return share[2] * row_ahead(base) + share[3] * row_ahead(ahead)

    flow, flow_edge = [], []
    for t in range(frames + 1):
        frame = first_frame + t - 1
        valid = (frame >= 0) & (frame <= total_frames - 2)
        ahead = from_next(cells[t], above[t])
        flow.append(jnp.where(valid, cells[t + 1] - moved(coef, cells[t], ahead), 0.0))
        if t > 0:
            value = below[t + 1] - moved(edge, below[t], cells[t][0:1])
            flow_edge.append(jnp.where(valid & (me > 0), value, 0.0))
    total = jnp.zeros((SUB, LANES), jnp.float32)
    for t in range(frames):
        square = flow[t + 1] * flow[t + 1]
        for r in range(0, shard, SUB):
            total += square[r : r + SUB]
        base, side = flow[t + 1], flow_edge[t]
        spread_to = (
            coef[0] * base
            + from_last(coef[1] * base, edge[1] * side)
            + row_behind(coef[2] * base + from_last(coef[3] * base, edge[3] * side))
        )
        prior_ref[t] = flow[t] - spread_to
    flow_ref[...] = total


def final_kernel(plan, entries, *refs):
    mods, half, width, shard = plan.mods, plan.half, plan.width, plan.shard
    pieces = refs[:mods]
    prior_ref, coef_ref, edge_ref, hess_ref, curvature_ref = refs[mods:]
    me = place_on("mod")
    lane = lax.broadcasted_iota(jnp.int32, (half, LANES), 1)
    for parity in range(2):
        own = pl.ds(parity, half, stride=2)
        for f in range(plan.frames):
            hess_ref[f, own, :] = prior_ref[f, own, :]
        for k, piece in enumerate(pieces):
            source = me ^ k
            frame, group = source // plan.groups, source % plan.groups
            turn = (group * width - parity * width + LANES) % LANES
            moved = pltpu.roll(piece[0:half, :], turn, 1)
            hess_ref[frame, own, :] += jnp.where(lane // width == group, moved, 0.0)
    zero_row = jnp.zeros((1, LANES), jnp.float32)
    total, above, below = zero_row, zero_row, zero_row
    for k, piece in enumerate(pieces):
        source = me ^ k
        total += piece[half : half + 1, :]
        above = jnp.where(source == me + 1, piece[half + 1 : half + 2, :], above)
        below = jnp.where(source == me - 1, piece[half + 2 : half + 3, :], below)
    last = slice(shard - 1, shard)
    rim = slice(SUB - 1, SUB)
    hess_ref[0, last, :] -= coef_ref[1, last, :] * above + coef_ref[3, last, :] * row_ahead(above)
    hess_ref[plan.frames - 1, 0:1, :] -= edge_ref[1, rim, :] * below + row_behind(edge_ref[3, rim, :] * below)
    curvature_ref[0] = jnp.sum(total) / entries


def exchange(arrays, axis):
    count = lax.axis_size(axis)
    return [arrays[0]] + [
        lax.ppermute(arrays[k], axis, [(i, i ^ k) for i in range(count)]) for k in range(1, count)
    ]


def per_device(phase, direction, pupil_mask, mod_tilts, wind_codes, noise_weight):
    frames, shard, rows = phase.shape
    mods, steps = lax.axis_size("mod"), lax.axis_size("tm")
    plan = Plan(frames, shard, rows, mod_tilts.shape[0], mods)
    total_frames = frames * steps
    cells, wide = plan.cells, plan.tiles * LANES
    tables = [jnp.asarray(t) for t in roof_tables(plan)]
    phase, direction, pupil_mask, wind_codes, noise_weight, *tables = [
        pltpu.with_memory_space_constraint(array, pltpu.HBM)
        for array in (phase, direction, pupil_mask, wind_codes, noise_weight, *tables)
    ]

    def f32(*shape):
        return jax.ShapeDtypeStruct(shape, jnp.float32)

    def bf16(*shape):
        return jax.ShapeDtypeStruct(shape, jnp.bfloat16)

    def scratch(shape):
        return pltpu.VMEM(shape.shape, shape.dtype)

    def call(kernel, name, outs, in_specs, out_specs=None, scratch_shapes=()):
        return pl.pallas_call(
            kernel,
            out_shape=outs,
            in_specs=in_specs,
            out_specs=out_specs or [VMEM] * len(outs),
            scratch_shapes=list(scratch_shapes),
            compiler_params=params(),
            name=name,
        )

    packed = call(
        functools.partial(pack_kernel, plan),
        "pack",
        [f32(shard + plan.extra, LANES)] * mods + [f32(*phase.shape), f32(shard, LANES), f32(shard, LANES)],
        [HBM] * 3,
        scratch_shapes=[scratch(phase), pltpu.SMEM(mod_tilts.shape, jnp.int32), pltpu.SemaphoreType.DMA((3,))],
    )(mod_tilts, phase, direction)
    packed, (direction_near, first_frame, second_frame) = packed[:mods], packed[mods:]
    pieces = exchange(packed, "mod")
    first_frame = lax.ppermute(first_frame, "tm", [(i, i ^ 1) for i in range(steps) if i ^ 1 < steps])
    second_frame = lax.ppermute(
        second_frame, "tm", [p for i in range(1, steps - 1, 2) for p in ((i, i + 1), (i + 1, i))]
    )

    prepared = call(
        functools.partial(prep_kernel, plan),
        "prepare",
        [bf16(*t.shape) for t in tables]
        + [f32(2, cells, LANES), f32(2, 2, cells, LANES), f32(4, shard, LANES), f32(4, SUB, LANES)],
        [VMEM] + [HBM] * 7,
        scratch_shapes=[
            pltpu.VMEM(pupil_mask.shape, jnp.int32),
            pltpu.VMEM(noise_weight.shape[1:], jnp.float32),
            pltpu.VMEM((shard + SUB, LANES), jnp.int32),
            pltpu.SemaphoreType.DMA((8,)),
        ],
    )(packed[0], pupil_mask, noise_weight, wind_codes, *tables)
    even, odd, even_back, odd_back, mask, noise, coef, edge = prepared

    prior, flow_total, prev_frame, next_frame = call(
        functools.partial(prior_kernel, plan, steps),
        "prior",
        [f32(*phase.shape), f32(SUB, LANES), f32(shard, LANES), f32(shard, LANES)],
        [VMEM] * (mods + 4),
    )(*pieces[1:], direction_near, first_frame, second_frame, coef, edge)

    cosine, sine, fold, start, total = call(
        functools.partial(forward_kernel, plan),
        "forward",
        [f32(2, cells, wide), f32(2, cells, wide), bf16(2, 3 * cells, 2 * wide), f32(2, cells, LANES), f32(SUB, LANES)],
        [VMEM] * (mods + 5),
        scratch_shapes=[
            scratch(s)
            for s in (f32(2, cells, LANES), f32(2, cells, LANES), bf16(2, 3 * cells, 4 * wide), f32(2, cells, 4 * wide))
        ],
    )(*pieces, mask, noise, even, odd, flow_total)
    totals = exchange([total] * steps, "tm")

    grad = call(
        functools.partial(backward_kernel, plan),
        "backward",
        [f32(cells, LANES)],
        [VMEM] * 6,
        scratch_shapes=[scratch(f32(2, cells, 2 * wide))],
    )(cosine, sine, fold, start, even_back, odd_back)[0]

    sent = call(
        functools.partial(send_kernel, plan, steps),
        "send_back",
        [f32(plan.half + SUB, LANES)] * mods,
        [VMEM] * (steps + 3),
    )(*totals, grad, prev_frame, next_frame)
    returned = exchange(sent, "mod")

    hess_vec, curvature = call(
        functools.partial(final_kernel, plan, float(total_frames * plan.pupil * rows)),
        "join",
        [f32(*phase.shape), f32(1)],
        [VMEM] * (mods + 3),
        out_specs=[VMEM, SMEM],
    )(*returned, prior, coef, edge)
    return hess_vec, curvature


def solution(mesh):
    return jax.shard_map(
        per_device,
        mesh=mesh,
        in_specs=(
            P(("grp", "tm"), "mod", None),
            P(("grp", "tm"), "mod", None),
            P(),
            P("mod"),
            P("grp", None),
            P(("grp", "tm"), None, None),
        ),
        out_specs=(P(("grp", "tm"), "mod", None), P("grp")),
        check_vma=False,
    )
```

```python
import functools

import jax
import jax.numpy as jnp
import ml_dtypes
import numpy as np
from jax import lax
from jax.experimental import pallas as pl
from jax.experimental.pallas import tpu as pltpu
from jax.sharding import PartitionSpec as P

LANES = 128
SUB = 8
CHUNK = 32
VMEM = pl.BlockSpec(memory_space=pltpu.VMEM)
SMEM = pl.BlockSpec(memory_space=pltpu.SMEM)
HBM = pl.BlockSpec(memory_space=pltpu.HBM)


def params():
    return pltpu.CompilerParams(vmem_limit_bytes=48 * 1024 * 1024)


class Plan:
    def __init__(self, frames, shard, rows, points, mods):
        self.frames, self.shard, self.rows, self.mods = frames, shard, rows, mods
        self.points = points
        self.pupil = shard * mods
        self.length = 2 * self.pupil
        assert rows == LANES and mods % frames == 0 and frames % 2 == 0 and mods % 2 == 0
        self.groups = mods // frames
        self.width = rows // self.groups
        assert 2 * self.width <= LANES
        self.copies = LANES // self.width
        self.total_points = points * mods
        assert self.total_points % self.copies == 0
        self.tiles = self.total_points // self.copies
        self.half = shard // 2
        self.cells = self.pupil // 2
        self.extra = -(-(points + 2 * frames) // SUB) * SUB


def roof_tables(plan):
    cells, length = plan.cells, plan.length
    index = np.arange(cells)
    turned = (index + cells // 2) % cells

    def kernel(gap):
        return 2.0 / length / np.cos(2.0 * np.pi * gap / length)

    even = kernel(2 * turned[:, None] - (2 * index[None, :] + 1))
    odd = kernel(2 * turned[:, None] + 1 - 2 * index[None, :])

    def split(table):
        high = table.astype(ml_dtypes.bfloat16)
        low = (table - high.astype(np.float64)).astype(ml_dtypes.bfloat16)
        return np.concatenate([high, high, low], axis=1)

    return split(even), split(odd), split(even.T), split(odd.T)


def spread(cells, plan, first):
    lane = lax.broadcasted_iota(jnp.int32, cells.shape, 1)
    width = plan.width
    if 2 * width == LANES:
        other = pltpu.roll(cells, width, 1)
        keep = (lane < width) if first == 0 else (lane >= width)
        return jnp.where(keep, cells, other)
    if first:
        cells = pltpu.roll(cells, LANES - first, 1)
    cells = jnp.where(lane < width, cells, 0.0)
    step = width
    while step < LANES:
        cells = cells + pltpu.roll(cells, step, 1)
        step *= 2
    return cells


def lane_sum(cells, plan):
    step = plan.width
    while step < LANES:
        cells = cells + pltpu.roll(cells, step, 1)
        step *= 2
    return cells


def place_on(axis):
    return lax.axis_index(axis)


def place_on(axis):
    return lax.axis_index(axis)


def pack_kernel(plan, phase_hbm, direction_hbm, *refs):
    outs = refs[: plan.mods]
    direction_ref, phase_ref, sems = refs[plan.mods :]
    loads = [
        pltpu.make_async_copy(source, target, sems.at[i])
        for i, (source, target) in enumerate(((direction_hbm, direction_ref), (phase_hbm, phase_ref)))
    ]
    for load in loads:
        load.start()
    me = place_on("mod")
    width, half, shard, frames = plan.width, plan.half, plan.shard, plan.frames
    lane = lax.broadcasted_iota(jnp.int32, (half, LANES), 1)
    for load in loads:
        load.wait()
    for k, out in enumerate(outs):
        dest = me ^ k
        frame, group = dest // plan.groups, dest % plan.groups
        back = (LANES - group * width) % LANES
        ahead = (LANES + width - group * width) % LANES
        for parity in range(2):
            own = pl.ds(parity, half, stride=2)
            one = pltpu.roll(phase_ref[frame, own, :], back, 1)
            two = pltpu.roll(direction_ref[frame, own, :], ahead, 1)
            out[parity * half : (parity + 1) * half, :] = jnp.where(lane < width, one, two)
        rows = []
        for f in range(frames):
            rows += [direction_ref[f, 0:1, :], direction_ref[f, shard - 1 : shard, :]]
        rows += [jnp.zeros((1, LANES), jnp.float32)] * (plan.extra - len(rows))
        out[shard : shard + plan.extra, :] = jnp.concatenate(rows, axis=0)
    for f in range(frames):
        start = shard + plan.extra + f * shard
        outs[1][start : start + shard, :] = direction_ref[f]


def relay_kernel(plan, own_ref, piece_ref, after_ref, pair_ref, send_ref):
    shard, frames = plan.shard, plan.frames
    side = place_on("mod") % 2
    for f in range(frames):
        start = shard + plan.extra + f * shard
        pair_ref[f, pl.ds(pl.multiple_of(side * shard, SUB), shard), :] = own_ref[f]
        pair_ref[f, pl.ds(pl.multiple_of((1 - side) * shard, SUB), shard), :] = piece_ref[start : start + shard, :]
    send_ref[...] = pair_ref[side * (frames - 1)]


def label_kernel(plan, tilt_ref, *refs):
    at = plan.shard + 2 * plan.frames
    for out in refs[plan.mods :]:
        out[at : at + plan.points, :] = tilt_ref[...]


def prep_kernel(plan, seed_ref, mask_hbm, noise_hbm, codes_hbm, *refs):
    mask_out, noise_out, coef_out, edge_out, mask_ref, noise_ref, codes_ref, sems = refs
    me = place_on("mod")
    shard, cells, quarter_line = plan.shard, plan.cells, plan.pupil // 2
    frame, group = me // plan.groups, me % plan.groups
    group_back = (LANES - group * plan.width) % LANES
    reach = 2 * shard
    begin = pl.multiple_of((me // 2) * reach, SUB)
    before = pl.multiple_of(jnp.maximum(begin - SUB, 0), SUB)
    pairs = [
        (mask_hbm, mask_ref),
        (noise_hbm.at[frame], noise_ref),
        (codes_hbm.at[pl.ds(before, SUB)], codes_ref.at[0:SUB]),
        (codes_hbm.at[pl.ds(begin, reach)], codes_ref.at[SUB : SUB + reach]),
    ]
    loads = [pltpu.make_async_copy(source, target, sems.at[i]) for i, (source, target) in enumerate(pairs)]
    for load in loads:
        load.start()

    lane_group = lax.broadcasted_iota(jnp.int32, (CHUNK, LANES), 1) // plan.width

    def own_rows(cells_in):
        if plan.copies == 2:
            return jnp.where(lane_group == group, cells_in, pltpu.roll(cells_in, plan.width, 1))
        return spread(pltpu.roll(cells_in, group_back, 1), plan, 0)

    loads[0].wait()
    for parity in range(2):
        for row in range(0, cells, CHUNK):
            picked = mask_ref[pl.ds(2 * row + parity, CHUNK, stride=2), :].astype(jnp.float32)
            mask_out[parity, row : row + CHUNK, :] = own_rows(picked)
    loads[1].wait()
    for parity in range(2):
        for row in range(0, cells, CHUNK):
            low_half = row < cells // 2
            inner = 2 * (row % (cells // 2)) + parity
            for side, block in enumerate((2, 0) if low_half else (1, 3)):
                picked = noise_ref[pl.ds(block * quarter_line + inner, CHUNK, stride=2), :]
                noise_out[side, parity, row : row + CHUNK, :] = own_rows(picked)
    loads[2].wait()
    loads[3].wait()
    for i, share in enumerate(shares(codes_ref[SUB : SUB + reach, :])):
        coef_out[i] = share
    for i, share in enumerate(shares(codes_ref[0:SUB, :])):
        edge_out[i] = jnp.where(me > 1, share, 0.0)


def wave(turns):
    quarters = jnp.round(turns * 4.0)
    angle = (turns - quarters * 0.25) * (2.0 * np.pi)
    square = angle * angle
    sin_part = ((-1.9515295891e-4 * square + 8.3321608736e-3) * square - 1.6666654611e-1) * square * angle + angle
    cos_part = (
        (2.443315711809948e-5 * square - 1.388731625493765e-3) * square + 4.166664568298827e-2
    ) * (square * square) + (1.0 - 0.5 * square)
    count = quarters.astype(jnp.int32)
    odd = (count & 1) != 0
    cosine = jnp.where(odd, sin_part, cos_part)
    sine = jnp.where(odd, cos_part, sin_part)
    cosine = jnp.where(((count + 1) & 2) != 0, -cosine, cosine)
    sine = jnp.where((count & 2) != 0, -sine, sine)
    return cosine, sine


def put_split(ref, row, rows, cells, column, value):
    high = value.astype(jnp.bfloat16)
    low = (value - high.astype(jnp.float32)).astype(jnp.bfloat16)
    where = slice(column, column + LANES)
    ref[row : row + rows, where] = high
    ref[cells + row : cells + row + rows, where] = low
    ref[2 * cells + row : 2 * cells + row + rows, where] = high


def forward_kernel(plan, *refs):
    mods, half, cells = plan.mods, plan.half, plan.cells
    tiles, wide = plan.tiles, plan.tiles * LANES
    pieces = refs[:mods]
    mask_ref, noise_ref = refs[mods : mods + 2]
    tables_hbm = refs[mods + 2 : mods + 6]
    cos_ref, sin_ref, image_ref, weight_ref, total_ref, even_back_ref, odd_back_ref = refs[mods + 6 : mods + 13]
    turn_ref, dir_ref, even_in_ref, odd_in_ref, even_ref, odd_ref, sems = refs[mods + 13 :]
    loads = [
        pltpu.make_async_copy(source, target, sems.at[i])
        for i, (source, target) in enumerate(zip(tables_hbm, (even_ref, odd_ref, even_back_ref, odd_back_ref)))
    ]
    for load in (loads[1], loads[0], loads[2], loads[3]):
        load.start()
    me = place_on("mod")
    lane_row = lax.broadcasted_iota(jnp.int32, (1, LANES), 1)

    for k, piece in enumerate(pieces):
        place = pl.ds(pl.multiple_of((me ^ k) * half, SUB), half)
        for parity in range(2):
            cells_in = piece[parity * half : (parity + 1) * half, :]
            turn_ref[parity, place, :] = spread(cells_in, plan, 0) * (0.5 / np.pi)
            dir_ref[parity, place, :] = spread(cells_in, plan, plan.width)

    tilt_rows = [jnp.zeros((1, LANES), jnp.float32)] * tiles
    for k, piece in enumerate(pieces):
        for p in range(plan.points):
            tile, slot = divmod(k * plan.points + p, plan.copies)
            at = plan.shard + 2 * plan.frames + p
            row = piece[at : at + 1, :]
            tilt_rows[tile] = jnp.where(lane_row // plan.width == slot, row, tilt_rows[tile])

    def tilted(tile, spots):
        tilt = spots.astype(jnp.float32) / plan.length * tilt_rows[tile]
        return wave(tilt - jnp.round(tilt))

    steps = [tilted(tile, jnp.full((1, LANES), 2 * CHUNK, jnp.int32)) for tile in range(tiles)]
    spots = lax.broadcasted_iota(jnp.int32, (CHUNK, LANES), 0) * 2 + plan.pupil // 2

    def fields(parity, ref):
        tilts = [tilted(tile, spots + parity) for tile in range(tiles)]
        for row in range(0, cells, CHUNK):
            here = slice(row, row + CHUNK)
            mask = mask_ref[parity, here, :]
            push = dir_ref[parity, here, :]
            turns = turn_ref[parity, here, :]
            flat_cos, flat_sin = wave(turns)
            flat_cos, flat_sin = flat_cos * mask, flat_sin * mask
            for tile in range(tiles):
                tilt_cos, tilt_sin = tilts[tile]
                cosine = flat_cos * tilt_cos - flat_sin * tilt_sin
                sine = flat_sin * tilt_cos + flat_cos * tilt_sin
                step_cos, step_sin = steps[tile]
                tilts[tile] = (
                    tilt_cos * step_cos - tilt_sin * step_sin,
                    tilt_sin * step_cos + tilt_cos * step_sin,
                )
                at = tile * LANES
                cos_ref[parity, here, at : at + LANES] = cosine
                sin_ref[parity, here, at : at + LANES] = sine
                put_split(ref, row, CHUNK, cells, at, cosine)
                put_split(ref, row, CHUNK, cells, wide + at, sine)
                put_split(ref, row, CHUNK, cells, 2 * wide + at, -sine * push)
                put_split(ref, row, CHUNK, cells, 3 * wide + at, cosine * push)

    def signals(parity, total):
        for row in range(0, cells, CHUNK):
            here = slice(row, row + CHUNK)
            push = dir_ref[parity, here, :]
            even_sum = odd_sum = shift = 0.0
            for tile in range(tiles):
                at = tile * LANES
                cosine = cos_ref[parity, here, at : at + LANES]
                sine = sin_ref[parity, here, at : at + LANES]
                image_cos, image_sin, push_real, push_imag = [
                    image_ref[parity, here, q * wide + at : q * wide + at + LANES] for q in range(4)
                ]
                even_sum += image_sin * push_imag + image_cos * push_real
                odd_sum += cosine * (push_imag - push * image_cos) - sine * (push_real + push * image_sin)
                shift += cosine * image_cos + sine * image_sin
            even_sum = lane_sum(even_sum, plan) * 2.0
            odd_sum = lane_sum(odd_sum, plan)
            signal_after, signal_before = even_sum + odd_sum, even_sum - odd_sum
            weighted_after = noise_ref[0, parity, here, :] * signal_after
            weighted_before = noise_ref[1, parity, here, :] * signal_before
            squares = weighted_after * signal_after + weighted_before * signal_before
            for r in range(0, CHUNK, SUB):
                total += squares[r : r + SUB]
            gap = (weighted_after - weighted_before) * 0.5
            weight_ref[0, parity, here, :] = weighted_after + weighted_before
            weight_ref[1, parity, here, :] = gap
            weight_ref[2, parity, here, :] = -gap * shift
        return total

    def image(parity, table, ref):
        image_ref[parity] = jnp.dot(table[...], ref[...], preferred_element_type=jnp.float32)

    fields(0, even_in_ref)
    fields(1, odd_in_ref)
    loads[1].wait()
    image(1, odd_ref, even_in_ref)
    loads[0].wait()
    image(0, even_ref, odd_in_ref)
    total = signals(1, jnp.zeros((SUB, LANES), jnp.float32))
    total = signals(0, total)
    total_ref[...] = total / plan.copies
    for load in loads[2:]:
        load.wait()


def backward_kernel(plan, *refs):
    cos_ref, sin_ref, image_ref, weight_ref, even_ref, odd_ref, halo_ref, prior_ref = refs[:8]
    outs, (grad_ref, even_in_ref, odd_in_ref, back_ref) = refs[8:-4], refs[-4:]
    half, cells, shard, tiles, wide = plan.half, plan.cells, plan.shard, plan.tiles, plan.tiles * LANES
    me = place_on("mod")

    def fold(parity, ref):
        for row in range(0, cells, CHUNK):
            here = slice(row, row + CHUNK)
            both, gap = weight_ref[0, parity, here, :], weight_ref[1, parity, here, :]
            for tile in range(tiles):
                at = tile * LANES
                cosine = cos_ref[parity, here, at : at + LANES]
                sine = sin_ref[parity, here, at : at + LANES]
                image_cos = image_ref[parity, here, at : at + LANES]
                image_sin = image_ref[parity, here, wide + at : wide + at + LANES]
                put_split(ref, row, CHUNK, cells, at, gap * cosine + both * image_sin)
                put_split(ref, row, CHUNK, cells, wide + at, gap * sine - both * image_cos)

    def back(parity, table, ref):
        back_ref[parity] = jnp.dot(table[...], ref[...], preferred_element_type=jnp.float32)

    fold(0, even_in_ref)
    fold(1, odd_in_ref)
    back(1, even_ref, even_in_ref)
    back(0, odd_ref, odd_in_ref)
    lane = lax.broadcasted_iota(jnp.int32, (CHUNK, LANES), 1)
    for row in range(0, cells, CHUNK):
        here = slice(row, row + CHUNK)
        grads = []
        for parity in range(2):
            grad = weight_ref[2, parity, here, :]
            for tile in range(tiles):
                at = tile * LANES
                grad += cos_ref[parity, here, at : at + LANES] * back_ref[parity, here, at : at + LANES]
                grad += sin_ref[parity, here, at : at + LANES] * back_ref[parity, here, wide + at : wide + at + LANES]
            grads.append(lane_sum(grad, plan) * 2.0)
        grad_ref[here, :] = jnp.where(lane < plan.width, grads[0], grads[1])
    rows = [halo_ref[0:1, :], halo_ref[2 * shard - 1 : 2 * shard, :]]
    rows += [jnp.zeros((1, LANES), jnp.float32)] * (SUB - len(rows))
    tail = jnp.concatenate(rows, axis=0)
    for k, out in enumerate(outs):
        place = pl.ds(pl.multiple_of((me ^ k) * half, SUB), half)
        out[0:half, :] = grad_ref[place, :]
        out[half : half + SUB, :] = tail
    for f in range(plan.frames // 2):
        start = half + SUB + f * shard
        theirs = pl.ds(pl.multiple_of((1 - me % 2) * shard, SUB), shard)
        outs[1][start : start + shard, :] = prior_ref[f, theirs, :]


def seal_kernel(plan, steps, *refs):
    total = refs[0][...]
    for ref in refs[1:steps]:
        total += ref[...]
    for out in refs[steps + plan.mods :]:
        out[plan.half + 2 : plan.half + 3, :] = jnp.sum(total, axis=0, keepdims=True)


def row_ahead(cells):
    lane = lax.broadcasted_iota(jnp.int32, cells.shape, 1)
    return jnp.where(lane == LANES - 1, 0.0, pltpu.roll(cells, LANES - 1, 1))


def row_behind(cells):
    lane = lax.broadcasted_iota(jnp.int32, cells.shape, 1)
    return jnp.where(lane == 0, 0.0, pltpu.roll(cells, 1, 1))


def shares(codes):
    ahead_x = ((codes & 3).astype(jnp.float32) + 0.5) / 4.0
    ahead_r = ((codes >> 2).astype(jnp.float32) + 0.5) / 4.0
    return (1.0 - ahead_x) * (1.0 - ahead_r), ahead_x * (1.0 - ahead_r), (1.0 - ahead_x) * ahead_r, ahead_x * ahead_r


def prior_kernel(plan, steps, *refs):
    mods, shard, frames = plan.mods, plan.shard, plan.frames
    pieces, refs = refs[: mods - 1], refs[mods - 1 :]
    pair_ref, halo_ref, coef_ref, edge_ref, data_ref, prior_ref, total_ref = refs
    me, step = place_on("mod"), place_on("tm")
    side, base, reach, held = me % 2, me - me % 2, 2 * shard, frames // 2
    first_frame, total_frames = step * frames + side * held, steps * frames
    zero_row = jnp.zeros((1, LANES), jnp.float32)

    halo = halo_ref[...]
    cells, below, above = [], [], []
    for t in range(held + 2):
        frame = side * held + t - 1
        inside = (frame >= 0) & (frame < frames)
        cells.append(jnp.where(inside, pair_ref[jnp.clip(frame, 0, frames - 1)], halo))
        low, high = zero_row, zero_row
        for k in range(2, mods):
            source = me ^ k
            for f in range(frames):
                at = shard + 2 * f
                here = frame == f
                high = jnp.where((source == base + 2) & here, pieces[k - 1][at : at + 1, :], high)
                low = jnp.where((source == base - 1) & here, pieces[k - 1][at + 1 : at + 2, :], low)
        below.append(low)
        above.append(high)

    row_id = lax.broadcasted_iota(jnp.int32, (reach, LANES), 0)

    def from_next(body, last):
        return jnp.where(row_id == reach - 1, last, pltpu.roll(body, reach - 1, 0))

    def from_last(body, first):
        return jnp.where(row_id == 0, first, pltpu.roll(body, 1, 0))

    coef = [coef_ref[i] for i in range(4)]
    edge = [edge_ref[i, SUB - 1 : SUB, :] for i in range(4)]

    def moved(share, base, ahead):
        return share[0] * base + share[1] * ahead + share[2] * row_ahead(base) + share[3] * row_ahead(ahead)

    flow, flow_edge = [], []
    for t in range(held + 1):
        frame = first_frame + t - 1
        valid = (frame >= 0) & (frame <= total_frames - 2)
        ahead = from_next(cells[t], above[t])
        flow.append(jnp.where(valid, cells[t + 1] - moved(coef, cells[t], ahead), 0.0))
        if t > 0:
            value = below[t + 1] - moved(edge, below[t], cells[t][0:1])
            flow_edge.append(jnp.where(valid & (me > 1), value, 0.0))
    total = data_ref[...]
    for t in range(held):
        square = flow[t + 1] * flow[t + 1]
        for r in range(0, reach, SUB):
            total += square[r : r + SUB]
        own, rim = flow[t + 1], flow_edge[t]
        spread_to = (
            coef[0] * own
            + from_last(coef[1] * own, edge[1] * rim)
            + row_behind(coef[2] * own + from_last(coef[3] * own, edge[3] * rim))
        )
        prior_ref[t] = flow[t] - spread_to
    total_ref[...] = total


def final_kernel(plan, entries, *refs):
    mods, half, width, shard = plan.mods, plan.half, plan.width, plan.shard
    pieces = refs[:mods]
    prior_ref, coef_ref, edge_ref, hess_ref, curvature_ref = refs[mods:]
    me = place_on("mod")
    side, held = me % 2, plan.frames // 2
    mine = pl.ds(pl.multiple_of(side * shard, SUB), shard)
    for f in range(held):
        start = half + SUB + f * shard
        hess_ref[side * held + f] = prior_ref[f, mine, :]
        hess_ref[(1 - side) * held + f] = pieces[1][start : start + shard, :]
    lane = lax.broadcasted_iota(jnp.int32, (half, LANES), 1)
    for parity in range(2):
        own = pl.ds(parity, half, stride=2)
        for k, piece in enumerate(pieces):
            source = me ^ k
            frame, group = source // plan.groups, source % plan.groups
            turn = (group * width - parity * width + LANES) % LANES
            moved = pltpu.roll(piece[0:half, :], turn, 1)
            hess_ref[frame, own, :] += jnp.where(lane // width == group, moved, 0.0)
    zero_row = jnp.zeros((1, LANES), jnp.float32)
    total, above, below = zero_row, zero_row, zero_row
    for k, piece in enumerate(pieces):
        source = me ^ k
        total += piece[half + 2 : half + 3, :]
        above = jnp.where((source == me + 1) & (side == 1), piece[half : half + 1, :], above)
        below = jnp.where((source == me - 1) & (side == 0), piece[half + 1 : half + 2, :], below)
    last, top, rim = slice(shard - 1, shard), slice(2 * shard - 1, 2 * shard), slice(SUB - 1, SUB)
    hess_ref[0, last, :] -= coef_ref[1, top, :] * above + coef_ref[3, top, :] * row_ahead(above)
    hess_ref[plan.frames - 1, 0:1, :] -= edge_ref[1, rim, :] * below + row_behind(edge_ref[3, rim, :] * below)
    curvature_ref[0] = jnp.sum(total) / entries


def exchange(arrays, axis):
    count = lax.axis_size(axis)
    came = {0: arrays[0]}
    for k in reversed(range(1, count)):
        came[k] = lax.ppermute(arrays[k], axis, [(i, i ^ k) for i in range(count)])
    return [came[k] for k in range(count)]


def per_device(phase, direction, pupil_mask, mod_tilts, wind_codes, noise_weight):
    frames, shard, rows = phase.shape
    mods, steps = lax.axis_size("mod"), lax.axis_size("tm")
    plan = Plan(frames, shard, rows, mod_tilts.shape[0], mods)
    total_frames = frames * steps
    cells, wide = plan.cells, plan.tiles * LANES
    tables = [jnp.asarray(t) for t in roof_tables(plan)]
    phase, direction, pupil_mask, wind_codes, noise_weight, *tables = [
        pltpu.with_memory_space_constraint(array, pltpu.HBM)
        for array in (phase, direction, pupil_mask, wind_codes, noise_weight, *tables)
    ]

    def f32(*shape):
        return jax.ShapeDtypeStruct(shape, jnp.float32)

    def bf16(*shape):
        return jax.ShapeDtypeStruct(shape, jnp.bfloat16)

    def scratch(shape):
        return pltpu.VMEM(shape.shape, shape.dtype)

    def call(kernel, name, outs, in_specs, out_specs=None, scratch_shapes=(), aliases=None, work=0.02):
        return pl.pallas_call(
            kernel,
            out_shape=outs,
            in_specs=in_specs,
            out_specs=out_specs or [VMEM] * len(outs),
            scratch_shapes=list(scratch_shapes),
            input_output_aliases=aliases or {},
            compiler_params=params(),
            cost_estimate=pl.CostEstimate(
                flops=int(work * 1.1e9), bytes_accessed=int(work * 3.6e6), transcendentals=0
            ),
            name=name,
        )

    rows_in = shard + plan.extra
    *packed, direction_near = call(
        functools.partial(pack_kernel, plan),
        "pack",
        [f32(rows_in + (frames * shard if k == 1 else 0), LANES) for k in range(mods)] + [f32(*phase.shape)],
        [HBM] * 2,
        scratch_shapes=[scratch(phase), pltpu.SemaphoreType.DMA((2,))],
        work=1.2,
    )(phase, direction)
    tilts = jnp.broadcast_to(mod_tilts.astype(jnp.float32)[:, None], (plan.points, LANES))
    packed = call(
        functools.partial(label_kernel, plan),
        "label",
        [f32(*p.shape) for p in packed],
        [VMEM] * (mods + 1),
        aliases={k + 1: k for k in range(mods)},
    )(tilts, *packed)
    pieces = exchange(packed, "mod")

    mask, noise, coef, edge = call(
        functools.partial(prep_kernel, plan),
        "prepare",
        [f32(2, cells, LANES), f32(2, 2, cells, LANES), f32(4, 2 * shard, LANES), f32(4, SUB, LANES)],
        [VMEM] + [HBM] * 3,
        scratch_shapes=[
            pltpu.VMEM(pupil_mask.shape, jnp.int32),
            pltpu.VMEM(noise_weight.shape[1:], jnp.float32),
            pltpu.VMEM((2 * shard + SUB, LANES), jnp.int32),
            pltpu.SemaphoreType.DMA((4,)),
        ],
        work=1.5,
    )(packed[0], pupil_mask, noise_weight, wind_codes)

    pair, edge_frame = call(
        functools.partial(relay_kernel, plan),
        "relay",
        [f32(frames, 2 * shard, LANES), f32(2 * shard, LANES)],
        [VMEM] * 3,
        work=0.05,
    )(direction_near, pieces[1], edge)
    ends = [(t * mods + m, (t + 1) * mods + m - 1) for t in range(steps - 1) for m in range(1, mods, 2)]
    halo = lax.ppermute(edge_frame, ("tm", "mod"), ends + [(b, a) for a, b in ends])

    table = bf16(*tables[0].shape)
    cosine, sine, image, weights, data_total, even_back, odd_back = call(
        functools.partial(forward_kernel, plan),
        "forward",
        [f32(2, cells, wide), f32(2, cells, wide), f32(2, cells, 4 * wide), f32(3, 2, cells, LANES), f32(SUB, LANES)]
        + [table] * 2,
        [VMEM] * (mods + 2) + [HBM] * 4,
        scratch_shapes=[
            scratch(s)
            for s in (f32(2, cells, LANES),) * 2 + (bf16(3 * cells, 4 * wide),) * 2 + (table,) * 2
        ]
        + [pltpu.SemaphoreType.DMA((4,))],
        work=2.8,
    )(*pieces, mask, noise, *tables)

    prior, total = call(
        functools.partial(prior_kernel, plan, steps),
        "prior",
        [f32(frames // 2, 2 * shard, LANES), f32(SUB, LANES)],
        [VMEM] * (mods + 4),
        work=0.4,
    )(*pieces[1:], pair, halo, coef, edge, data_total)
    totals = exchange([total] * steps, "tm")

    sent = call(
        functools.partial(backward_kernel, plan),
        "backward",
        [f32(plan.half + SUB + (frames // 2 * shard if k == 1 else 0), LANES) for k in range(mods)],
        [VMEM] * 8,
        scratch_shapes=[
            scratch(s)
            for s in (f32(cells, LANES),) + (bf16(3 * cells, 2 * wide),) * 2 + (f32(2, cells, 2 * wide),)
        ],
        work=0.8,
    )(cosine, sine, image, weights, even_back, odd_back, halo, prior)
    sent = call(
        functools.partial(seal_kernel, plan, steps),
        "seal",
        [f32(*p.shape) for p in sent],
        [VMEM] * (steps + mods),
        aliases={steps + k: k for k in range(mods)},
    )(*reversed(totals), *sent)
    returned = exchange(sent, "mod")

    hess_vec, curvature = call(
        functools.partial(final_kernel, plan, float(total_frames * plan.pupil * rows)),
        "join",
        [f32(*phase.shape), f32(1)],
        [VMEM] * (mods + 3),
        out_specs=[VMEM, SMEM],
        work=0.8,
    )(*returned, prior, coef, edge)
    return hess_vec, curvature


def solution(mesh):
    return jax.shard_map(
        per_device,
        mesh=mesh,
        in_specs=(
            P(("grp", "tm"), "mod", None),
            P(("grp", "tm"), "mod", None),
            P(),
            P("mod"),
            P("grp", None),
            P(("grp", "tm"), None, None),
        ),
        out_specs=(P(("grp", "tm"), "mod", None), P("grp")),
        check_vma=False,
    )
```

```python
import functools

import jax
import jax.numpy as jnp
import ml_dtypes
import numpy as np
from jax import lax
from jax.experimental import pallas as pl
from jax.experimental.pallas import tpu as pltpu
from jax.sharding import PartitionSpec as P

LANES = 128
SUB = 8
CHUNK = 32
VMEM = pl.BlockSpec(memory_space=pltpu.VMEM)
SMEM = pl.BlockSpec(memory_space=pltpu.SMEM)
HBM = pl.BlockSpec(memory_space=pltpu.HBM)


def params():
    return pltpu.CompilerParams(vmem_limit_bytes=48 * 1024 * 1024)


class Plan:
    def __init__(self, frames, shard, rows, points, mods):
        self.frames, self.shard, self.rows, self.mods = frames, shard, rows, mods
        self.points = points
        self.pupil = shard * mods
        self.length = 2 * self.pupil
        assert rows == LANES and mods % frames == 0 and frames % 2 == 0 and mods % 2 == 0
        self.groups = mods // frames
        self.width = rows // self.groups
        assert 2 * self.width <= LANES
        self.copies = LANES // self.width
        self.total_points = points * mods
        assert self.total_points % self.copies == 0
        self.tiles = self.total_points // self.copies
        self.half = shard // 2
        self.cells = self.pupil // 2
        self.extra = -(-(points + 2 * frames) // SUB) * SUB


def roof_tables(plan):
    cells, length = plan.cells, plan.length
    index = np.arange(cells)
    turned = (index + cells // 2) % cells

    def kernel(gap):
        return 2.0 / length / np.cos(2.0 * np.pi * gap / length)

    even = kernel(2 * turned[:, None] - (2 * index[None, :] + 1))
    odd = kernel(2 * turned[:, None] + 1 - 2 * index[None, :])

    def split(table):
        high = table.astype(ml_dtypes.bfloat16)
        low = (table - high.astype(np.float64)).astype(ml_dtypes.bfloat16)
        return np.concatenate([high, high, low], axis=1)

    return split(even), split(odd), split(even.T), split(odd.T)


def spread(cells, plan, first):
    lane = lax.broadcasted_iota(jnp.int32, cells.shape, 1)
    width = plan.width
    if 2 * width == LANES:
        other = pltpu.roll(cells, width, 1)
        keep = (lane < width) if first == 0 else (lane >= width)
        return jnp.where(keep, cells, other)
    if first:
        cells = pltpu.roll(cells, LANES - first, 1)
    cells = jnp.where(lane < width, cells, 0.0)
    step = width
    while step < LANES:
        cells = cells + pltpu.roll(cells, step, 1)
        step *= 2
    return cells


def lane_sum(cells, plan):
    step = plan.width
    while step < LANES:
        cells = cells + pltpu.roll(cells, step, 1)
        step *= 2
    return cells


def place_on(axis):
    return lax.axis_index(axis)


def place_on(axis):
    return lax.axis_index(axis)


def pack_kernel(plan, phase_hbm, direction_hbm, *refs):
    outs = refs[: plan.mods]
    direction_ref, phase_ref, sems = refs[plan.mods :]
    loads = [
        pltpu.make_async_copy(source, target, sems.at[i])
        for i, (source, target) in enumerate(((direction_hbm, direction_ref), (phase_hbm, phase_ref)))
    ]
    for load in loads:
        load.start()
    me = place_on("mod")
    width, half, shard, frames = plan.width, plan.half, plan.shard, plan.frames
    lane = lax.broadcasted_iota(jnp.int32, (half, LANES), 1)
    for load in loads:
        load.wait()
    for k, out in enumerate(outs):
        dest = me ^ k
        frame, group = dest // plan.groups, dest % plan.groups
        back = (LANES - group * width) % LANES
        ahead = (LANES + width - group * width) % LANES
        for parity in range(2):
            own = pl.ds(parity, half, stride=2)
            one = pltpu.roll(phase_ref[frame, own, :], back, 1)
            two = pltpu.roll(direction_ref[frame, own, :], ahead, 1)
            out[parity * half : (parity + 1) * half, :] = jnp.where(lane < width, one, two)
        rows = []
        for f in range(frames):
            rows += [direction_ref[f, 0:1, :], direction_ref[f, shard - 1 : shard, :]]
        rows += [jnp.zeros((1, LANES), jnp.float32)] * (plan.extra - len(rows))
        out[shard : shard + plan.extra, :] = jnp.concatenate(rows, axis=0)
    for f in range(frames):
        start = shard + plan.extra + f * shard
        outs[1][start : start + shard, :] = direction_ref[f]


def relay_kernel(plan, own_ref, piece_ref, after_ref, pair_ref, send_ref):
    shard, frames = plan.shard, plan.frames
    side = place_on("mod") % 2
    for f in range(frames):
        start = shard + plan.extra + f * shard
        pair_ref[f, pl.ds(pl.multiple_of(side * shard, SUB), shard), :] = own_ref[f]
        pair_ref[f, pl.ds(pl.multiple_of((1 - side) * shard, SUB), shard), :] = piece_ref[start : start + shard, :]
    send_ref[...] = pair_ref[side * (frames - 1)]


def label_kernel(plan, tilt_ref, *refs):
    at = plan.shard + 2 * plan.frames
    for out in refs[plan.mods :]:
        out[at : at + plan.points, :] = tilt_ref[...]


def prep_kernel(plan, seed_ref, mask_hbm, noise_hbm, codes_hbm, *refs):
    mask_out, noise_out, coef_out, edge_out, mask_ref, noise_ref, codes_ref, sems = refs
    me = place_on("mod")
    shard, cells, quarter_line = plan.shard, plan.cells, plan.pupil // 2
    frame, group = me // plan.groups, me % plan.groups
    group_back = (LANES - group * plan.width) % LANES
    reach = 2 * shard
    begin = pl.multiple_of((me // 2) * reach, SUB)
    before = pl.multiple_of(jnp.maximum(begin - SUB, 0), SUB)
    pairs = [
        (mask_hbm, mask_ref),
        (noise_hbm.at[frame], noise_ref),
        (codes_hbm.at[pl.ds(before, SUB)], codes_ref.at[0:SUB]),
        (codes_hbm.at[pl.ds(begin, reach)], codes_ref.at[SUB : SUB + reach]),
    ]
    loads = [pltpu.make_async_copy(source, target, sems.at[i]) for i, (source, target) in enumerate(pairs)]
    for load in loads:
        load.start()

    lane_group = lax.broadcasted_iota(jnp.int32, (CHUNK, LANES), 1) // plan.width

    def own_rows(cells_in):
        if plan.copies == 2:
            return jnp.where(lane_group == group, cells_in, pltpu.roll(cells_in, plan.width, 1))
        return spread(pltpu.roll(cells_in, group_back, 1), plan, 0)

    loads[0].wait()
    for parity in range(2):
        for row in range(0, cells, CHUNK):
            picked = mask_ref[pl.ds(2 * row + parity, CHUNK, stride=2), :].astype(jnp.float32)
            mask_out[parity, row : row + CHUNK, :] = own_rows(picked)
    loads[1].wait()
    for parity in range(2):
        for row in range(0, cells, CHUNK):
            low_half = row < cells // 2
            inner = 2 * (row % (cells // 2)) + parity
            for side, block in enumerate((2, 0) if low_half else (1, 3)):
                picked = noise_ref[pl.ds(block * quarter_line + inner, CHUNK, stride=2), :]
                noise_out[side, parity, row : row + CHUNK, :] = own_rows(picked)
    loads[2].wait()
    loads[3].wait()
    for i, share in enumerate(shares(codes_ref[SUB : SUB + reach, :])):
        coef_out[i] = share
    for i, share in enumerate(shares(codes_ref[0:SUB, :])):
        edge_out[i] = jnp.where(me > 1, share, 0.0)


def wave(turns):
    quarters = jnp.round(turns * 4.0)
    angle = (turns - quarters * 0.25) * (2.0 * np.pi)
    square = angle * angle
    sin_part = ((-1.9515295891e-4 * square + 8.3321608736e-3) * square - 1.6666654611e-1) * square * angle + angle
    cos_part = (
        (2.443315711809948e-5 * square - 1.388731625493765e-3) * square + 4.166664568298827e-2
    ) * (square * square) + (1.0 - 0.5 * square)
    count = quarters.astype(jnp.int32)
    odd = (count & 1) != 0
    cosine = jnp.where(odd, sin_part, cos_part)
    sine = jnp.where(odd, cos_part, sin_part)
    cosine = jnp.where(((count + 1) & 2) != 0, -cosine, cosine)
    sine = jnp.where((count & 2) != 0, -sine, sine)
    return cosine, sine


def put_split(ref, row, rows, cells, column, value):
    high = value.astype(jnp.bfloat16)
    low = (value - high.astype(jnp.float32)).astype(jnp.bfloat16)
    where = slice(column, column + LANES)
    ref[row : row + rows, where] = high
    ref[cells + row : cells + row + rows, where] = low
    ref[2 * cells + row : 2 * cells + row + rows, where] = high


def forward_kernel(plan, *refs):
    mods, half, cells = plan.mods, plan.half, plan.cells
    tiles, wide = plan.tiles, plan.tiles * LANES
    pieces = refs[:mods]
    mask_ref, noise_ref = refs[mods : mods + 2]
    tables_hbm = refs[mods + 2 : mods + 6]
    cos_ref, sin_ref, image_ref, weight_ref, total_ref, even_back_ref, odd_back_ref = refs[mods + 6 : mods + 13]
    turn_ref, dir_ref, even_in_ref, odd_in_ref, even_ref, odd_ref, sems = refs[mods + 13 :]
    loads = [
        pltpu.make_async_copy(source, target, sems.at[i])
        for i, (source, target) in enumerate(zip(tables_hbm, (even_ref, odd_ref, even_back_ref, odd_back_ref)))
    ]
    for load in (loads[1], loads[0], loads[2], loads[3]):
        load.start()
    me = place_on("mod")
    lane_row = lax.broadcasted_iota(jnp.int32, (1, LANES), 1)

    for k, piece in enumerate(pieces):
        place = pl.ds(pl.multiple_of((me ^ k) * half, SUB), half)
        for parity in range(2):
            cells_in = piece[parity * half : (parity + 1) * half, :]
            turn_ref[parity, place, :] = spread(cells_in, plan, 0) * (0.5 / np.pi)
            dir_ref[parity, place, :] = spread(cells_in, plan, plan.width)

    tilt_rows = [jnp.zeros((1, LANES), jnp.float32)] * tiles
    for k, piece in enumerate(pieces):
        for p in range(plan.points):
            tile, slot = divmod(k * plan.points + p, plan.copies)
            at = plan.shard + 2 * plan.frames + p
            row = piece[at : at + 1, :]
            tilt_rows[tile] = jnp.where(lane_row // plan.width == slot, row, tilt_rows[tile])

    def tilted(tile, spots):
        tilt = spots.astype(jnp.float32) / plan.length * tilt_rows[tile]
        return wave(tilt - jnp.round(tilt))

    steps = [tilted(tile, jnp.full((1, LANES), 2 * CHUNK, jnp.int32)) for tile in range(tiles)]
    spots = lax.broadcasted_iota(jnp.int32, (CHUNK, LANES), 0) * 2 + plan.pupil // 2

    def fields(parity, ref):
        tilts = [tilted(tile, spots + parity) for tile in range(tiles)]
        for row in range(0, cells, CHUNK):
            here = slice(row, row + CHUNK)
            mask = mask_ref[parity, here, :]
            push = dir_ref[parity, here, :]
            turns = turn_ref[parity, here, :]
            flat_cos, flat_sin = wave(turns)
            flat_cos, flat_sin = flat_cos * mask, flat_sin * mask
            for tile in range(tiles):
                tilt_cos, tilt_sin = tilts[tile]
                cosine = flat_cos * tilt_cos - flat_sin * tilt_sin
                sine = flat_sin * tilt_cos + flat_cos * tilt_sin
                step_cos, step_sin = steps[tile]
                tilts[tile] = (
                    tilt_cos * step_cos - tilt_sin * step_sin,
                    tilt_sin * step_cos + tilt_cos * step_sin,
                )
                at = tile * LANES
                cos_ref[parity, here, at : at + LANES] = cosine
                sin_ref[parity, here, at : at + LANES] = sine
                put_split(ref, row, CHUNK, cells, at, cosine)
                put_split(ref, row, CHUNK, cells, wide + at, sine)
                put_split(ref, row, CHUNK, cells, 2 * wide + at, -sine * push)
                put_split(ref, row, CHUNK, cells, 3 * wide + at, cosine * push)

    def signals(parity, total):
        for row in range(0, cells, CHUNK):
            here = slice(row, row + CHUNK)
            push = dir_ref[parity, here, :]
            even_sum = odd_sum = shift = 0.0
            for tile in range(tiles):
                at = tile * LANES
                cosine = cos_ref[parity, here, at : at + LANES]
                sine = sin_ref[parity, here, at : at + LANES]
                image_cos, image_sin, push_real, push_imag = [
                    image_ref[parity, here, q * wide + at : q * wide + at + LANES] for q in range(4)
                ]
                even_sum += image_sin * push_imag + image_cos * push_real
                odd_sum += cosine * (push_imag - push * image_cos) - sine * (push_real + push * image_sin)
                shift += cosine * image_cos + sine * image_sin
            even_sum = lane_sum(even_sum, plan) * 2.0
            odd_sum = lane_sum(odd_sum, plan)
            signal_after, signal_before = even_sum + odd_sum, even_sum - odd_sum
            weighted_after = noise_ref[0, parity, here, :] * signal_after
            weighted_before = noise_ref[1, parity, here, :] * signal_before
            squares = weighted_after * signal_after + weighted_before * signal_before
            for r in range(0, CHUNK, SUB):
                total += squares[r : r + SUB]
            gap = (weighted_after - weighted_before) * 0.5
            weight_ref[0, parity, here, :] = weighted_after + weighted_before
            weight_ref[1, parity, here, :] = gap
            weight_ref[2, parity, here, :] = -gap * shift
        return total

    def image(parity, table, ref):
        image_ref[parity] = jnp.dot(table[...], ref[...], preferred_element_type=jnp.float32)

    fields(0, even_in_ref)
    fields(1, odd_in_ref)
    loads[1].wait()
    image(1, odd_ref, even_in_ref)
    loads[0].wait()
    image(0, even_ref, odd_in_ref)
    total = signals(1, jnp.zeros((SUB, LANES), jnp.float32))
    total = signals(0, total)
    total_ref[...] = total / plan.copies
    for load in loads[2:]:
        load.wait()


def backward_kernel(plan, *refs):
    cos_ref, sin_ref, image_ref, weight_ref, even_ref, odd_ref, halo_ref, prior_ref = refs[:8]
    outs, (grad_ref, even_in_ref, odd_in_ref, back_ref) = refs[8:-4], refs[-4:]
    half, cells, shard, tiles, wide = plan.half, plan.cells, plan.shard, plan.tiles, plan.tiles * LANES
    me = place_on("mod")

    def fold(parity, ref):
        for row in range(0, cells, CHUNK):
            here = slice(row, row + CHUNK)
            both, gap = weight_ref[0, parity, here, :], weight_ref[1, parity, here, :]
            for tile in range(tiles):
                at = tile * LANES
                cosine = cos_ref[parity, here, at : at + LANES]
                sine = sin_ref[parity, here, at : at + LANES]
                image_cos = image_ref[parity, here, at : at + LANES]
                image_sin = image_ref[parity, here, wide + at : wide + at + LANES]
                put_split(ref, row, CHUNK, cells, at, gap * cosine + both * image_sin)
                put_split(ref, row, CHUNK, cells, wide + at, gap * sine - both * image_cos)

    def back(parity, table, ref):
        back_ref[parity] = jnp.dot(table[...], ref[...], preferred_element_type=jnp.float32)

    fold(0, even_in_ref)
    fold(1, odd_in_ref)
    back(1, even_ref, even_in_ref)
    back(0, odd_ref, odd_in_ref)
    lane = lax.broadcasted_iota(jnp.int32, (CHUNK, LANES), 1)
    for row in range(0, cells, CHUNK):
        here = slice(row, row + CHUNK)
        grads = []
        for parity in range(2):
            grad = weight_ref[2, parity, here, :]
            for tile in range(tiles):
                at = tile * LANES
                grad += cos_ref[parity, here, at : at + LANES] * back_ref[parity, here, at : at + LANES]
                grad += sin_ref[parity, here, at : at + LANES] * back_ref[parity, here, wide + at : wide + at + LANES]
            grads.append(lane_sum(grad, plan) * 2.0)
        grad_ref[here, :] = jnp.where(lane < plan.width, grads[0], grads[1])
    step, side = place_on("tm"), me % 2
    alone = jnp.where(side == 0, step == 0, step == lax.axis_size("tm") - 1)
    rows = [jnp.where(alone, 0.0, r) for r in (halo_ref[0:1, :], halo_ref[2 * shard - 1 : 2 * shard, :])]
    rows += [jnp.zeros((1, LANES), jnp.float32)] * (SUB - len(rows))
    tail = jnp.concatenate(rows, axis=0)
    for k, out in enumerate(outs):
        place = pl.ds(pl.multiple_of((me ^ k) * half, SUB), half)
        out[0:half, :] = grad_ref[place, :]
        out[half : half + SUB, :] = tail
    for f in range(plan.frames // 2):
        start = half + SUB + f * shard
        theirs = pl.ds(pl.multiple_of((1 - me % 2) * shard, SUB), shard)
        outs[1][start : start + shard, :] = prior_ref[f, theirs, :]


def seal_kernel(plan, steps, *refs):
    total = refs[0][...]
    for ref in refs[1:steps]:
        total += ref[...]
    for out in refs[steps + plan.mods :]:
        out[plan.half + 2 : plan.half + 3, :] = jnp.sum(total, axis=0, keepdims=True)


def row_ahead(cells):
    lane = lax.broadcasted_iota(jnp.int32, cells.shape, 1)
    return jnp.where(lane == LANES - 1, 0.0, pltpu.roll(cells, LANES - 1, 1))


def row_behind(cells):
    lane = lax.broadcasted_iota(jnp.int32, cells.shape, 1)
    return jnp.where(lane == 0, 0.0, pltpu.roll(cells, 1, 1))


def shares(codes):
    ahead_x = ((codes & 3).astype(jnp.float32) + 0.5) / 4.0
    ahead_r = ((codes >> 2).astype(jnp.float32) + 0.5) / 4.0
    return (1.0 - ahead_x) * (1.0 - ahead_r), ahead_x * (1.0 - ahead_r), (1.0 - ahead_x) * ahead_r, ahead_x * ahead_r


def prior_kernel(plan, steps, *refs):
    mods, shard, frames = plan.mods, plan.shard, plan.frames
    pieces, refs = refs[: mods - 1], refs[mods - 1 :]
    pair_ref, halo_ref, coef_ref, edge_ref, data_ref, prior_ref, total_ref = refs
    me, step = place_on("mod"), place_on("tm")
    side, base, reach, held = me % 2, me - me % 2, 2 * shard, frames // 2
    first_frame, total_frames = step * frames + side * held, steps * frames
    zero_row = jnp.zeros((1, LANES), jnp.float32)

    alone = jnp.where(side == 0, step == 0, step == steps - 1)
    halo = jnp.where(alone, 0.0, halo_ref[...])
    cells, below, above = [], [], []
    for t in range(held + 2):
        frame = side * held + t - 1
        inside = (frame >= 0) & (frame < frames)
        cells.append(jnp.where(inside, pair_ref[jnp.clip(frame, 0, frames - 1)], halo))
        low, high = zero_row, zero_row
        for k in range(2, mods):
            source = me ^ k
            for f in range(frames):
                at = shard + 2 * f
                here = frame == f
                high = jnp.where((source == base + 2) & here, pieces[k - 1][at : at + 1, :], high)
                low = jnp.where((source == base - 1) & here, pieces[k - 1][at + 1 : at + 2, :], low)
        below.append(low)
        above.append(high)

    row_id = lax.broadcasted_iota(jnp.int32, (reach, LANES), 0)

    def from_next(body, last):
        return jnp.where(row_id == reach - 1, last, pltpu.roll(body, reach - 1, 0))

    def from_last(body, first):
        return jnp.where(row_id == 0, first, pltpu.roll(body, 1, 0))

    coef = [coef_ref[i] for i in range(4)]
    edge = [edge_ref[i, SUB - 1 : SUB, :] for i in range(4)]

    def moved(share, base, ahead):
        return share[0] * base + share[1] * ahead + share[2] * row_ahead(base) + share[3] * row_ahead(ahead)

    flow, flow_edge = [], []
    for t in range(held + 1):
        frame = first_frame + t - 1
        valid = (frame >= 0) & (frame <= total_frames - 2)
        ahead = from_next(cells[t], above[t])
        flow.append(jnp.where(valid, cells[t + 1] - moved(coef, cells[t], ahead), 0.0))
        if t > 0:
            value = below[t + 1] - moved(edge, below[t], cells[t][0:1])
            flow_edge.append(jnp.where(valid & (me > 1), value, 0.0))
    total = data_ref[...]
    for t in range(held):
        square = flow[t + 1] * flow[t + 1]
        for r in range(0, reach, SUB):
            total += square[r : r + SUB]
        own, rim = flow[t + 1], flow_edge[t]
        spread_to = (
            coef[0] * own
            + from_last(coef[1] * own, edge[1] * rim)
            + row_behind(coef[2] * own + from_last(coef[3] * own, edge[3] * rim))
        )
        prior_ref[t] = flow[t] - spread_to
    total_ref[...] = total


def final_kernel(plan, entries, *refs):
    mods, half, width, shard = plan.mods, plan.half, plan.width, plan.shard
    pieces = refs[:mods]
    prior_ref, coef_ref, edge_ref, hess_ref, curvature_ref = refs[mods:]
    me = place_on("mod")
    side, held = me % 2, plan.frames // 2
    mine = pl.ds(pl.multiple_of(side * shard, SUB), shard)
    for f in range(held):
        start = half + SUB + f * shard
        hess_ref[side * held + f] = prior_ref[f, mine, :]
        hess_ref[(1 - side) * held + f] = pieces[1][start : start + shard, :]
    lane = lax.broadcasted_iota(jnp.int32, (half, LANES), 1)
    for parity in range(2):
        own = pl.ds(parity, half, stride=2)
        for k, piece in enumerate(pieces):
            source = me ^ k
            frame, group = source // plan.groups, source % plan.groups
            turn = (group * width - parity * width + LANES) % LANES
            moved = pltpu.roll(piece[0:half, :], turn, 1)
            hess_ref[frame, own, :] += jnp.where(lane // width == group, moved, 0.0)
    zero_row = jnp.zeros((1, LANES), jnp.float32)
    total, above, below = zero_row, zero_row, zero_row
    for k, piece in enumerate(pieces):
        source = me ^ k
        total += piece[half + 2 : half + 3, :]
        above = jnp.where((source == me + 1) & (side == 1), piece[half : half + 1, :], above)
        below = jnp.where((source == me - 1) & (side == 0), piece[half + 1 : half + 2, :], below)
    last, top, rim = slice(shard - 1, shard), slice(2 * shard - 1, 2 * shard), slice(SUB - 1, SUB)
    hess_ref[0, last, :] -= coef_ref[1, top, :] * above + coef_ref[3, top, :] * row_ahead(above)
    hess_ref[plan.frames - 1, 0:1, :] -= edge_ref[1, rim, :] * below + row_behind(edge_ref[3, rim, :] * below)
    curvature_ref[0] = jnp.sum(total) / entries


def exchange(arrays, axis):
    count = lax.axis_size(axis)
    came = {0: arrays[0]}
    for k in reversed(range(1, count)):
        came[k] = lax.ppermute(arrays[k], axis, [(i, i ^ k) for i in range(count)])
    return [came[k] for k in range(count)]


def per_device(phase, direction, pupil_mask, mod_tilts, wind_codes, noise_weight):
    frames, shard, rows = phase.shape
    mods, steps = lax.axis_size("mod"), lax.axis_size("tm")
    plan = Plan(frames, shard, rows, mod_tilts.shape[0], mods)
    total_frames = frames * steps
    cells, wide = plan.cells, plan.tiles * LANES
    tables = [jnp.asarray(t) for t in roof_tables(plan)]
    phase, direction, pupil_mask, wind_codes, noise_weight, *tables = [
        pltpu.with_memory_space_constraint(array, pltpu.HBM)
        for array in (phase, direction, pupil_mask, wind_codes, noise_weight, *tables)
    ]

    def f32(*shape):
        return jax.ShapeDtypeStruct(shape, jnp.float32)

    def bf16(*shape):
        return jax.ShapeDtypeStruct(shape, jnp.bfloat16)

    def scratch(shape):
        return pltpu.VMEM(shape.shape, shape.dtype)

    def call(kernel, name, outs, in_specs, out_specs=None, scratch_shapes=(), aliases=None, work=0.02):
        return pl.pallas_call(
            kernel,
            out_shape=outs,
            in_specs=in_specs,
            out_specs=out_specs or [VMEM] * len(outs),
            scratch_shapes=list(scratch_shapes),
            input_output_aliases=aliases or {},
            compiler_params=params(),
            cost_estimate=pl.CostEstimate(
                flops=int(work * 1.1e9), bytes_accessed=int(work * 3.6e6), transcendentals=0
            ),
            name=name,
        )

    rows_in = shard + plan.extra
    *packed, direction_near = call(
        functools.partial(pack_kernel, plan),
        "pack",
        [f32(rows_in + (frames * shard if k == 1 else 0), LANES) for k in range(mods)] + [f32(*phase.shape)],
        [HBM] * 2,
        scratch_shapes=[scratch(phase), pltpu.SemaphoreType.DMA((2,))],
        work=1.2,
    )(phase, direction)
    tilts = jnp.broadcast_to(mod_tilts.astype(jnp.float32)[:, None], (plan.points, LANES))
    packed = call(
        functools.partial(label_kernel, plan),
        "label",
        [f32(*p.shape) for p in packed],
        [VMEM] * (mods + 1),
        aliases={k + 1: k for k in range(mods)},
    )(tilts, *packed)
    pieces = exchange(packed, "mod")

    mask, noise, coef, edge = call(
        functools.partial(prep_kernel, plan),
        "prepare",
        [f32(2, cells, LANES), f32(2, 2, cells, LANES), f32(4, 2 * shard, LANES), f32(4, SUB, LANES)],
        [VMEM] + [HBM] * 3,
        scratch_shapes=[
            pltpu.VMEM(pupil_mask.shape, jnp.int32),
            pltpu.VMEM(noise_weight.shape[1:], jnp.float32),
            pltpu.VMEM((2 * shard + SUB, LANES), jnp.int32),
            pltpu.SemaphoreType.DMA((4,)),
        ],
        work=1.5,
    )(packed[0], pupil_mask, noise_weight, wind_codes)

    pair, edge_frame = call(
        functools.partial(relay_kernel, plan),
        "relay",
        [f32(frames, 2 * shard, LANES), f32(2 * shard, LANES)],
        [VMEM] * 3,
        work=0.05,
    )(direction_near, pieces[1], edge)
    ends = [(t * mods + m, (t + 1) * mods + m - 1) for t in range(steps - 1) for m in range(1, mods, 2)]
    ends += [((steps - 1) * mods + m, m - 1) for m in range(1, mods, 2)]
    halo = lax.ppermute(edge_frame, ("tm", "mod"), ends + [(b, a) for a, b in ends])

    table = bf16(*tables[0].shape)
    cosine, sine, image, weights, data_total, even_back, odd_back = call(
        functools.partial(forward_kernel, plan),
        "forward",
        [f32(2, cells, wide), f32(2, cells, wide), f32(2, cells, 4 * wide), f32(3, 2, cells, LANES), f32(SUB, LANES)]
        + [table] * 2,
        [VMEM] * (mods + 2) + [HBM] * 4,
        scratch_shapes=[
            scratch(s)
            for s in (f32(2, cells, LANES),) * 2 + (bf16(3 * cells, 4 * wide),) * 2 + (table,) * 2
        ]
        + [pltpu.SemaphoreType.DMA((4,))],
        work=2.8,
    )(*pieces, mask, noise, *tables)

    prior, total = call(
        functools.partial(prior_kernel, plan, steps),
        "prior",
        [f32(frames // 2, 2 * shard, LANES), f32(SUB, LANES)],
        [VMEM] * (mods + 4),
        work=0.4,
    )(*pieces[1:], pair, halo, coef, edge, data_total)
    totals = exchange([total] * steps, "tm")

    sent = call(
        functools.partial(backward_kernel, plan),
        "backward",
        [f32(plan.half + SUB + (frames // 2 * shard if k == 1 else 0), LANES) for k in range(mods)],
        [VMEM] * 8,
        scratch_shapes=[
            scratch(s)
            for s in (f32(cells, LANES),) + (bf16(3 * cells, 2 * wide),) * 2 + (f32(2, cells, 2 * wide),)
        ],
        work=0.8,
    )(cosine, sine, image, weights, even_back, odd_back, halo, prior)
    sent = call(
        functools.partial(seal_kernel, plan, steps),
        "seal",
        [f32(*p.shape) for p in sent],
        [VMEM] * (steps + mods),
        aliases={steps + k: k for k in range(mods)},
    )(*totals[2:], *totals[:2], *sent)
    returned = exchange(sent, "mod")

    hess_vec, curvature = call(
        functools.partial(final_kernel, plan, float(total_frames * plan.pupil * rows)),
        "join",
        [f32(*phase.shape), f32(1)],
        [VMEM] * (mods + 3),
        out_specs=[VMEM, SMEM],
        work=0.8,
    )(*returned, prior, coef, edge)
    return hess_vec, curvature


def solution(mesh):
    return jax.shard_map(
        per_device,
        mesh=mesh,
        in_specs=(
            P(("grp", "tm"), "mod", None),
            P(("grp", "tm"), "mod", None),
            P(),
            P("mod"),
            P("grp", None),
            P(("grp", "tm"), None, None),
        ),
        out_specs=(P(("grp", "tm"), "mod", None), P("grp")),
        check_vma=False,
    )
```

```python
import functools

import jax
import jax.numpy as jnp
import ml_dtypes
import numpy as np
from jax import lax
from jax.experimental import pallas as pl
from jax.experimental.pallas import tpu as pltpu
from jax.sharding import PartitionSpec as P

LANES = 128
SUB = 8
CHUNK = 32
VMEM = pl.BlockSpec(memory_space=pltpu.VMEM)
SMEM = pl.BlockSpec(memory_space=pltpu.SMEM)
HBM = pl.BlockSpec(memory_space=pltpu.HBM)


def params():
    return pltpu.CompilerParams(vmem_limit_bytes=48 * 1024 * 1024)


class Plan:
    def __init__(self, frames, shard, rows, points, mods):
        self.frames, self.shard, self.rows, self.mods = frames, shard, rows, mods
        self.points = points
        self.pupil = shard * mods
        self.length = 2 * self.pupil
        assert rows == LANES and mods % frames == 0 and frames % 2 == 0 and mods % 2 == 0
        self.groups = mods // frames
        self.width = rows // self.groups
        assert 2 * self.width <= LANES
        self.copies = LANES // self.width
        self.total_points = points * mods
        assert self.total_points % self.copies == 0
        self.tiles = self.total_points // self.copies
        self.half = shard // 2
        self.cells = self.pupil // 2
        self.extra = -(-(points + 2 * frames) // SUB) * SUB


def roof_tables(plan):
    cells, length = plan.cells, plan.length
    index = np.arange(cells)
    turned = (index + cells // 2) % cells

    def kernel(gap):
        return 2.0 / length / np.cos(2.0 * np.pi * gap / length)

    even = kernel(2 * turned[:, None] - (2 * index[None, :] + 1))
    odd = kernel(2 * turned[:, None] + 1 - 2 * index[None, :])

    def split(table):
        high = table.astype(ml_dtypes.bfloat16)
        low = (table - high.astype(np.float64)).astype(ml_dtypes.bfloat16)
        return np.concatenate([high, high, low], axis=1)

    return split(even), split(odd), split(even.T), split(odd.T)


def spread(cells, plan, first):
    lane = lax.broadcasted_iota(jnp.int32, cells.shape, 1)
    width = plan.width
    if 2 * width == LANES:
        other = pltpu.roll(cells, width, 1)
        keep = (lane < width) if first == 0 else (lane >= width)
        return jnp.where(keep, cells, other)
    if first:
        cells = pltpu.roll(cells, LANES - first, 1)
    cells = jnp.where(lane < width, cells, 0.0)
    step = width
    while step < LANES:
        cells = cells + pltpu.roll(cells, step, 1)
        step *= 2
    return cells


def lane_sum(cells, plan):
    step = plan.width
    while step < LANES:
        cells = cells + pltpu.roll(cells, step, 1)
        step *= 2
    return cells


def place_on(axis):
    return lax.axis_index(axis)


def place_on(axis):
    return lax.axis_index(axis)


def pack_kernel(plan, phase_hbm, direction_hbm, *refs):
    outs = refs[: plan.mods]
    direction_ref, phase_ref, sems = refs[plan.mods :]
    loads = [
        pltpu.make_async_copy(source, target, sems.at[i])
        for i, (source, target) in enumerate(((direction_hbm, direction_ref), (phase_hbm, phase_ref)))
    ]
    for load in loads:
        load.start()
    me = place_on("mod")
    width, half, shard, frames = plan.width, plan.half, plan.shard, plan.frames
    lane = lax.broadcasted_iota(jnp.int32, (half, LANES), 1)
    for load in loads:
        load.wait()
    for k, out in enumerate(outs):
        dest = me ^ k
        frame, group = dest // plan.groups, dest % plan.groups
        back = (LANES - group * width) % LANES
        ahead = (LANES + width - group * width) % LANES
        for parity in range(2):
            own = pl.ds(parity, half, stride=2)
            one = pltpu.roll(phase_ref[frame, own, :], back, 1)
            two = pltpu.roll(direction_ref[frame, own, :], ahead, 1)
            out[parity * half : (parity + 1) * half, :] = jnp.where(lane < width, one, two)
        rows = []
        for f in range(frames):
            rows += [direction_ref[f, 0:1, :], direction_ref[f, shard - 1 : shard, :]]
        rows += [jnp.zeros((1, LANES), jnp.float32)] * (plan.extra - len(rows))
        out[shard : shard + plan.extra, :] = jnp.concatenate(rows, axis=0)
    for f in range(frames):
        start = shard + plan.extra + f * shard
        outs[1][start : start + shard, :] = direction_ref[f]


def relay_kernel(plan, own_ref, piece_ref, after_ref, pair_ref, send_ref):
    shard, frames = plan.shard, plan.frames
    side = place_on("mod") % 2
    for f in range(frames):
        start = shard + plan.extra + f * shard
        pair_ref[f, pl.ds(pl.multiple_of(side * shard, SUB), shard), :] = own_ref[f]
        pair_ref[f, pl.ds(pl.multiple_of((1 - side) * shard, SUB), shard), :] = piece_ref[start : start + shard, :]
    send_ref[...] = pair_ref[side * (frames - 1)]


def label_kernel(plan, tilt_ref, *refs):
    at = plan.shard + 2 * plan.frames
    for out in refs[plan.mods :]:
        out[at : at + plan.points, :] = tilt_ref[...]


def prep_kernel(plan, seed_ref, mask_hbm, noise_hbm, codes_hbm, *refs):
    tables_hbm, refs = refs[:4], refs[4:]
    mask_out, noise_out, coef_out, edge_out, *tables, mask_ref, noise_ref, codes_ref, sems = refs
    me = place_on("mod")
    shard, cells, quarter_line = plan.shard, plan.cells, plan.pupil // 2
    frame, group = me // plan.groups, me % plan.groups
    group_back = (LANES - group * plan.width) % LANES
    reach = 2 * shard
    begin = pl.multiple_of((me // 2) * reach, SUB)
    before = pl.multiple_of(jnp.maximum(begin - SUB, 0), SUB)
    pairs = [
        (mask_hbm, mask_ref),
        (noise_hbm.at[frame], noise_ref),
        (codes_hbm.at[pl.ds(before, SUB)], codes_ref.at[0:SUB]),
        (codes_hbm.at[pl.ds(begin, reach)], codes_ref.at[SUB : SUB + reach]),
        *zip(tables_hbm, tables),
    ]
    loads = [pltpu.make_async_copy(source, target, sems.at[i]) for i, (source, target) in enumerate(pairs)]
    for load in loads:
        load.start()

    lane_group = lax.broadcasted_iota(jnp.int32, (CHUNK, LANES), 1) // plan.width

    def own_rows(cells_in):
        if plan.copies == 2:
            return jnp.where(lane_group == group, cells_in, pltpu.roll(cells_in, plan.width, 1))
        return spread(pltpu.roll(cells_in, group_back, 1), plan, 0)

    loads[0].wait()
    for parity in range(2):
        for row in range(0, cells, CHUNK):
            picked = mask_ref[pl.ds(2 * row + parity, CHUNK, stride=2), :].astype(jnp.float32)
            mask_out[parity, row : row + CHUNK, :] = own_rows(picked)
    loads[1].wait()
    for parity in range(2):
        for row in range(0, cells, CHUNK):
            low_half = row < cells // 2
            inner = 2 * (row % (cells // 2)) + parity
            for side, block in enumerate((2, 0) if low_half else (1, 3)):
                picked = noise_ref[pl.ds(block * quarter_line + inner, CHUNK, stride=2), :]
                noise_out[side, parity, row : row + CHUNK, :] = own_rows(picked)
    loads[2].wait()
    loads[3].wait()
    for i, share in enumerate(shares(codes_ref[SUB : SUB + reach, :])):
        coef_out[i] = share
    for i, share in enumerate(shares(codes_ref[0:SUB, :])):
        edge_out[i] = jnp.where(me > 1, share, 0.0)
    for load in loads[4:]:
        load.wait()


def wave(turns):
    quarters = jnp.round(turns * 4.0)
    angle = (turns - quarters * 0.25) * (2.0 * np.pi)
    square = angle * angle
    sin_part = ((-1.9515295891e-4 * square + 8.3321608736e-3) * square - 1.6666654611e-1) * square * angle + angle
    cos_part = (
        (2.443315711809948e-5 * square - 1.388731625493765e-3) * square + 4.166664568298827e-2
    ) * (square * square) + (1.0 - 0.5 * square)
    count = quarters.astype(jnp.int32)
    odd = (count & 1) != 0
    cosine = jnp.where(odd, sin_part, cos_part)
    sine = jnp.where(odd, cos_part, sin_part)
    cosine = jnp.where(((count + 1) & 2) != 0, -cosine, cosine)
    sine = jnp.where((count & 2) != 0, -sine, sine)
    return cosine, sine


def put_split(ref, row, rows, cells, column, value):
    high = value.astype(jnp.bfloat16)
    low = (value - high.astype(jnp.float32)).astype(jnp.bfloat16)
    where = slice(column, column + LANES)
    ref[row : row + rows, where] = high
    ref[cells + row : cells + row + rows, where] = low
    ref[2 * cells + row : 2 * cells + row + rows, where] = high


def forward_kernel(plan, *refs):
    mods, half, cells = plan.mods, plan.half, plan.cells
    tiles, wide = plan.tiles, plan.tiles * LANES
    pieces = refs[:mods]
    mask_ref, noise_ref, even_ref, odd_ref = refs[mods : mods + 4]
    cos_ref, sin_ref, image_ref, weight_ref, total_ref = refs[mods + 4 : mods + 9]
    turn_ref, dir_ref, even_in_ref, odd_in_ref = refs[mods + 9 :]
    me = place_on("mod")
    lane_row = lax.broadcasted_iota(jnp.int32, (1, LANES), 1)

    for k, piece in enumerate(pieces):
        place = pl.ds(pl.multiple_of((me ^ k) * half, SUB), half)
        for parity in range(2):
            cells_in = piece[parity * half : (parity + 1) * half, :]
            turn_ref[parity, place, :] = spread(cells_in, plan, 0) * (0.5 / np.pi)
            dir_ref[parity, place, :] = spread(cells_in, plan, plan.width)

    tilt_rows = [jnp.zeros((1, LANES), jnp.float32)] * tiles
    for k, piece in enumerate(pieces):
        for p in range(plan.points):
            tile, slot = divmod(k * plan.points + p, plan.copies)
            at = plan.shard + 2 * plan.frames + p
            row = piece[at : at + 1, :]
            tilt_rows[tile] = jnp.where(lane_row // plan.width == slot, row, tilt_rows[tile])

    def tilted(tile, spots):
        tilt = spots.astype(jnp.float32) / plan.length * tilt_rows[tile]
        return wave(tilt - jnp.round(tilt))

    steps = [tilted(tile, jnp.full((1, LANES), 2 * CHUNK, jnp.int32)) for tile in range(tiles)]
    spots = lax.broadcasted_iota(jnp.int32, (CHUNK, LANES), 0) * 2 + plan.pupil // 2

    def fields(parity, ref):
        tilts = [tilted(tile, spots + parity) for tile in range(tiles)]
        for row in range(0, cells, CHUNK):
            here = slice(row, row + CHUNK)
            mask = mask_ref[parity, here, :]
            push = dir_ref[parity, here, :]
            turns = turn_ref[parity, here, :]
            flat_cos, flat_sin = wave(turns)
            flat_cos, flat_sin = flat_cos * mask, flat_sin * mask
            for tile in range(tiles):
                tilt_cos, tilt_sin = tilts[tile]
                cosine = flat_cos * tilt_cos - flat_sin * tilt_sin
                sine = flat_sin * tilt_cos + flat_cos * tilt_sin
                step_cos, step_sin = steps[tile]
                tilts[tile] = (
                    tilt_cos * step_cos - tilt_sin * step_sin,
                    tilt_sin * step_cos + tilt_cos * step_sin,
                )
                at = tile * LANES
                cos_ref[parity, here, at : at + LANES] = cosine
                sin_ref[parity, here, at : at + LANES] = sine
                put_split(ref, row, CHUNK, cells, at, cosine)
                put_split(ref, row, CHUNK, cells, wide + at, sine)
                put_split(ref, row, CHUNK, cells, 2 * wide + at, -sine * push)
                put_split(ref, row, CHUNK, cells, 3 * wide + at, cosine * push)

    def signals(parity, total):
        for row in range(0, cells, CHUNK):
            here = slice(row, row + CHUNK)
            push = dir_ref[parity, here, :]
            even_sum = odd_sum = shift = 0.0
            for tile in range(tiles):
                at = tile * LANES
                cosine = cos_ref[parity, here, at : at + LANES]
                sine = sin_ref[parity, here, at : at + LANES]
                image_cos, image_sin, push_real, push_imag = [
                    image_ref[parity, here, q * wide + at : q * wide + at + LANES] for q in range(4)
                ]
                even_sum += image_sin * push_imag + image_cos * push_real
                odd_sum += cosine * (push_imag - push * image_cos) - sine * (push_real + push * image_sin)
                shift += cosine * image_cos + sine * image_sin
            even_sum = lane_sum(even_sum, plan) * 2.0
            odd_sum = lane_sum(odd_sum, plan)
            signal_after, signal_before = even_sum + odd_sum, even_sum - odd_sum
            weighted_after = noise_ref[0, parity, here, :] * signal_after
            weighted_before = noise_ref[1, parity, here, :] * signal_before
            squares = weighted_after * signal_after + weighted_before * signal_before
            for r in range(0, CHUNK, SUB):
                total += squares[r : r + SUB]
            gap = (weighted_after - weighted_before) * 0.5
            weight_ref[0, parity, here, :] = weighted_after + weighted_before
            weight_ref[1, parity, here, :] = gap
            weight_ref[2, parity, here, :] = -gap * shift
        return total

    def image(parity, table, ref):
        image_ref[parity] = jnp.dot(table[...], ref[...], preferred_element_type=jnp.float32)

    fields(0, even_in_ref)
    fields(1, odd_in_ref)
    image(1, odd_ref, even_in_ref)
    image(0, even_ref, odd_in_ref)
    total = signals(1, jnp.zeros((SUB, LANES), jnp.float32))
    total = signals(0, total)
    total_ref[...] = total / plan.copies


def backward_kernel(plan, *refs):
    cos_ref, sin_ref, image_ref, weight_ref, even_ref, odd_ref, halo_ref, flow_ref, rim_ref, coef_ref, edge_ref = refs[:11]
    outs, prior_ref, (grad_ref, even_in_ref, odd_in_ref, back_ref) = refs[11:-5], refs[-5], refs[-4:]
    half, cells, shard, tiles, wide = plan.half, plan.cells, plan.shard, plan.tiles, plan.tiles * LANES
    me = place_on("mod")

    def fold(parity, ref):
        for row in range(0, cells, CHUNK):
            here = slice(row, row + CHUNK)
            both, gap = weight_ref[0, parity, here, :], weight_ref[1, parity, here, :]
            for tile in range(tiles):
                at = tile * LANES
                cosine = cos_ref[parity, here, at : at + LANES]
                sine = sin_ref[parity, here, at : at + LANES]
                image_cos = image_ref[parity, here, at : at + LANES]
                image_sin = image_ref[parity, here, wide + at : wide + at + LANES]
                put_split(ref, row, CHUNK, cells, at, gap * cosine + both * image_sin)
                put_split(ref, row, CHUNK, cells, wide + at, gap * sine - both * image_cos)

    def back(parity, table, ref):
        back_ref[parity] = jnp.dot(table[...], ref[...], preferred_element_type=jnp.float32)

    fold(0, even_in_ref)
    fold(1, odd_in_ref)
    back(1, even_ref, even_in_ref)
    back(0, odd_ref, odd_in_ref)
    lane = lax.broadcasted_iota(jnp.int32, (CHUNK, LANES), 1)
    for row in range(0, cells, CHUNK):
        here = slice(row, row + CHUNK)
        grads = []
        for parity in range(2):
            grad = weight_ref[2, parity, here, :]
            for tile in range(tiles):
                at = tile * LANES
                grad += cos_ref[parity, here, at : at + LANES] * back_ref[parity, here, at : at + LANES]
                grad += sin_ref[parity, here, at : at + LANES] * back_ref[parity, here, wide + at : wide + at + LANES]
            grads.append(lane_sum(grad, plan) * 2.0)
        grad_ref[here, :] = jnp.where(lane < plan.width, grads[0], grads[1])
    step, side = place_on("tm"), me % 2
    alone = jnp.where(side == 0, step == 0, step == lax.axis_size("tm") - 1)
    rows = [jnp.where(alone, 0.0, r) for r in (halo_ref[0:1, :], halo_ref[2 * shard - 1 : 2 * shard, :])]
    rows += [jnp.zeros((1, LANES), jnp.float32)] * (SUB - len(rows))
    tail = jnp.concatenate(rows, axis=0)
    for k, out in enumerate(outs):
        place = pl.ds(pl.multiple_of((me ^ k) * half, SUB), half)
        out[0:half, :] = grad_ref[place, :]
        out[half : half + SUB, :] = tail
    prior_terms(plan, flow_ref, rim_ref, coef_ref, edge_ref, prior_ref)
    for f in range(plan.frames // 2):
        start = half + SUB + f * shard
        theirs = pl.ds(pl.multiple_of((1 - me % 2) * shard, SUB), shard)
        outs[1][start : start + shard, :] = prior_ref[f, theirs, :]


def prior_terms(plan, flow_ref, rim_ref, coef_ref, edge_ref, prior_ref):
    reach = 2 * plan.shard
    row_id = lax.broadcasted_iota(jnp.int32, (reach, LANES), 0)

    def from_last(body, first):
        return jnp.where(row_id == 0, first, pltpu.roll(body, 1, 0))

    for t in range(plan.frames // 2):
        own, rim = flow_ref[t + 1], rim_ref[t : t + 1, :]
        ahead, both = [
            from_last(coef_ref[i] * own, edge_ref[i, SUB - 1 : SUB, :] * rim) for i in (1, 3)
        ]
        prior_ref[t] = flow_ref[t] - (coef_ref[0] * own + ahead + row_behind(coef_ref[2] * own + both))


def seal_kernel(plan, steps, *refs):
    total = refs[0][...]
    for ref in refs[1:steps]:
        total += ref[...]
    for out in refs[steps + plan.mods :]:
        out[plan.half + 2 : plan.half + 3, :] = jnp.sum(total, axis=0, keepdims=True)


def row_ahead(cells):
    lane = lax.broadcasted_iota(jnp.int32, cells.shape, 1)
    return jnp.where(lane == LANES - 1, 0.0, pltpu.roll(cells, LANES - 1, 1))


def row_behind(cells):
    lane = lax.broadcasted_iota(jnp.int32, cells.shape, 1)
    return jnp.where(lane == 0, 0.0, pltpu.roll(cells, 1, 1))


def shares(codes):
    ahead_x = ((codes & 3).astype(jnp.float32) + 0.5) / 4.0
    ahead_r = ((codes >> 2).astype(jnp.float32) + 0.5) / 4.0
    return (1.0 - ahead_x) * (1.0 - ahead_r), ahead_x * (1.0 - ahead_r), (1.0 - ahead_x) * ahead_r, ahead_x * ahead_r


def prior_kernel(plan, steps, *refs):
    mods, shard, frames = plan.mods, plan.shard, plan.frames
    pieces, refs = refs[: mods - 1], refs[mods - 1 :]
    pair_ref, halo_ref, coef_ref, edge_ref, data_ref, flow_ref, rim_ref, total_ref = refs
    me, step = place_on("mod"), place_on("tm")
    side, base, reach, held = me % 2, me - me % 2, 2 * shard, frames // 2
    first_frame, total_frames = step * frames + side * held, steps * frames
    zero_row = jnp.zeros((1, LANES), jnp.float32)

    alone = jnp.where(side == 0, step == 0, step == steps - 1)
    halo = jnp.where(alone, 0.0, halo_ref[...])
    cells, below, above = [], [], []
    for t in range(held + 2):
        frame = side * held + t - 1
        inside = (frame >= 0) & (frame < frames)
        cells.append(jnp.where(inside, pair_ref[jnp.clip(frame, 0, frames - 1)], halo))
        low, high = zero_row, zero_row
        for k in range(2, mods):
            source = me ^ k
            for f in range(frames):
                at = shard + 2 * f
                here = frame == f
                high = jnp.where((source == base + 2) & here, pieces[k - 1][at : at + 1, :], high)
                low = jnp.where((source == base - 1) & here, pieces[k - 1][at + 1 : at + 2, :], low)
        below.append(low)
        above.append(high)

    row_id = lax.broadcasted_iota(jnp.int32, (reach, LANES), 0)

    def from_next(body, last):
        return jnp.where(row_id == reach - 1, last, pltpu.roll(body, reach - 1, 0))

    coef = [coef_ref[i] for i in range(4)]
    edge = [edge_ref[i, SUB - 1 : SUB, :] for i in range(4)]

    def moved(share, base, ahead):
        return share[0] * base + share[1] * ahead + share[2] * row_ahead(base) + share[3] * row_ahead(ahead)

    flow, flow_edge = [], []
    for t in range(held + 1):
        frame = first_frame + t - 1
        valid = (frame >= 0) & (frame <= total_frames - 2)
        ahead = from_next(cells[t], above[t])
        flow.append(jnp.where(valid, cells[t + 1] - moved(coef, cells[t], ahead), 0.0))
        if t > 0:
            value = below[t + 1] - moved(edge, below[t], cells[t][0:1])
            flow_edge.append(jnp.where(valid & (me > 1), value, 0.0))
    total = data_ref[...]
    for t in range(held):
        square = flow[t + 1] * flow[t + 1]
        for r in range(0, reach, SUB):
            total += square[r : r + SUB]
    for t in range(held + 1):
        flow_ref[t] = flow[t]
    rim_ref[...] = jnp.concatenate(flow_edge + [zero_row] * (SUB - held), axis=0)
    total_ref[...] = total


def final_kernel(plan, entries, *refs):
    mods, half, width, shard = plan.mods, plan.half, plan.width, plan.shard
    pieces = refs[:mods]
    prior_ref, coef_ref, edge_ref, hess_ref, curvature_ref = refs[mods:]
    me = place_on("mod")
    side, held = me % 2, plan.frames // 2
    mine = pl.ds(pl.multiple_of(side * shard, SUB), shard)
    for f in range(held):
        start = half + SUB + f * shard
        hess_ref[side * held + f] = prior_ref[f, mine, :]
        hess_ref[(1 - side) * held + f] = pieces[1][start : start + shard, :]
    lane = lax.broadcasted_iota(jnp.int32, (half, LANES), 1)
    for parity in range(2):
        own = pl.ds(parity, half, stride=2)
        for k, piece in enumerate(pieces):
            source = me ^ k
            frame, group = source // plan.groups, source % plan.groups
            turn = (group * width - parity * width + LANES) % LANES
            moved = pltpu.roll(piece[0:half, :], turn, 1)
            hess_ref[frame, own, :] += jnp.where(lane // width == group, moved, 0.0)
    zero_row = jnp.zeros((1, LANES), jnp.float32)
    total, above, below = zero_row, zero_row, zero_row
    for k, piece in enumerate(pieces):
        source = me ^ k
        total += piece[half + 2 : half + 3, :]
        above = jnp.where((source == me + 1) & (side == 1), piece[half : half + 1, :], above)
        below = jnp.where((source == me - 1) & (side == 0), piece[half + 1 : half + 2, :], below)
    last, top, rim = slice(shard - 1, shard), slice(2 * shard - 1, 2 * shard), slice(SUB - 1, SUB)
    hess_ref[0, last, :] -= coef_ref[1, top, :] * above + coef_ref[3, top, :] * row_ahead(above)
    hess_ref[plan.frames - 1, 0:1, :] -= edge_ref[1, rim, :] * below + row_behind(edge_ref[3, rim, :] * below)
    curvature_ref[0] = jnp.sum(total) / entries


def exchange(arrays, axis):
    count = lax.axis_size(axis)
    came = {0: arrays[0]}
    for k in reversed(range(1, count)):
        came[k] = lax.ppermute(arrays[k], axis, [(i, i ^ k) for i in range(count)])
    return [came[k] for k in range(count)]


def per_device(phase, direction, pupil_mask, mod_tilts, wind_codes, noise_weight):
    frames, shard, rows = phase.shape
    mods, steps = lax.axis_size("mod"), lax.axis_size("tm")
    plan = Plan(frames, shard, rows, mod_tilts.shape[0], mods)
    total_frames = frames * steps
    cells, wide = plan.cells, plan.tiles * LANES
    tables = [jnp.asarray(t) for t in roof_tables(plan)]
    phase, direction, pupil_mask, wind_codes, noise_weight, *tables = [
        pltpu.with_memory_space_constraint(array, pltpu.HBM)
        for array in (phase, direction, pupil_mask, wind_codes, noise_weight, *tables)
    ]

    def f32(*shape):
        return jax.ShapeDtypeStruct(shape, jnp.float32)

    def bf16(*shape):
        return jax.ShapeDtypeStruct(shape, jnp.bfloat16)

    def scratch(shape):
        return pltpu.VMEM(shape.shape, shape.dtype)

    def call(kernel, name, outs, in_specs, out_specs=None, scratch_shapes=(), aliases=None, work=0.02):
        return pl.pallas_call(
            kernel,
            out_shape=outs,
            in_specs=in_specs,
            out_specs=out_specs or [VMEM] * len(outs),
            scratch_shapes=list(scratch_shapes),
            input_output_aliases=aliases or {},
            compiler_params=params(),
            cost_estimate=pl.CostEstimate(
                flops=int(work * 1.1e9), bytes_accessed=int(work * 3.6e6), transcendentals=0
            ),
            name=name,
        )

    rows_in = shard + plan.extra
    *packed, direction_near = call(
        functools.partial(pack_kernel, plan),
        "pack",
        [f32(rows_in + (frames * shard if k == 1 else 0), LANES) for k in range(mods)] + [f32(*phase.shape)],
        [HBM] * 2,
        scratch_shapes=[scratch(phase), pltpu.SemaphoreType.DMA((2,))],
        work=1.2,
    )(phase, direction)
    tilts = jnp.broadcast_to(mod_tilts.astype(jnp.float32)[:, None], (plan.points, LANES))
    packed = call(
        functools.partial(label_kernel, plan),
        "label",
        [f32(*p.shape) for p in packed],
        [VMEM] * (mods + 1),
        aliases={k + 1: k for k in range(mods)},
    )(tilts, *packed)
    pieces = exchange(packed, "mod")

    table = bf16(*tables[0].shape)
    mask, noise, coef, edge, even, odd, even_back, odd_back = call(
        functools.partial(prep_kernel, plan),
        "prepare",
        [f32(2, cells, LANES), f32(2, 2, cells, LANES), f32(4, 2 * shard, LANES), f32(4, SUB, LANES)]
        + [table] * 4,
        [VMEM] + [HBM] * 7,
        scratch_shapes=[
            pltpu.VMEM(pupil_mask.shape, jnp.int32),
            pltpu.VMEM(noise_weight.shape[1:], jnp.float32),
            pltpu.VMEM((2 * shard + SUB, LANES), jnp.int32),
            pltpu.SemaphoreType.DMA((8,)),
        ],
        work=1.5,
    )(packed[0], pupil_mask, noise_weight, wind_codes, *tables)

    pair, edge_frame = call(
        functools.partial(relay_kernel, plan),
        "relay",
        [f32(frames, 2 * shard, LANES), f32(2 * shard, LANES)],
        [VMEM] * 3,
        work=0.05,
    )(direction_near, pieces[1], edge)
    ends = [(t * mods + m, (t + 1) * mods + m - 1) for t in range(steps - 1) for m in range(1, mods, 2)]
    ends += [((steps - 1) * mods + m, m - 1) for m in range(1, mods, 2)]
    halo = lax.ppermute(edge_frame, ("tm", "mod"), ends + [(b, a) for a, b in ends])

    cosine, sine, image, weights, data_total = call(
        functools.partial(forward_kernel, plan),
        "forward",
        [f32(2, cells, wide), f32(2, cells, wide), f32(2, cells, 4 * wide), f32(3, 2, cells, LANES), f32(SUB, LANES)],
        [VMEM] * (mods + 4),
        scratch_shapes=[
            scratch(s)
            for s in (f32(2, cells, LANES),) * 2 + (bf16(3 * cells, 4 * wide),) * 2
        ],
        work=2.8,
    )(*pieces, mask, noise, even, odd)

    flow, rim, total = call(
        functools.partial(prior_kernel, plan, steps),
        "prior",
        [f32(frames // 2 + 1, 2 * shard, LANES), f32(SUB, LANES), f32(SUB, LANES)],
        [VMEM] * (mods + 4),
        work=0.4,
    )(*pieces[1:], pair, halo, coef, edge, data_total)
    totals = exchange([total] * steps, "tm")

    *sent, prior = call(
        functools.partial(backward_kernel, plan),
        "backward",
        [f32(plan.half + SUB + (frames // 2 * shard if k == 1 else 0), LANES) for k in range(mods)]
        + [f32(frames // 2, 2 * shard, LANES)],
        [VMEM] * 11,
        scratch_shapes=[
            scratch(s)
            for s in (f32(cells, LANES),) + (bf16(3 * cells, 2 * wide),) * 2 + (f32(2, cells, 2 * wide),)
        ],
        work=0.8,
    )(cosine, sine, image, weights, even_back, odd_back, halo, flow, rim, coef, edge)
    sent = call(
        functools.partial(seal_kernel, plan, steps),
        "seal",
        [f32(*p.shape) for p in sent],
        [VMEM] * (steps + mods),
        aliases={steps + k: k for k in range(mods)},
    )(*totals[2:], *totals[:2], *sent)
    returned = exchange(sent, "mod")

    hess_vec, curvature = call(
        functools.partial(final_kernel, plan, float(total_frames * plan.pupil * rows)),
        "join",
        [f32(*phase.shape), f32(1)],
        [VMEM] * (mods + 3),
        out_specs=[VMEM, SMEM],
        work=0.8,
    )(*returned, prior, coef, edge)
    return hess_vec, curvature


def solution(mesh):
    return jax.shard_map(
        per_device,
        mesh=mesh,
        in_specs=(
            P(("grp", "tm"), "mod", None),
            P(("grp", "tm"), "mod", None),
            P(),
            P("mod"),
            P("grp", None),
            P(("grp", "tm"), None, None),
        ),
        out_specs=(P(("grp", "tm"), "mod", None), P("grp")),
        check_vma=False,
    )
```

```python
import functools

import jax
import jax.numpy as jnp
import ml_dtypes
import numpy as np
from jax import lax
from jax.experimental import pallas as pl
from jax.experimental.pallas import tpu as pltpu
from jax.sharding import PartitionSpec as P

LANES = 128
SUB = 8
CHUNK = 32
VMEM = pl.BlockSpec(memory_space=pltpu.VMEM)
SMEM = pl.BlockSpec(memory_space=pltpu.SMEM)
HBM = pl.BlockSpec(memory_space=pltpu.HBM)


def params():
    return pltpu.CompilerParams(vmem_limit_bytes=48 * 1024 * 1024)


class Plan:
    def __init__(self, frames, shard, rows, points, mods):
        self.frames, self.shard, self.rows, self.mods = frames, shard, rows, mods
        self.points = points
        self.pupil = shard * mods
        self.length = 2 * self.pupil
        assert rows == LANES and mods % frames == 0 and frames % 2 == 0 and mods % 2 == 0
        self.groups = mods // frames
        self.width = rows // self.groups
        assert 2 * self.width <= LANES
        self.copies = LANES // self.width
        self.total_points = points * mods
        assert self.total_points % self.copies == 0
        self.tiles = self.total_points // self.copies
        self.half = shard // 2
        self.cells = self.pupil // 2
        self.extra = -(-(points + 2 * frames) // SUB) * SUB


def roof_tables(plan):
    cells, length = plan.cells, plan.length
    index = np.arange(cells)
    turned = (index + cells // 2) % cells

    def kernel(gap):
        return 2.0 / length / np.cos(2.0 * np.pi * gap / length)

    even = kernel(2 * turned[:, None] - (2 * index[None, :] + 1))
    odd = kernel(2 * turned[:, None] + 1 - 2 * index[None, :])

    def split(table):
        high = table.astype(ml_dtypes.bfloat16)
        low = (table - high.astype(np.float64)).astype(ml_dtypes.bfloat16)
        return np.concatenate([high, low], axis=0)

    return split(even), split(odd), split(even.T), split(odd.T)


def spread(cells, plan, first):
    lane = lax.broadcasted_iota(jnp.int32, cells.shape, 1)
    width = plan.width
    if 2 * width == LANES:
        other = pltpu.roll(cells, width, 1)
        keep = (lane < width) if first == 0 else (lane >= width)
        return jnp.where(keep, cells, other)
    if first:
        cells = pltpu.roll(cells, LANES - first, 1)
    cells = jnp.where(lane < width, cells, 0.0)
    step = width
    while step < LANES:
        cells = cells + pltpu.roll(cells, step, 1)
        step *= 2
    return cells


def lane_sum(cells, plan):
    step = plan.width
    while step < LANES:
        cells = cells + pltpu.roll(cells, step, 1)
        step *= 2
    return cells


def place_on(axis):
    return lax.axis_index(axis)


def place_on(axis):
    return lax.axis_index(axis)


def pack_kernel(plan, phase_hbm, direction_hbm, *refs):
    outs = refs[: plan.mods]
    direction_ref, phase_ref, sems = refs[plan.mods :]
    loads = [
        pltpu.make_async_copy(source, target, sems.at[i])
        for i, (source, target) in enumerate(((direction_hbm, direction_ref), (phase_hbm, phase_ref)))
    ]
    for load in loads:
        load.start()
    me = place_on("mod")
    width, half, shard, frames = plan.width, plan.half, plan.shard, plan.frames
    lane = lax.broadcasted_iota(jnp.int32, (half, LANES), 1)
    for load in loads:
        load.wait()
    for k, out in enumerate(outs):
        dest = me ^ k
        frame, group = dest // plan.groups, dest % plan.groups
        back = (LANES - group * width) % LANES
        ahead = (LANES + width - group * width) % LANES
        for parity in range(2):
            own = pl.ds(parity, half, stride=2)
            one = pltpu.roll(phase_ref[frame, own, :], back, 1)
            two = pltpu.roll(direction_ref[frame, own, :], ahead, 1)
            out[parity * half : (parity + 1) * half, :] = jnp.where(lane < width, one, two)
        rows = []
        for f in range(frames):
            rows += [direction_ref[f, 0:1, :], direction_ref[f, shard - 1 : shard, :]]
        rows += [jnp.zeros((1, LANES), jnp.float32)] * (plan.extra - len(rows))
        out[shard : shard + plan.extra, :] = jnp.concatenate(rows, axis=0)
    for f in range(frames):
        start = shard + plan.extra + f * shard
        outs[1][start : start + shard, :] = direction_ref[f]


def relay_kernel(plan, own_ref, piece_ref, after_ref, pair_ref, send_ref):
    shard, frames = plan.shard, plan.frames
    side = place_on("mod") % 2
    for f in range(frames):
        start = shard + plan.extra + f * shard
        pair_ref[f, pl.ds(pl.multiple_of(side * shard, SUB), shard), :] = own_ref[f]
        pair_ref[f, pl.ds(pl.multiple_of((1 - side) * shard, SUB), shard), :] = piece_ref[start : start + shard, :]
    send_ref[...] = pair_ref[side * (frames - 1)]


def label_kernel(plan, tilt_ref, *refs):
    at = plan.shard + 2 * plan.frames
    for out in refs[plan.mods :]:
        out[at : at + plan.points, :] = tilt_ref[...]


def prep_kernel(plan, seed_ref, mask_hbm, noise_hbm, codes_hbm, *refs):
    tables_hbm, refs = refs[:4], refs[4:]
    mask_out, noise_out, coef_out, edge_out, *tables, mask_ref, noise_ref, codes_ref, sems = refs
    me = place_on("mod")
    shard, cells, quarter_line = plan.shard, plan.cells, plan.pupil // 2
    frame, group = me // plan.groups, me % plan.groups
    group_back = (LANES - group * plan.width) % LANES
    reach = 2 * shard
    begin = pl.multiple_of((me // 2) * reach, SUB)
    before = pl.multiple_of(jnp.maximum(begin - SUB, 0), SUB)
    pairs = [
        (mask_hbm, mask_ref),
        (noise_hbm.at[frame], noise_ref),
        (codes_hbm.at[pl.ds(before, SUB)], codes_ref.at[0:SUB]),
        (codes_hbm.at[pl.ds(begin, reach)], codes_ref.at[SUB : SUB + reach]),
        *zip(tables_hbm, tables),
    ]
    loads = [pltpu.make_async_copy(source, target, sems.at[i]) for i, (source, target) in enumerate(pairs)]
    for load in loads:
        load.start()

    lane_group = lax.broadcasted_iota(jnp.int32, (CHUNK, LANES), 1) // plan.width

    def own_rows(cells_in):
        if plan.copies == 2:
            return jnp.where(lane_group == group, cells_in, pltpu.roll(cells_in, plan.width, 1))
        return spread(pltpu.roll(cells_in, group_back, 1), plan, 0)

    loads[0].wait()
    for parity in range(2):
        for row in range(0, cells, CHUNK):
            picked = mask_ref[pl.ds(2 * row + parity, CHUNK, stride=2), :].astype(jnp.float32)
            mask_out[parity, row : row + CHUNK, :] = own_rows(picked)
    loads[1].wait()
    for parity in range(2):
        for row in range(0, cells, CHUNK):
            low_half = row < cells // 2
            inner = 2 * (row % (cells // 2)) + parity
            for side, block in enumerate((2, 0) if low_half else (1, 3)):
                picked = noise_ref[pl.ds(block * quarter_line + inner, CHUNK, stride=2), :]
                noise_out[side, parity, row : row + CHUNK, :] = own_rows(picked)
    loads[2].wait()
    loads[3].wait()
    for i, share in enumerate(shares(codes_ref[SUB : SUB + reach, :])):
        coef_out[i] = share
    for i, share in enumerate(shares(codes_ref[0:SUB, :])):
        edge_out[i] = jnp.where(me > 1, share, 0.0)
    for load in loads[4:]:
        load.wait()


def wave(turns):
    quarters = jnp.round(turns * 4.0)
    angle = (turns - quarters * 0.25) * (2.0 * np.pi)
    square = angle * angle
    sin_part = ((-1.9515295891e-4 * square + 8.3321608736e-3) * square - 1.6666654611e-1) * square * angle + angle
    cos_part = (
        (2.443315711809948e-5 * square - 1.388731625493765e-3) * square + 4.166664568298827e-2
    ) * (square * square) + (1.0 - 0.5 * square)
    count = quarters.astype(jnp.int32)
    odd = (count & 1) != 0
    cosine = jnp.where(odd, sin_part, cos_part)
    sine = jnp.where(odd, cos_part, sin_part)
    cosine = jnp.where(((count + 1) & 2) != 0, -cosine, cosine)
    sine = jnp.where((count & 2) != 0, -sine, sine)
    return cosine, sine


def product(table_ref, ref):
    cells = ref.shape[0] // 2
    first = jnp.dot(table_ref[...], ref[:cells], preferred_element_type=jnp.float32)
    second = jnp.dot(table_ref[:cells], ref[cells:], preferred_element_type=jnp.float32)
    return first[:cells] + first[cells:] + second


def put_split(ref, row, rows, cells, column, value):
    high = value.astype(jnp.bfloat16)
    low = (value - high.astype(jnp.float32)).astype(jnp.bfloat16)
    where = slice(column, column + LANES)
    ref[row : row + rows, where] = high
    ref[cells + row : cells + row + rows, where] = low


def forward_kernel(plan, *refs):
    mods, half, cells = plan.mods, plan.half, plan.cells
    tiles, wide = plan.tiles, plan.tiles * LANES
    pieces = refs[:mods]
    mask_ref, noise_ref, even_ref, odd_ref = refs[mods : mods + 4]
    cos_ref, sin_ref, image_ref, weight_ref, total_ref = refs[mods + 4 : mods + 9]
    turn_ref, dir_ref, even_in_ref, odd_in_ref = refs[mods + 9 :]
    me = place_on("mod")
    lane_row = lax.broadcasted_iota(jnp.int32, (1, LANES), 1)

    for k, piece in enumerate(pieces):
        place = pl.ds(pl.multiple_of((me ^ k) * half, SUB), half)
        for parity in range(2):
            cells_in = piece[parity * half : (parity + 1) * half, :]
            turn_ref[parity, place, :] = spread(cells_in, plan, 0) * (0.5 / np.pi)
            dir_ref[parity, place, :] = spread(cells_in, plan, plan.width)

    tilt_rows = [jnp.zeros((1, LANES), jnp.float32)] * tiles
    for k, piece in enumerate(pieces):
        for p in range(plan.points):
            tile, slot = divmod(k * plan.points + p, plan.copies)
            at = plan.shard + 2 * plan.frames + p
            row = piece[at : at + 1, :]
            tilt_rows[tile] = jnp.where(lane_row // plan.width == slot, row, tilt_rows[tile])

    def tilted(tile, spots):
        tilt = spots.astype(jnp.float32) / plan.length * tilt_rows[tile]
        return wave(tilt - jnp.round(tilt))

    steps = [tilted(tile, jnp.full((1, LANES), 2 * CHUNK, jnp.int32)) for tile in range(tiles)]
    spots = lax.broadcasted_iota(jnp.int32, (CHUNK, LANES), 0) * 2 + plan.pupil // 2

    def fields(parity, ref):
        tilts = [tilted(tile, spots + parity) for tile in range(tiles)]
        for row in range(0, cells, CHUNK):
            here = slice(row, row + CHUNK)
            mask = mask_ref[parity, here, :]
            push = dir_ref[parity, here, :]
            turns = turn_ref[parity, here, :]
            flat_cos, flat_sin = wave(turns)
            flat_cos, flat_sin = flat_cos * mask, flat_sin * mask
            for tile in range(tiles):
                tilt_cos, tilt_sin = tilts[tile]
                cosine = flat_cos * tilt_cos - flat_sin * tilt_sin
                sine = flat_sin * tilt_cos + flat_cos * tilt_sin
                step_cos, step_sin = steps[tile]
                tilts[tile] = (
                    tilt_cos * step_cos - tilt_sin * step_sin,
                    tilt_sin * step_cos + tilt_cos * step_sin,
                )
                at = tile * LANES
                cos_ref[parity, here, at : at + LANES] = cosine
                sin_ref[parity, here, at : at + LANES] = sine
                put_split(ref, row, CHUNK, cells, at, cosine)
                put_split(ref, row, CHUNK, cells, wide + at, sine)
                put_split(ref, row, CHUNK, cells, 2 * wide + at, -sine * push)
                put_split(ref, row, CHUNK, cells, 3 * wide + at, cosine * push)

    def signals(parity, total):
        for row in range(0, cells, CHUNK):
            here = slice(row, row + CHUNK)
            push = dir_ref[parity, here, :]
            even_sum = odd_sum = shift = 0.0
            for tile in range(tiles):
                at = tile * LANES
                cosine = cos_ref[parity, here, at : at + LANES]
                sine = sin_ref[parity, here, at : at + LANES]
                image_cos, image_sin, push_real, push_imag = [
                    image_ref[parity, here, q * wide + at : q * wide + at + LANES] for q in range(4)
                ]
                even_sum += image_sin * push_imag + image_cos * push_real
                odd_sum += cosine * (push_imag - push * image_cos) - sine * (push_real + push * image_sin)
                shift += cosine * image_cos + sine * image_sin
            even_sum = lane_sum(even_sum, plan) * 2.0
            odd_sum = lane_sum(odd_sum, plan)
            signal_after, signal_before = even_sum + odd_sum, even_sum - odd_sum
            weighted_after = noise_ref[0, parity, here, :] * signal_after
            weighted_before = noise_ref[1, parity, here, :] * signal_before
            squares = weighted_after * signal_after + weighted_before * signal_before
            for r in range(0, CHUNK, SUB):
                total += squares[r : r + SUB]
            gap = (weighted_after - weighted_before) * 0.5
            weight_ref[0, parity, here, :] = weighted_after + weighted_before
            weight_ref[1, parity, here, :] = gap
            weight_ref[2, parity, here, :] = -gap * shift
        return total

    def image(parity, table, ref):
        image_ref[parity] = product(table, ref)

    fields(0, even_in_ref)
    fields(1, odd_in_ref)
    image(1, odd_ref, even_in_ref)
    image(0, even_ref, odd_in_ref)
    total = signals(1, jnp.zeros((SUB, LANES), jnp.float32))
    total = signals(0, total)
    total_ref[...] = total / plan.copies


def backward_kernel(plan, *refs):
    cos_ref, sin_ref, image_ref, weight_ref, even_ref, odd_ref, halo_ref, flow_ref, rim_ref, coef_ref, edge_ref = refs[:11]
    outs, prior_ref, (grad_ref, even_in_ref, odd_in_ref, back_ref) = refs[11:-5], refs[-5], refs[-4:]
    half, cells, shard, tiles, wide = plan.half, plan.cells, plan.shard, plan.tiles, plan.tiles * LANES
    me = place_on("mod")

    def fold(parity, ref):
        for row in range(0, cells, CHUNK):
            here = slice(row, row + CHUNK)
            both, gap = weight_ref[0, parity, here, :], weight_ref[1, parity, here, :]
            for tile in range(tiles):
                at = tile * LANES
                cosine = cos_ref[parity, here, at : at + LANES]
                sine = sin_ref[parity, here, at : at + LANES]
                image_cos = image_ref[parity, here, at : at + LANES]
                image_sin = image_ref[parity, here, wide + at : wide + at + LANES]
                put_split(ref, row, CHUNK, cells, at, gap * cosine + both * image_sin)
                put_split(ref, row, CHUNK, cells, wide + at, gap * sine - both * image_cos)

    def back(parity, table, ref):
        back_ref[parity] = product(table, ref)

    fold(0, even_in_ref)
    fold(1, odd_in_ref)
    back(1, even_ref, even_in_ref)
    back(0, odd_ref, odd_in_ref)
    lane = lax.broadcasted_iota(jnp.int32, (CHUNK, LANES), 1)
    for row in range(0, cells, CHUNK):
        here = slice(row, row + CHUNK)
        grads = []
        for parity in range(2):
            grad = weight_ref[2, parity, here, :]
            for tile in range(tiles):
                at = tile * LANES
                grad += cos_ref[parity, here, at : at + LANES] * back_ref[parity, here, at : at + LANES]
                grad += sin_ref[parity, here, at : at + LANES] * back_ref[parity, here, wide + at : wide + at + LANES]
            grads.append(lane_sum(grad, plan) * 2.0)
        grad_ref[here, :] = jnp.where(lane < plan.width, grads[0], grads[1])
    step, side = place_on("tm"), me % 2
    alone = jnp.where(side == 0, step == 0, step == lax.axis_size("tm") - 1)
    rows = [jnp.where(alone, 0.0, r) for r in (halo_ref[0:1, :], halo_ref[2 * shard - 1 : 2 * shard, :])]
    rows += [jnp.zeros((1, LANES), jnp.float32)] * (SUB - len(rows))
    tail = jnp.concatenate(rows, axis=0)
    def put(out, at, k):
        place = pl.ds(pl.multiple_of((me ^ k) * half, SUB), half)
        out[at : at + half, :] = grad_ref[place, :]
        out[at + half : at + half + SUB, :] = tail

    *even_outs, near_out = outs
    for k in range(0, plan.mods, 2):
        put(even_outs[k // 2], 0, k)
    for k in range(1, plan.mods, 2):
        put(near_out, (k // 2) * (half + SUB), k)
    prior_terms(plan, flow_ref, rim_ref, coef_ref, edge_ref, prior_ref)
    theirs = pl.ds(pl.multiple_of((1 - me % 2) * shard, SUB), shard)
    for f in range(plan.frames // 2):
        start = plan.mods // 2 * (half + SUB) + f * shard
        near_out[start : start + shard, :] = prior_ref[f, theirs, :]


def prior_terms(plan, flow_ref, rim_ref, coef_ref, edge_ref, prior_ref):
    reach = 2 * plan.shard
    row_id = lax.broadcasted_iota(jnp.int32, (reach, LANES), 0)

    def from_last(body, first):
        return jnp.where(row_id == 0, first, pltpu.roll(body, 1, 0))

    for t in range(plan.frames // 2):
        own, rim = flow_ref[t + 1], rim_ref[t : t + 1, :]
        ahead, both = [
            from_last(coef_ref[i] * own, edge_ref[i, SUB - 1 : SUB, :] * rim) for i in (1, 3)
        ]
        prior_ref[t] = flow_ref[t] - (coef_ref[0] * own + ahead + row_behind(coef_ref[2] * own + both))


def sum_kernel(*refs):
    total = refs[0][...]
    for ref in refs[1:-1]:
        total += ref[...]
    refs[-1][...] = jnp.broadcast_to(jnp.sum(total, axis=0, keepdims=True), total.shape)


def seal_kernel(plan, total_ref, *refs):
    size, count = plan.half + SUB, plan.mods // 2 - 1
    own, near_ref, outs = refs[:count], refs[count], refs[count + 1 :]
    for i, out in enumerate(outs):
        out[0:size, :] = own[i][...]
        out[plan.half + 2 : plan.half + 3, :] = total_ref[0:1, :]
        out[size : 2 * size, :] = near_ref[(i + 1) * size : (i + 2) * size, :]


def row_ahead(cells):
    lane = lax.broadcasted_iota(jnp.int32, cells.shape, 1)
    return jnp.where(lane == LANES - 1, 0.0, pltpu.roll(cells, LANES - 1, 1))


def row_behind(cells):
    lane = lax.broadcasted_iota(jnp.int32, cells.shape, 1)
    return jnp.where(lane == 0, 0.0, pltpu.roll(cells, 1, 1))


def shares(codes):
    ahead_x = ((codes & 3).astype(jnp.float32) + 0.5) / 4.0
    ahead_r = ((codes >> 2).astype(jnp.float32) + 0.5) / 4.0
    return (1.0 - ahead_x) * (1.0 - ahead_r), ahead_x * (1.0 - ahead_r), (1.0 - ahead_x) * ahead_r, ahead_x * ahead_r


def prior_kernel(plan, steps, *refs):
    mods, shard, frames = plan.mods, plan.shard, plan.frames
    pieces, refs = refs[: mods - 1], refs[mods - 1 :]
    pair_ref, halo_ref, coef_ref, edge_ref, data_ref, flow_ref, rim_ref, total_ref = refs
    me, step = place_on("mod"), place_on("tm")
    side, base, reach, held = me % 2, me - me % 2, 2 * shard, frames // 2
    first_frame, total_frames = step * frames + side * held, steps * frames
    zero_row = jnp.zeros((1, LANES), jnp.float32)

    alone = jnp.where(side == 0, step == 0, step == steps - 1)
    halo = jnp.where(alone, 0.0, halo_ref[...])
    cells, below, above = [], [], []
    for t in range(held + 2):
        frame = side * held + t - 1
        inside = (frame >= 0) & (frame < frames)
        cells.append(jnp.where(inside, pair_ref[jnp.clip(frame, 0, frames - 1)], halo))
        low, high = zero_row, zero_row
        for k in range(2, mods):
            source = me ^ k
            for f in range(frames):
                at = shard + 2 * f
                here = frame == f
                high = jnp.where((source == base + 2) & here, pieces[k - 1][at : at + 1, :], high)
                low = jnp.where((source == base - 1) & here, pieces[k - 1][at + 1 : at + 2, :], low)
        below.append(low)
        above.append(high)

    row_id = lax.broadcasted_iota(jnp.int32, (reach, LANES), 0)

    def from_next(body, last):
        return jnp.where(row_id == reach - 1, last, pltpu.roll(body, reach - 1, 0))

    coef = [coef_ref[i] for i in range(4)]
    edge = [edge_ref[i, SUB - 1 : SUB, :] for i in range(4)]

    def moved(share, base, ahead):
        return share[0] * base + share[1] * ahead + share[2] * row_ahead(base) + share[3] * row_ahead(ahead)

    flow, flow_edge = [], []
    for t in range(held + 1):
        frame = first_frame + t - 1
        valid = (frame >= 0) & (frame <= total_frames - 2)
        ahead = from_next(cells[t], above[t])
        flow.append(jnp.where(valid, cells[t + 1] - moved(coef, cells[t], ahead), 0.0))
        if t > 0:
            value = below[t + 1] - moved(edge, below[t], cells[t][0:1])
            flow_edge.append(jnp.where(valid & (me > 1), value, 0.0))
    total = data_ref[...]
    for t in range(held):
        square = flow[t + 1] * flow[t + 1]
        for r in range(0, reach, SUB):
            total += square[r : r + SUB]
    for t in range(held + 1):
        flow_ref[t] = flow[t]
    rim_ref[...] = jnp.concatenate(flow_edge + [zero_row] * (SUB - held), axis=0)
    total_ref[...] = total


def final_kernel(plan, entries, *refs):
    mods, half, width, shard = plan.mods, plan.half, plan.width, plan.shard
    size, pairs = half + SUB, plan.mods // 2
    own_ref, near_ref, far = refs[0], refs[1], refs[2 : pairs + 1]
    sums, refs = refs[pairs + 1 : 2 * pairs + 2], refs[2 * pairs + 2 :]
    prior_ref, coef_ref, edge_ref, hess_ref, curvature_ref = refs
    pieces = [(own_ref, 0), (near_ref, 0)]
    for ref in far:
        pieces += [(ref, 0), (ref, size)]
    me = place_on("mod")
    side, held = me % 2, plan.frames // 2
    mine = pl.ds(pl.multiple_of(side * shard, SUB), shard)
    for f in range(held):
        start = pairs * size + f * shard
        hess_ref[side * held + f] = prior_ref[f, mine, :]
        hess_ref[(1 - side) * held + f] = near_ref[start : start + shard, :]
    lane = lax.broadcasted_iota(jnp.int32, (half, LANES), 1)
    for parity in range(2):
        own = pl.ds(parity, half, stride=2)
        for k, (piece, at) in enumerate(pieces):
            source = me ^ k
            frame, group = source // plan.groups, source % plan.groups
            turn = (group * width - parity * width + LANES) % LANES
            moved = pltpu.roll(piece[at : at + half, :], turn, 1)
            hess_ref[frame, own, :] += jnp.where(lane // width == group, moved, 0.0)
    zero_row = jnp.zeros((1, LANES), jnp.float32)
    total, above, below = zero_row, zero_row, zero_row
    for ref in sums:
        total += ref[0:1, :]
    for ref in far:
        total += ref[half + 2 : half + 3, :]
    for k, (piece, at) in enumerate(pieces):
        source, at = me ^ k, at + half
        above = jnp.where((source == me + 1) & (side == 1), piece[at : at + 1, :], above)
        below = jnp.where((source == me - 1) & (side == 0), piece[at + 1 : at + 2, :], below)
    last, top, rim = slice(shard - 1, shard), slice(2 * shard - 1, 2 * shard), slice(SUB - 1, SUB)
    hess_ref[0, last, :] -= coef_ref[1, top, :] * above + coef_ref[3, top, :] * row_ahead(above)
    hess_ref[plan.frames - 1, 0:1, :] -= edge_ref[1, rim, :] * below + row_behind(edge_ref[3, rim, :] * below)
    curvature_ref[0] = jnp.sum(total) / entries


def exchange(arrays, axis):
    count = lax.axis_size(axis)
    return [arrays[0]] + [
        lax.ppermute(arrays[k], axis, [(i, i ^ k) for i in range(count)]) for k in range(1, count)
    ]


def per_device(phase, direction, pupil_mask, mod_tilts, wind_codes, noise_weight):
    frames, shard, rows = phase.shape
    mods, steps = lax.axis_size("mod"), lax.axis_size("tm")
    plan = Plan(frames, shard, rows, mod_tilts.shape[0], mods)
    total_frames = frames * steps
    cells, wide = plan.cells, plan.tiles * LANES
    tables = [jnp.asarray(t) for t in roof_tables(plan)]
    phase, direction, pupil_mask, wind_codes, noise_weight, *tables = [
        pltpu.with_memory_space_constraint(array, pltpu.HBM)
        for array in (phase, direction, pupil_mask, wind_codes, noise_weight, *tables)
    ]

    def f32(*shape):
        return jax.ShapeDtypeStruct(shape, jnp.float32)

    def bf16(*shape):
        return jax.ShapeDtypeStruct(shape, jnp.bfloat16)

    def scratch(shape):
        return pltpu.VMEM(shape.shape, shape.dtype)

    def call(kernel, name, outs, in_specs, out_specs=None, scratch_shapes=(), aliases=None, work=0.02):
        return pl.pallas_call(
            kernel,
            out_shape=outs,
            in_specs=in_specs,
            out_specs=out_specs or [VMEM] * len(outs),
            scratch_shapes=list(scratch_shapes),
            input_output_aliases=aliases or {},
            compiler_params=params(),
            cost_estimate=pl.CostEstimate(
                flops=int(work * 1.1e9), bytes_accessed=int(work * 3.6e6), transcendentals=0
            ),
            name=name,
        )

    rows_in = shard + plan.extra
    *packed, direction_near = call(
        functools.partial(pack_kernel, plan),
        "pack",
        [f32(rows_in + (frames * shard if k == 1 else 0), LANES) for k in range(mods)] + [f32(*phase.shape)],
        [HBM] * 2,
        scratch_shapes=[scratch(phase), pltpu.SemaphoreType.DMA((2,))],
        work=1.2,
    )(phase, direction)
    tilts = jnp.broadcast_to(mod_tilts.astype(jnp.float32)[:, None], (plan.points, LANES))
    packed = call(
        functools.partial(label_kernel, plan),
        "label",
        [f32(*p.shape) for p in packed],
        [VMEM] * (mods + 1),
        aliases={k + 1: k for k in range(mods)},
    )(tilts, *packed)
    pieces = exchange(packed, "mod")

    table = bf16(*tables[0].shape)
    mask, noise, coef, edge, even, odd, even_back, odd_back = call(
        functools.partial(prep_kernel, plan),
        "prepare",
        [f32(2, cells, LANES), f32(2, 2, cells, LANES), f32(4, 2 * shard, LANES), f32(4, SUB, LANES)]
        + [table] * 4,
        [VMEM] + [HBM] * 7,
        scratch_shapes=[
            pltpu.VMEM(pupil_mask.shape, jnp.int32),
            pltpu.VMEM(noise_weight.shape[1:], jnp.float32),
            pltpu.VMEM((2 * shard + SUB, LANES), jnp.int32),
            pltpu.SemaphoreType.DMA((8,)),
        ],
        work=1.5,
    )(packed[0], pupil_mask, noise_weight, wind_codes, *tables)

    pair, edge_frame = call(
        functools.partial(relay_kernel, plan),
        "relay",
        [f32(frames, 2 * shard, LANES), f32(2 * shard, LANES)],
        [VMEM] * 3,
        work=0.05,
    )(direction_near, pieces[1], edge)
    ends = [(t * mods + m, (t + 1) * mods + m - 1) for t in range(steps - 1) for m in range(1, mods, 2)]
    lone = [m for m in range(0, mods, 2)] + [(steps - 1) * mods + m for m in range(1, mods, 2)]
    if mods % 4 == 0:
        ends += [(a, a ^ 2) for a in lone if a & 2]
    else:
        ends += list(zip(lone[: mods // 2], lone[mods // 2 :]))
    halo = lax.ppermute(edge_frame, ("tm", "mod"), ends + [(b, a) for a, b in ends])

    cosine, sine, image, weights, data_total = call(
        functools.partial(forward_kernel, plan),
        "forward",
        [f32(2, cells, wide), f32(2, cells, wide), f32(2, cells, 4 * wide), f32(3, 2, cells, LANES), f32(SUB, LANES)],
        [VMEM] * (mods + 4),
        scratch_shapes=[
            scratch(s)
            for s in (f32(2, cells, LANES),) * 2 + (bf16(2 * cells, 4 * wide),) * 2
        ],
        work=2.8,
    )(*pieces, mask, noise, even, odd)

    flow, rim, total = call(
        functools.partial(prior_kernel, plan, steps),
        "prior",
        [f32(frames // 2 + 1, 2 * shard, LANES), f32(SUB, LANES), f32(SUB, LANES)],
        [VMEM] * (mods + 4),
        work=0.4,
    )(*pieces[1:], pair, halo, coef, edge, data_total)
    totals = [
        lax.ppermute(total, "tm", [(i, (i + k) % steps) for i in range(steps)]) for k in range(1, steps)
    ]

    size, pairs = plan.half + SUB, mods // 2
    *sent, near, prior = call(
        functools.partial(backward_kernel, plan),
        "backward",
        [f32(size, LANES)] * pairs
        + [f32(pairs * size + frames // 2 * shard, LANES), f32(frames // 2, 2 * shard, LANES)],
        [VMEM] * 11,
        scratch_shapes=[
            scratch(s)
            for s in (f32(cells, LANES),) + (bf16(2 * cells, 2 * wide),) * 2 + (f32(2, cells, 2 * wide),)
        ],
        work=0.8,
    )(cosine, sine, image, weights, even_back, odd_back, halo, flow, rim, coef, edge)

    def swap(array, k):
        return lax.ppermute(array, "mod", [(i, i ^ k) for i in range(mods)])

    near = swap(near, 1)
    total = call(sum_kernel, "sum", [f32(SUB, LANES)], [VMEM] * steps, work=3.0)(*totals, total)[0]
    joined = call(
        functools.partial(seal_kernel, plan),
        "seal",
        [f32(2 * size, LANES)] * (pairs - 1),
        [VMEM] * (pairs + 1),
    )(total, *sent[1:], near)
    far = [swap(array, 2 * k + 2) for k, array in enumerate(joined)]
    sums = [total] + [swap(total, k) for k in range(mods - 1, 0, -2)]

    hess_vec, curvature = call(
        functools.partial(final_kernel, plan, float(total_frames * plan.pupil * rows)),
        "join",
        [f32(*phase.shape), f32(1)],
        [VMEM] * (2 * pairs + 5),
        out_specs=[VMEM, SMEM],
        work=0.8,
    )(sent[0], near, *far, *sums, prior, coef, edge)
    return hess_vec, curvature


def solution(mesh):
    return jax.shard_map(
        per_device,
        mesh=mesh,
        in_specs=(
            P(("grp", "tm"), "mod", None),
            P(("grp", "tm"), "mod", None),
            P(),
            P("mod"),
            P("grp", None),
            P(("grp", "tm"), None, None),
        ),
        out_specs=(P(("grp", "tm"), "mod", None), P("grp")),
        check_vma=False,
    )
```

```python
import functools

import jax
import jax.numpy as jnp
import ml_dtypes
import numpy as np
from jax import lax
from jax.experimental import pallas as pl
from jax.experimental.pallas import tpu as pltpu
from jax.sharding import PartitionSpec as P

LANES = 128
SUB = 8
CHUNK = 32
VMEM = pl.BlockSpec(memory_space=pltpu.VMEM)
SMEM = pl.BlockSpec(memory_space=pltpu.SMEM)
HBM = pl.BlockSpec(memory_space=pltpu.HBM)


def params():
    return pltpu.CompilerParams(vmem_limit_bytes=48 * 1024 * 1024)


class Plan:
    def __init__(self, frames, shard, rows, points, mods):
        self.frames, self.shard, self.rows, self.mods = frames, shard, rows, mods
        self.points = points
        self.pupil = shard * mods
        self.length = 2 * self.pupil
        assert rows == LANES and mods % frames == 0 and frames % 2 == 0 and mods % 2 == 0
        self.groups = mods // frames
        self.width = rows // self.groups
        assert 2 * self.width <= LANES
        self.copies = LANES // self.width
        self.total_points = points * mods
        assert self.total_points % self.copies == 0
        self.tiles = self.total_points // self.copies
        self.half = shard // 2
        self.cells = self.pupil // 2
        self.extra = -(-(points + 2 * frames) // SUB) * SUB


def roof_tables(plan):
    cells, length = plan.cells, plan.length
    index = np.arange(cells)
    turned = (index + cells // 2) % cells

    def kernel(gap):
        return 2.0 / length / np.cos(2.0 * np.pi * gap / length)

    even = kernel(2 * turned[:, None] - (2 * index[None, :] + 1))
    odd = kernel(2 * turned[:, None] + 1 - 2 * index[None, :])

    def split(table):
        high = table.astype(ml_dtypes.bfloat16)
        low = (table - high.astype(np.float64)).astype(ml_dtypes.bfloat16)
        return np.concatenate([high, low], axis=0)

    return split(even), split(odd), split(even.T), split(odd.T)


def spread(cells, plan, first):
    lane = lax.broadcasted_iota(jnp.int32, cells.shape, 1)
    width = plan.width
    if 2 * width == LANES:
        other = pltpu.roll(cells, width, 1)
        keep = (lane < width) if first == 0 else (lane >= width)
        return jnp.where(keep, cells, other)
    if first:
        cells = pltpu.roll(cells, LANES - first, 1)
    cells = jnp.where(lane < width, cells, 0.0)
    step = width
    while step < LANES:
        cells = cells + pltpu.roll(cells, step, 1)
        step *= 2
    return cells


def lane_sum(cells, plan):
    step = plan.width
    while step < LANES:
        cells = cells + pltpu.roll(cells, step, 1)
        step *= 2
    return cells


def place_on(axis):
    return lax.axis_index(axis)


def place_on(axis):
    return lax.axis_index(axis)


def tilt_kernel(tilt_ref, out_ref):
    out_ref[...] = tilt_ref[...]


def pack_kernel(plan, tilt_ref, phase_ref, direction_ref, *refs):
    outs, near_ref = refs[: plan.mods], refs[plan.mods]
    me = place_on("mod")
    width, half, shard, frames = plan.width, plan.half, plan.shard, plan.frames
    lane = lax.broadcasted_iota(jnp.int32, (half, LANES), 1)
    for k, out in enumerate(outs):
        dest = me ^ k
        frame, group = dest // plan.groups, dest % plan.groups
        back = (LANES - group * width) % LANES
        ahead = (LANES + width - group * width) % LANES
        for parity in range(2):
            own = pl.ds(parity, half, stride=2)
            one = pltpu.roll(phase_ref[frame, own, :], back, 1)
            two = pltpu.roll(direction_ref[frame, own, :], ahead, 1)
            out[parity * half : (parity + 1) * half, :] = jnp.where(lane < width, one, two)
        rows = []
        for f in range(frames):
            rows += [direction_ref[f, 0:1, :], direction_ref[f, shard - 1 : shard, :]]
        rows += [tilt_ref[p : p + 1, :] for p in range(plan.points)]
        rows += [jnp.zeros((1, LANES), jnp.float32)] * (plan.extra - len(rows))
        out[shard : shard + plan.extra, :] = jnp.concatenate(rows, axis=0)
    for f in range(frames):
        start = shard + plan.extra + f * shard
        outs[1][start : start + shard, :] = direction_ref[f]
        near_ref[f] = direction_ref[f]


def relay_kernel(plan, own_ref, piece_ref, after_ref, pair_ref, send_ref):
    shard, frames = plan.shard, plan.frames
    side = place_on("mod") % 2
    for f in range(frames):
        start = shard + plan.extra + f * shard
        pair_ref[f, pl.ds(pl.multiple_of(side * shard, SUB), shard), :] = own_ref[f]
        pair_ref[f, pl.ds(pl.multiple_of((1 - side) * shard, SUB), shard), :] = piece_ref[start : start + shard, :]
    send_ref[...] = pair_ref[side * (frames - 1)]


def prep_kernel(plan, seed_ref, mask_hbm, noise_hbm, codes_hbm, *refs):
    tables_hbm, refs = refs[:4], refs[4:]
    mask_out, noise_out, coef_out, edge_out, *tables, mask_ref, noise_ref, codes_ref, sems = refs
    me = place_on("mod")
    shard, cells, quarter_line = plan.shard, plan.cells, plan.pupil // 2
    frame, group = me // plan.groups, me % plan.groups
    group_back = (LANES - group * plan.width) % LANES
    reach = 2 * shard
    begin = pl.multiple_of((me // 2) * reach, SUB)
    before = pl.multiple_of(jnp.maximum(begin - SUB, 0), SUB)
    pairs = [
        (mask_hbm, mask_ref),
        (noise_hbm.at[frame], noise_ref),
        (codes_hbm.at[pl.ds(before, SUB)], codes_ref.at[0:SUB]),
        (codes_hbm.at[pl.ds(begin, reach)], codes_ref.at[SUB : SUB + reach]),
        *zip(tables_hbm, tables),
    ]
    loads = [pltpu.make_async_copy(source, target, sems.at[i]) for i, (source, target) in enumerate(pairs)]
    for load in loads:
        load.start()

    lane_group = lax.broadcasted_iota(jnp.int32, (CHUNK, LANES), 1) // plan.width

    def own_rows(cells_in):
        if plan.copies == 2:
            return jnp.where(lane_group == group, cells_in, pltpu.roll(cells_in, plan.width, 1))
        return spread(pltpu.roll(cells_in, group_back, 1), plan, 0)

    loads[0].wait()
    for parity in range(2):
        for row in range(0, cells, CHUNK):
            picked = mask_ref[pl.ds(2 * row + parity, CHUNK, stride=2), :].astype(jnp.float32)
            mask_out[parity, row : row + CHUNK, :] = own_rows(picked)
    loads[1].wait()
    for parity in range(2):
        for row in range(0, cells, CHUNK):
            low_half = row < cells // 2
            inner = 2 * (row % (cells // 2)) + parity
            for side, block in enumerate((2, 0) if low_half else (1, 3)):
                picked = noise_ref[pl.ds(block * quarter_line + inner, CHUNK, stride=2), :]
                noise_out[side, parity, row : row + CHUNK, :] = own_rows(picked)
    loads[2].wait()
    loads[3].wait()
    for i, share in enumerate(shares(codes_ref[SUB : SUB + reach, :])):
        coef_out[i] = share
    for i, share in enumerate(shares(codes_ref[0:SUB, :])):
        edge_out[i] = jnp.where(me > 1, share, 0.0)
    for load in loads[4:]:
        load.wait()


def wave(turns):
    quarters = jnp.round(turns * 4.0)
    angle = (turns - quarters * 0.25) * (2.0 * np.pi)
    square = angle * angle
    sin_part = ((-1.9515295891e-4 * square + 8.3321608736e-3) * square - 1.6666654611e-1) * square * angle + angle
    cos_part = (
        (2.443315711809948e-5 * square - 1.388731625493765e-3) * square + 4.166664568298827e-2
    ) * (square * square) + (1.0 - 0.5 * square)
    count = quarters.astype(jnp.int32)
    odd = (count & 1) != 0
    cosine = jnp.where(odd, sin_part, cos_part)
    sine = jnp.where(odd, cos_part, sin_part)
    cosine = jnp.where(((count + 1) & 2) != 0, -cosine, cosine)
    sine = jnp.where((count & 2) != 0, -sine, sine)
    return cosine, sine


def product(table_ref, ref):
    cells = ref.shape[0] // 2
    first = jnp.dot(table_ref[...], ref[:cells], preferred_element_type=jnp.float32)
    second = jnp.dot(table_ref[:cells], ref[cells:], preferred_element_type=jnp.float32)
    return first[:cells] + first[cells:] + second


def put_split(ref, row, rows, cells, column, value):
    high = value.astype(jnp.bfloat16)
    low = (value - high.astype(jnp.float32)).astype(jnp.bfloat16)
    where = slice(column, column + LANES)
    ref[row : row + rows, where] = high
    ref[cells + row : cells + row + rows, where] = low


def forward_kernel(plan, *refs):
    mods, half, cells = plan.mods, plan.half, plan.cells
    tiles, wide = plan.tiles, plan.tiles * LANES
    pieces = refs[:mods]
    mask_ref, noise_ref, even_ref, odd_ref = refs[mods : mods + 4]
    cos_ref, sin_ref, image_ref, weight_ref, total_ref = refs[mods + 4 : mods + 9]
    turn_ref, dir_ref, even_in_ref, odd_in_ref = refs[mods + 9 :]
    me = place_on("mod")
    lane_row = lax.broadcasted_iota(jnp.int32, (1, LANES), 1)

    for k, piece in enumerate(pieces):
        place = pl.ds(pl.multiple_of((me ^ k) * half, SUB), half)
        for parity in range(2):
            cells_in = piece[parity * half : (parity + 1) * half, :]
            turn_ref[parity, place, :] = spread(cells_in, plan, 0) * (0.5 / np.pi)
            dir_ref[parity, place, :] = spread(cells_in, plan, plan.width)

    tilt_rows = [jnp.zeros((1, LANES), jnp.float32)] * tiles
    for k, piece in enumerate(pieces):
        for p in range(plan.points):
            tile, slot = divmod(k * plan.points + p, plan.copies)
            at = plan.shard + 2 * plan.frames + p
            row = piece[at : at + 1, :]
            tilt_rows[tile] = jnp.where(lane_row // plan.width == slot, row, tilt_rows[tile])

    def tilted(tile, spots):
        tilt = spots.astype(jnp.float32) / plan.length * tilt_rows[tile]
        return wave(tilt - jnp.round(tilt))

    steps = [tilted(tile, jnp.full((1, LANES), 2 * CHUNK, jnp.int32)) for tile in range(tiles)]
    spots = lax.broadcasted_iota(jnp.int32, (CHUNK, LANES), 0) * 2 + plan.pupil // 2

    def fields(parity, ref):
        tilts = [tilted(tile, spots + parity) for tile in range(tiles)]
        for row in range(0, cells, CHUNK):
            here = slice(row, row + CHUNK)
            mask = mask_ref[parity, here, :]
            push = dir_ref[parity, here, :]
            turns = turn_ref[parity, here, :]
            flat_cos, flat_sin = wave(turns)
            flat_cos, flat_sin = flat_cos * mask, flat_sin * mask
            for tile in range(tiles):
                tilt_cos, tilt_sin = tilts[tile]
                cosine = flat_cos * tilt_cos - flat_sin * tilt_sin
                sine = flat_sin * tilt_cos + flat_cos * tilt_sin
                step_cos, step_sin = steps[tile]
                tilts[tile] = (
                    tilt_cos * step_cos - tilt_sin * step_sin,
                    tilt_sin * step_cos + tilt_cos * step_sin,
                )
                at = tile * LANES
                cos_ref[parity, here, at : at + LANES] = cosine
                sin_ref[parity, here, at : at + LANES] = sine
                put_split(ref, row, CHUNK, cells, at, cosine)
                put_split(ref, row, CHUNK, cells, wide + at, sine)
                put_split(ref, row, CHUNK, cells, 2 * wide + at, -sine * push)
                put_split(ref, row, CHUNK, cells, 3 * wide + at, cosine * push)

    def signals(parity, total):
        for row in range(0, cells, CHUNK):
            here = slice(row, row + CHUNK)
            push = dir_ref[parity, here, :]
            even_sum = odd_sum = shift = 0.0
            for tile in range(tiles):
                at = tile * LANES
                cosine = cos_ref[parity, here, at : at + LANES]
                sine = sin_ref[parity, here, at : at + LANES]
                image_cos, image_sin, push_real, push_imag = [
                    image_ref[parity, here, q * wide + at : q * wide + at + LANES] for q in range(4)
                ]
                even_sum += image_sin * push_imag + image_cos * push_real
                odd_sum += cosine * (push_imag - push * image_cos) - sine * (push_real + push * image_sin)
                shift += cosine * image_cos + sine * image_sin
            even_sum = lane_sum(even_sum, plan) * 2.0
            odd_sum = lane_sum(odd_sum, plan)
            signal_after, signal_before = even_sum + odd_sum, even_sum - odd_sum
            weighted_after = noise_ref[0, parity, here, :] * signal_after
            weighted_before = noise_ref[1, parity, here, :] * signal_before
            squares = weighted_after * signal_after + weighted_before * signal_before
            for r in range(0, CHUNK, SUB):
                total += squares[r : r + SUB]
            gap = (weighted_after - weighted_before) * 0.5
            weight_ref[0, parity, here, :] = weighted_after + weighted_before
            weight_ref[1, parity, here, :] = gap
            weight_ref[2, parity, here, :] = -gap * shift
        return total

    def image(parity, table, ref):
        image_ref[parity] = product(table, ref)

    fields(0, even_in_ref)
    fields(1, odd_in_ref)
    image(1, odd_ref, even_in_ref)
    image(0, even_ref, odd_in_ref)
    total = signals(1, jnp.zeros((SUB, LANES), jnp.float32))
    total = signals(0, total)
    total_ref[...] = total / plan.copies


def backward_kernel(plan, *refs):
    cos_ref, sin_ref, image_ref, weight_ref, even_ref, odd_ref, halo_ref, flow_ref, rim_ref, coef_ref, edge_ref = refs[:11]
    outs, prior_ref, (grad_ref, even_in_ref, odd_in_ref, back_ref) = refs[11:-5], refs[-5], refs[-4:]
    half, cells, shard, tiles, wide = plan.half, plan.cells, plan.shard, plan.tiles, plan.tiles * LANES
    me = place_on("mod")

    def fold(parity, ref):
        for row in range(0, cells, CHUNK):
            here = slice(row, row + CHUNK)
            both, gap = weight_ref[0, parity, here, :], weight_ref[1, parity, here, :]
            for tile in range(tiles):
                at = tile * LANES
                cosine = cos_ref[parity, here, at : at + LANES]
                sine = sin_ref[parity, here, at : at + LANES]
                image_cos = image_ref[parity, here, at : at + LANES]
                image_sin = image_ref[parity, here, wide + at : wide + at + LANES]
                put_split(ref, row, CHUNK, cells, at, gap * cosine + both * image_sin)
                put_split(ref, row, CHUNK, cells, wide + at, gap * sine - both * image_cos)

    def back(parity, table, ref):
        back_ref[parity] = product(table, ref)

    fold(0, even_in_ref)
    fold(1, odd_in_ref)
    back(1, even_ref, even_in_ref)
    back(0, odd_ref, odd_in_ref)
    lane = lax.broadcasted_iota(jnp.int32, (CHUNK, LANES), 1)
    for row in range(0, cells, CHUNK):
        here = slice(row, row + CHUNK)
        grads = []
        for parity in range(2):
            grad = weight_ref[2, parity, here, :]
            for tile in range(tiles):
                at = tile * LANES
                grad += cos_ref[parity, here, at : at + LANES] * back_ref[parity, here, at : at + LANES]
                grad += sin_ref[parity, here, at : at + LANES] * back_ref[parity, here, wide + at : wide + at + LANES]
            grads.append(lane_sum(grad, plan) * 2.0)
        grad_ref[here, :] = jnp.where(lane < plan.width, grads[0], grads[1])
    step, side = place_on("tm"), me % 2
    alone = jnp.where(side == 0, step == 0, step == lax.axis_size("tm") - 1)
    rows = [jnp.where(alone, 0.0, r) for r in (halo_ref[0:1, :], halo_ref[2 * shard - 1 : 2 * shard, :])]
    rows += [jnp.zeros((1, LANES), jnp.float32)] * (SUB - len(rows))
    tail = jnp.concatenate(rows, axis=0)
    def put(out, at, k):
        place = pl.ds(pl.multiple_of((me ^ k) * half, SUB), half)
        out[at : at + half, :] = grad_ref[place, :]
        out[at + half : at + half + SUB, :] = tail

    *even_outs, near_out = outs
    for k in range(0, plan.mods, 2):
        put(even_outs[k // 2], 0, k)
    for k in range(1, plan.mods, 2):
        put(near_out, (k // 2) * (half + SUB), k)
    prior_terms(plan, flow_ref, rim_ref, coef_ref, edge_ref, prior_ref)
    theirs = pl.ds(pl.multiple_of((1 - me % 2) * shard, SUB), shard)
    for f in range(plan.frames // 2):
        start = plan.mods // 2 * (half + SUB) + f * shard
        near_out[start : start + shard, :] = prior_ref[f, theirs, :]


def prior_terms(plan, flow_ref, rim_ref, coef_ref, edge_ref, prior_ref):
    reach = 2 * plan.shard
    row_id = lax.broadcasted_iota(jnp.int32, (reach, LANES), 0)

    def from_last(body, first):
        return jnp.where(row_id == 0, first, pltpu.roll(body, 1, 0))

    for t in range(plan.frames // 2):
        own, rim = flow_ref[t + 1], rim_ref[t : t + 1, :]
        ahead, both = [
            from_last(coef_ref[i] * own, edge_ref[i, SUB - 1 : SUB, :] * rim) for i in (1, 3)
        ]
        prior_ref[t] = flow_ref[t] - (coef_ref[0] * own + ahead + row_behind(coef_ref[2] * own + both))


def sum_kernel(*refs):
    total = refs[0][...]
    for ref in refs[1:-1]:
        total += ref[...]
    refs[-1][...] = jnp.broadcast_to(jnp.sum(total, axis=0, keepdims=True), total.shape)


def seal_kernel(plan, total_ref, *refs):
    size, count = plan.half + SUB, plan.mods // 2 - 1
    own, near_ref, outs = refs[:count], refs[count], refs[count + 1 :]
    for i, out in enumerate(outs):
        out[0:size, :] = own[i][...]
        out[plan.half + 2 : plan.half + 3, :] = total_ref[0:1, :]
        out[size : 2 * size, :] = near_ref[(i + 1) * size : (i + 2) * size, :]


def row_ahead(cells):
    lane = lax.broadcasted_iota(jnp.int32, cells.shape, 1)
    return jnp.where(lane == LANES - 1, 0.0, pltpu.roll(cells, LANES - 1, 1))


def row_behind(cells):
    lane = lax.broadcasted_iota(jnp.int32, cells.shape, 1)
    return jnp.where(lane == 0, 0.0, pltpu.roll(cells, 1, 1))


def shares(codes):
    ahead_x = ((codes & 3).astype(jnp.float32) + 0.5) / 4.0
    ahead_r = ((codes >> 2).astype(jnp.float32) + 0.5) / 4.0
    return (1.0 - ahead_x) * (1.0 - ahead_r), ahead_x * (1.0 - ahead_r), (1.0 - ahead_x) * ahead_r, ahead_x * ahead_r


def prior_kernel(plan, steps, *refs):
    mods, shard, frames = plan.mods, plan.shard, plan.frames
    pieces, refs = refs[: mods - 1], refs[mods - 1 :]
    pair_ref, halo_ref, coef_ref, edge_ref, data_ref, flow_ref, rim_ref, total_ref = refs
    me, step = place_on("mod"), place_on("tm")
    side, base, reach, held = me % 2, me - me % 2, 2 * shard, frames // 2
    first_frame, total_frames = step * frames + side * held, steps * frames
    zero_row = jnp.zeros((1, LANES), jnp.float32)

    alone = jnp.where(side == 0, step == 0, step == steps - 1)
    halo = jnp.where(alone, 0.0, halo_ref[...])
    cells, below, above = [], [], []
    for t in range(held + 2):
        frame = side * held + t - 1
        inside = (frame >= 0) & (frame < frames)
        cells.append(jnp.where(inside, pair_ref[jnp.clip(frame, 0, frames - 1)], halo))
        low, high = zero_row, zero_row
        for k in range(2, mods):
            source = me ^ k
            for f in range(frames):
                at = shard + 2 * f
                here = frame == f
                high = jnp.where((source == base + 2) & here, pieces[k - 1][at : at + 1, :], high)
                low = jnp.where((source == base - 1) & here, pieces[k - 1][at + 1 : at + 2, :], low)
        below.append(low)
        above.append(high)

    row_id = lax.broadcasted_iota(jnp.int32, (reach, LANES), 0)

    def from_next(body, last):
        return jnp.where(row_id == reach - 1, last, pltpu.roll(body, reach - 1, 0))

    coef = [coef_ref[i] for i in range(4)]
    edge = [edge_ref[i, SUB - 1 : SUB, :] for i in range(4)]

    def moved(share, base, ahead):
        return share[0] * base + share[1] * ahead + share[2] * row_ahead(base) + share[3] * row_ahead(ahead)

    flow, flow_edge = [], []
    for t in range(held + 1):
        frame = first_frame + t - 1
        valid = (frame >= 0) & (frame <= total_frames - 2)
        ahead = from_next(cells[t], above[t])
        flow.append(jnp.where(valid, cells[t + 1] - moved(coef, cells[t], ahead), 0.0))
        if t > 0:
            value = below[t + 1] - moved(edge, below[t], cells[t][0:1])
            flow_edge.append(jnp.where(valid & (me > 1), value, 0.0))
    total = data_ref[...]
    for t in range(held):
        square = flow[t + 1] * flow[t + 1]
        for r in range(0, reach, SUB):
            total += square[r : r + SUB]
    for t in range(held + 1):
        flow_ref[t] = flow[t]
    rim_ref[...] = jnp.concatenate(flow_edge + [zero_row] * (SUB - held), axis=0)
    total_ref[...] = total


def final_kernel(plan, entries, *refs):
    mods, half, width, shard = plan.mods, plan.half, plan.width, plan.shard
    size, pairs = half + SUB, plan.mods // 2
    own_ref, near_ref, far = refs[0], refs[1], refs[2 : pairs + 1]
    sums, refs = refs[pairs + 1 : 2 * pairs + 2], refs[2 * pairs + 2 :]
    prior_ref, coef_ref, edge_ref, hess_ref, curvature_ref = refs
    pieces = [(own_ref, 0), (near_ref, 0)]
    for ref in far:
        pieces += [(ref, 0), (ref, size)]
    me = place_on("mod")
    side, held = me % 2, plan.frames // 2
    mine = pl.ds(pl.multiple_of(side * shard, SUB), shard)
    for f in range(held):
        start = pairs * size + f * shard
        hess_ref[side * held + f] = prior_ref[f, mine, :]
        hess_ref[(1 - side) * held + f] = near_ref[start : start + shard, :]
    lane = lax.broadcasted_iota(jnp.int32, (half, LANES), 1)
    for parity in range(2):
        own = pl.ds(parity, half, stride=2)
        for k, (piece, at) in enumerate(pieces):
            source = me ^ k
            frame, group = source // plan.groups, source % plan.groups
            turn = (group * width - parity * width + LANES) % LANES
            moved = pltpu.roll(piece[at : at + half, :], turn, 1)
            hess_ref[frame, own, :] += jnp.where(lane // width == group, moved, 0.0)
    zero_row = jnp.zeros((1, LANES), jnp.float32)
    total, above, below = zero_row, zero_row, zero_row
    for ref in sums:
        total += ref[0:1, :]
    for ref in far:
        total += ref[half + 2 : half + 3, :]
    for k, (piece, at) in enumerate(pieces):
        source, at = me ^ k, at + half
        above = jnp.where((source == me + 1) & (side == 1), piece[at : at + 1, :], above)
        below = jnp.where((source == me - 1) & (side == 0), piece[at + 1 : at + 2, :], below)
    last, top, rim = slice(shard - 1, shard), slice(2 * shard - 1, 2 * shard), slice(SUB - 1, SUB)
    hess_ref[0, last, :] -= coef_ref[1, top, :] * above + coef_ref[3, top, :] * row_ahead(above)
    hess_ref[plan.frames - 1, 0:1, :] -= edge_ref[1, rim, :] * below + row_behind(edge_ref[3, rim, :] * below)
    curvature_ref[0] = jnp.sum(total) / entries


def exchange(arrays, axis):
    count = lax.axis_size(axis)
    return [arrays[0]] + [
        lax.ppermute(arrays[k], axis, [(i, i ^ k) for i in range(count)]) for k in range(1, count)
    ]


def per_device(phase, direction, pupil_mask, mod_tilts, wind_codes, noise_weight):
    frames, shard, rows = phase.shape
    mods, steps = lax.axis_size("mod"), lax.axis_size("tm")
    plan = Plan(frames, shard, rows, mod_tilts.shape[0], mods)
    total_frames = frames * steps
    cells, wide = plan.cells, plan.tiles * LANES
    tables = [jnp.asarray(t) for t in roof_tables(plan)]
    pupil_mask, wind_codes, noise_weight, *tables = [
        pltpu.with_memory_space_constraint(array, pltpu.HBM)
        for array in (pupil_mask, wind_codes, noise_weight, *tables)
    ]

    def f32(*shape):
        return jax.ShapeDtypeStruct(shape, jnp.float32)

    def bf16(*shape):
        return jax.ShapeDtypeStruct(shape, jnp.bfloat16)

    def scratch(shape):
        return pltpu.VMEM(shape.shape, shape.dtype)

    def call(kernel, name, outs, in_specs, out_specs=None, scratch_shapes=(), aliases=None, work=0.02):
        return pl.pallas_call(
            kernel,
            out_shape=outs,
            in_specs=in_specs,
            out_specs=out_specs or [VMEM] * len(outs),
            scratch_shapes=list(scratch_shapes),
            input_output_aliases=aliases or {},
            compiler_params=params(),
            cost_estimate=pl.CostEstimate(
                flops=int(work * 1.1e9), bytes_accessed=int(work * 3.6e6), transcendentals=0
            ),
            name=name,
        )

    rows_in = shard + plan.extra
    tilts = jnp.broadcast_to(mod_tilts.astype(jnp.float32)[:, None], (plan.points, LANES))
    tilts = call(tilt_kernel, "tilts", [f32(plan.points, LANES)], [VMEM], work=0.8)(tilts)[0]
    *packed, direction_near = call(
        functools.partial(pack_kernel, plan),
        "pack",
        [f32(rows_in + (frames * shard if k == 1 else 0), LANES) for k in range(mods)] + [f32(*phase.shape)],
        [VMEM] * 3,
        work=0.3,
    )(tilts, phase, direction)
    pieces = exchange(packed, "mod")

    table = bf16(*tables[0].shape)
    mask, noise, coef, edge, even, odd, even_back, odd_back = call(
        functools.partial(prep_kernel, plan),
        "prepare",
        [f32(2, cells, LANES), f32(2, 2, cells, LANES), f32(4, 2 * shard, LANES), f32(4, SUB, LANES)]
        + [table] * 4,
        [VMEM] + [HBM] * 7,
        scratch_shapes=[
            pltpu.VMEM(pupil_mask.shape, jnp.int32),
            pltpu.VMEM(noise_weight.shape[1:], jnp.float32),
            pltpu.VMEM((2 * shard + SUB, LANES), jnp.int32),
            pltpu.SemaphoreType.DMA((8,)),
        ],
        work=1.5,
    )(packed[0], pupil_mask, noise_weight, wind_codes, *tables)

    pair, edge_frame = call(
        functools.partial(relay_kernel, plan),
        "relay",
        [f32(frames, 2 * shard, LANES), f32(2 * shard, LANES)],
        [VMEM] * 3,
        work=0.05,
    )(direction_near, pieces[1], edge)
    ends = [(t * mods + m, (t + 1) * mods + m - 1) for t in range(steps - 1) for m in range(1, mods, 2)]
    lone = [m for m in range(0, mods, 2)] + [(steps - 1) * mods + m for m in range(1, mods, 2)]
    if mods % 4 == 0:
        ends += [(a, a ^ 2) for a in lone if a & 2]
    else:
        ends += list(zip(lone[: mods // 2], lone[mods // 2 :]))
    halo = lax.ppermute(edge_frame, ("tm", "mod"), ends + [(b, a) for a, b in ends])

    cosine, sine, image, weights, data_total = call(
        functools.partial(forward_kernel, plan),
        "forward",
        [f32(2, cells, wide), f32(2, cells, wide), f32(2, cells, 4 * wide), f32(3, 2, cells, LANES), f32(SUB, LANES)],
        [VMEM] * (mods + 4),
        scratch_shapes=[
            scratch(s)
            for s in (f32(2, cells, LANES),) * 2 + (bf16(2 * cells, 4 * wide),) * 2
        ],
        work=2.8,
    )(*pieces, mask, noise, even, odd)

    flow, rim, total = call(
        functools.partial(prior_kernel, plan, steps),
        "prior",
        [f32(frames // 2 + 1, 2 * shard, LANES), f32(SUB, LANES), f32(SUB, LANES)],
        [VMEM] * (mods + 4),
        work=0.4,
    )(*pieces[1:], pair, halo, coef, edge, data_total)
    totals = [
        lax.ppermute(total, "tm", [(i, (i + k) % steps) for i in range(steps)]) for k in range(1, steps)
    ]

    size, pairs = plan.half + SUB, mods // 2
    *sent, near, prior = call(
        functools.partial(backward_kernel, plan),
        "backward",
        [f32(size, LANES)] * pairs
        + [f32(pairs * size + frames // 2 * shard, LANES), f32(frames // 2, 2 * shard, LANES)],
        [VMEM] * 11,
        scratch_shapes=[
            scratch(s)
            for s in (f32(cells, LANES),) + (bf16(2 * cells, 2 * wide),) * 2 + (f32(2, cells, 2 * wide),)
        ],
        work=0.8,
    )(cosine, sine, image, weights, even_back, odd_back, halo, flow, rim, coef, edge)

    def swap(array, k):
        return lax.ppermute(array, "mod", [(i, i ^ k) for i in range(mods)])

    near = swap(near, 1)
    total = call(sum_kernel, "sum", [f32(SUB, LANES)], [VMEM] * steps, work=3.0)(*totals, total)[0]
    joined = call(
        functools.partial(seal_kernel, plan),
        "seal",
        [f32(2 * size, LANES)] * (pairs - 1),
        [VMEM] * (pairs + 1),
    )(total, *sent[1:], near)
    far = [swap(array, 2 * k + 2) for k, array in enumerate(joined)]
    sums = [total] + [swap(total, k) for k in range(mods - 1, 0, -2)]

    hess_vec, curvature = call(
        functools.partial(final_kernel, plan, float(total_frames * plan.pupil * rows)),
        "join",
        [f32(*phase.shape), f32(1)],
        [VMEM] * (2 * pairs + 5),
        out_specs=[VMEM, SMEM],
        work=0.8,
    )(sent[0], near, *far, *sums, prior, coef, edge)
    return hess_vec, curvature


def solution(mesh):
    return jax.shard_map(
        per_device,
        mesh=mesh,
        in_specs=(
            P(("grp", "tm"), "mod", None),
            P(("grp", "tm"), "mod", None),
            P(),
            P("mod"),
            P("grp", None),
            P(("grp", "tm"), None, None),
        ),
        out_specs=(P(("grp", "tm"), "mod", None), P("grp")),
        check_vma=False,
    )
```

```python
import functools

import jax
import jax.numpy as jnp
import ml_dtypes
import numpy as np
from jax import lax
from jax.experimental import pallas as pl
from jax.experimental.pallas import tpu as pltpu
from jax.sharding import PartitionSpec as P

LANES = 128
SUB = 8
CHUNK = 32
VMEM = pl.BlockSpec(memory_space=pltpu.VMEM)
SMEM = pl.BlockSpec(memory_space=pltpu.SMEM)
HBM = pl.BlockSpec(memory_space=pltpu.HBM)


def params():
    return pltpu.CompilerParams(vmem_limit_bytes=48 * 1024 * 1024)


class Plan:
    def __init__(self, frames, shard, rows, points, mods):
        self.frames, self.shard, self.rows, self.mods = frames, shard, rows, mods
        self.points = points
        self.pupil = shard * mods
        self.length = 2 * self.pupil
        assert rows == LANES and mods % frames == 0 and frames % 2 == 0 and mods % 2 == 0
        self.groups = mods // frames
        self.width = rows // self.groups
        assert 2 * self.width <= LANES
        self.copies = LANES // self.width
        self.total_points = points * mods
        assert self.total_points % self.copies == 0
        self.tiles = self.total_points // self.copies
        self.half = shard // 2
        self.cells = self.pupil // 2
        self.extra = -(-(points + 2 * frames) // SUB) * SUB


def roof_tables(plan):
    cells, length = plan.cells, plan.length
    index = np.arange(cells)
    turned = (index + cells // 2) % cells

    def kernel(gap):
        return 2.0 / length / np.cos(2.0 * np.pi * gap / length)

    even = kernel(2 * turned[:, None] - (2 * index[None, :] + 1))
    odd = kernel(2 * turned[:, None] + 1 - 2 * index[None, :])

    def split(table):
        high = table.astype(ml_dtypes.bfloat16)
        low = (table - high.astype(np.float64)).astype(ml_dtypes.bfloat16)
        return np.concatenate([high, low], axis=0)

    return split(even), split(odd), split(even.T), split(odd.T)


def spread(cells, plan, first):
    lane = lax.broadcasted_iota(jnp.int32, cells.shape, 1)
    width = plan.width
    if 2 * width == LANES:
        other = pltpu.roll(cells, width, 1)
        keep = (lane < width) if first == 0 else (lane >= width)
        return jnp.where(keep, cells, other)
    if first:
        cells = pltpu.roll(cells, LANES - first, 1)
    cells = jnp.where(lane < width, cells, 0.0)
    step = width
    while step < LANES:
        cells = cells + pltpu.roll(cells, step, 1)
        step *= 2
    return cells


def lane_sum(cells, plan):
    step = plan.width
    while step < LANES:
        cells = cells + pltpu.roll(cells, step, 1)
        step *= 2
    return cells


def place_on(axis):
    return lax.axis_index(axis)


def place_on(axis):
    return lax.axis_index(axis)


def tilt_kernel(tilt_ref, out_ref):
    out_ref[...] = tilt_ref[...]


def pack_kernel(plan, tilt_ref, phase_ref, direction_ref, *refs):
    outs, near_ref = refs[: plan.mods], refs[plan.mods]
    me = place_on("mod")
    width, half, shard, frames = plan.width, plan.half, plan.shard, plan.frames
    lane = lax.broadcasted_iota(jnp.int32, (half, LANES), 1)
    for k, out in enumerate(outs):
        dest = me ^ k
        frame, group = dest // plan.groups, dest % plan.groups
        back = (LANES - group * width) % LANES
        ahead = (LANES + width - group * width) % LANES
        for parity in range(2):
            own = pl.ds(parity, half, stride=2)
            one = pltpu.roll(phase_ref[frame, own, :], back, 1)
            two = pltpu.roll(direction_ref[frame, own, :], ahead, 1)
            out[parity * half : (parity + 1) * half, :] = jnp.where(lane < width, one, two)
        rows = []
        for f in range(frames):
            rows += [direction_ref[f, 0:1, :], direction_ref[f, shard - 1 : shard, :]]
        rows += [tilt_ref[p : p + 1, :] for p in range(plan.points)]
        rows += [jnp.zeros((1, LANES), jnp.float32)] * (plan.extra - len(rows))
        out[shard : shard + plan.extra, :] = jnp.concatenate(rows, axis=0)
    for f in range(frames):
        start = shard + plan.extra + f * shard
        outs[1][start : start + shard, :] = direction_ref[f]
        near_ref[f] = direction_ref[f]


def relay_kernel(plan, own_ref, piece_ref, after_ref, pair_ref, send_ref):
    shard, frames = plan.shard, plan.frames
    side = place_on("mod") % 2
    for f in range(frames):
        start = shard + plan.extra + f * shard
        pair_ref[f, pl.ds(pl.multiple_of(side * shard, SUB), shard), :] = own_ref[f]
        pair_ref[f, pl.ds(pl.multiple_of((1 - side) * shard, SUB), shard), :] = piece_ref[start : start + shard, :]
    send_ref[...] = pair_ref[side * (frames - 1)]


def prep_kernel(plan, seed_ref, mask_hbm, noise_hbm, codes_hbm, *refs):
    tables_hbm, refs = refs[:4], refs[4:]
    mask_out, noise_out, coef_out, edge_out, *tables, mask_ref, noise_ref, codes_ref, sems = refs
    me = place_on("mod")
    shard, cells, quarter_line = plan.shard, plan.cells, plan.pupil // 2
    frame, group = me // plan.groups, me % plan.groups
    group_back = (LANES - group * plan.width) % LANES
    reach = 2 * shard
    begin = pl.multiple_of((me // 2) * reach, SUB)
    before = pl.multiple_of(jnp.maximum(begin - SUB, 0), SUB)
    pairs = [
        (mask_hbm, mask_ref),
        (noise_hbm.at[frame], noise_ref),
        (codes_hbm.at[pl.ds(before, SUB)], codes_ref.at[0:SUB]),
        (codes_hbm.at[pl.ds(begin, reach)], codes_ref.at[SUB : SUB + reach]),
        *zip(tables_hbm, tables),
    ]
    loads = [pltpu.make_async_copy(source, target, sems.at[i]) for i, (source, target) in enumerate(pairs)]
    for load in loads:
        load.start()

    lane_group = lax.broadcasted_iota(jnp.int32, (CHUNK, LANES), 1) // plan.width

    def own_rows(cells_in):
        if plan.copies == 2:
            return jnp.where(lane_group == group, cells_in, pltpu.roll(cells_in, plan.width, 1))
        return spread(pltpu.roll(cells_in, group_back, 1), plan, 0)

    loads[0].wait()
    for parity in range(2):
        for row in range(0, cells, CHUNK):
            picked = mask_ref[pl.ds(2 * row + parity, CHUNK, stride=2), :].astype(jnp.float32)
            mask_out[parity, row : row + CHUNK, :] = own_rows(picked)
    loads[1].wait()
    for parity in range(2):
        for row in range(0, cells, CHUNK):
            low_half = row < cells // 2
            inner = 2 * (row % (cells // 2)) + parity
            for side, block in enumerate((2, 0) if low_half else (1, 3)):
                picked = noise_ref[pl.ds(block * quarter_line + inner, CHUNK, stride=2), :]
                noise_out[side, parity, row : row + CHUNK, :] = own_rows(picked)
    loads[2].wait()
    loads[3].wait()
    for i, share in enumerate(shares(codes_ref[SUB : SUB + reach, :])):
        coef_out[i] = share
    for i, share in enumerate(shares(codes_ref[0:SUB, :])):
        edge_out[i] = jnp.where(me > 1, share, 0.0)
    for load in loads[4:]:
        load.wait()


def wave(turns):
    quarters = jnp.round(turns * 4.0)
    angle = (turns - quarters * 0.25) * (2.0 * np.pi)
    square = angle * angle
    sin_part = ((-1.9515295891e-4 * square + 8.3321608736e-3) * square - 1.6666654611e-1) * square * angle + angle
    cos_part = (
        (2.443315711809948e-5 * square - 1.388731625493765e-3) * square + 4.166664568298827e-2
    ) * (square * square) + (1.0 - 0.5 * square)
    count = quarters.astype(jnp.int32)
    odd = (count & 1) != 0
    cosine = jnp.where(odd, sin_part, cos_part)
    sine = jnp.where(odd, cos_part, sin_part)
    cosine = jnp.where(((count + 1) & 2) != 0, -cosine, cosine)
    sine = jnp.where((count & 2) != 0, -sine, sine)
    return cosine, sine


def product(table_ref, ref):
    cells = ref.shape[0] // 2
    first = jnp.dot(table_ref[...], ref[:cells], preferred_element_type=jnp.float32)
    second = jnp.dot(table_ref[:cells], ref[cells:], preferred_element_type=jnp.float32)
    return first[:cells] + first[cells:] + second


def put_split(ref, row, rows, cells, column, value):
    high = value.astype(jnp.bfloat16)
    low = (value - high.astype(jnp.float32)).astype(jnp.bfloat16)
    where = slice(column, column + LANES)
    ref[row : row + rows, where] = high
    ref[cells + row : cells + row + rows, where] = low


def forward_kernel(plan, *refs):
    mods, half, cells = plan.mods, plan.half, plan.cells
    tiles, wide = plan.tiles, plan.tiles * LANES
    pieces = refs[:mods]
    mask_ref, noise_ref, even_ref, odd_ref = refs[mods : mods + 4]
    cos_ref, sin_ref, image_ref, weight_ref, total_ref = refs[mods + 4 : mods + 9]
    turn_ref, dir_ref, even_in_ref, odd_in_ref = refs[mods + 9 :]
    me = place_on("mod")
    lane_row = lax.broadcasted_iota(jnp.int32, (1, LANES), 1)

    for k, piece in enumerate(pieces):
        place = pl.ds(pl.multiple_of((me ^ k) * half, SUB), half)
        for parity in range(2):
            cells_in = piece[parity * half : (parity + 1) * half, :]
            turn_ref[parity, place, :] = spread(cells_in, plan, 0) * (0.5 / np.pi)
            dir_ref[parity, place, :] = spread(cells_in, plan, plan.width)

    tilt_rows = [jnp.zeros((1, LANES), jnp.float32)] * tiles
    for k, piece in enumerate(pieces):
        for p in range(plan.points):
            tile, slot = divmod(k * plan.points + p, plan.copies)
            at = plan.shard + 2 * plan.frames + p
            row = piece[at : at + 1, :]
            tilt_rows[tile] = jnp.where(lane_row // plan.width == slot, row, tilt_rows[tile])

    def tilted(tile, spots):
        tilt = spots.astype(jnp.float32) / plan.length * tilt_rows[tile]
        return wave(tilt - jnp.round(tilt))

    steps = [tilted(tile, jnp.full((1, LANES), 2 * CHUNK, jnp.int32)) for tile in range(tiles)]
    spots = lax.broadcasted_iota(jnp.int32, (CHUNK, LANES), 0) * 2 + plan.pupil // 2

    def fields(parity, ref):
        tilts = [tilted(tile, spots + parity) for tile in range(tiles)]
        for row in range(0, cells, CHUNK):
            here = slice(row, row + CHUNK)
            mask = mask_ref[parity, here, :]
            push = dir_ref[parity, here, :]
            turns = turn_ref[parity, here, :]
            flat_cos, flat_sin = wave(turns)
            flat_cos, flat_sin = flat_cos * mask, flat_sin * mask
            for tile in range(tiles):
                tilt_cos, tilt_sin = tilts[tile]
                cosine = flat_cos * tilt_cos - flat_sin * tilt_sin
                sine = flat_sin * tilt_cos + flat_cos * tilt_sin
                step_cos, step_sin = steps[tile]
                tilts[tile] = (
                    tilt_cos * step_cos - tilt_sin * step_sin,
                    tilt_sin * step_cos + tilt_cos * step_sin,
                )
                at = tile * LANES
                cos_ref[parity, here, at : at + LANES] = cosine
                sin_ref[parity, here, at : at + LANES] = sine
                put_split(ref, row, CHUNK, cells, at, cosine)
                put_split(ref, row, CHUNK, cells, wide + at, sine)
                put_split(ref, row, CHUNK, cells, 2 * wide + at, -sine * push)
                put_split(ref, row, CHUNK, cells, 3 * wide + at, cosine * push)

    def signals(parity, total):
        for row in range(0, cells, CHUNK):
            here = slice(row, row + CHUNK)
            push = dir_ref[parity, here, :]
            even_sum = odd_sum = shift = 0.0
            for tile in range(tiles):
                at = tile * LANES
                cosine = cos_ref[parity, here, at : at + LANES]
                sine = sin_ref[parity, here, at : at + LANES]
                image_cos, image_sin, push_real, push_imag = [
                    image_ref[parity, here, q * wide + at : q * wide + at + LANES] for q in range(4)
                ]
                even_sum += image_sin * push_imag + image_cos * push_real
                odd_sum += cosine * (push_imag - push * image_cos) - sine * (push_real + push * image_sin)
                shift += cosine * image_cos + sine * image_sin
            even_sum = lane_sum(even_sum, plan) * 2.0
            odd_sum = lane_sum(odd_sum, plan)
            signal_after, signal_before = even_sum + odd_sum, even_sum - odd_sum
            weighted_after = noise_ref[0, parity, here, :] * signal_after
            weighted_before = noise_ref[1, parity, here, :] * signal_before
            squares = weighted_after * signal_after + weighted_before * signal_before
            for r in range(0, CHUNK, SUB):
                total += squares[r : r + SUB]
            gap = (weighted_after - weighted_before) * 0.5
            weight_ref[0, parity, here, :] = weighted_after + weighted_before
            weight_ref[1, parity, here, :] = gap
            weight_ref[2, parity, here, :] = -gap * shift
        return total

    def image(parity, table, ref):
        image_ref[parity] = product(table, ref)

    fields(0, even_in_ref)
    fields(1, odd_in_ref)
    image(1, odd_ref, even_in_ref)
    image(0, even_ref, odd_in_ref)
    total = signals(1, jnp.zeros((SUB, LANES), jnp.float32))
    total = signals(0, total)
    total_ref[...] = total / plan.copies


def backward_kernel(plan, *refs):
    cos_ref, sin_ref, image_ref, weight_ref, even_ref, odd_ref, halo_ref, flow_ref, rim_ref, coef_ref, edge_ref = refs[:11]
    outs, prior_ref, (grad_ref, even_in_ref, odd_in_ref, back_ref) = refs[11:-5], refs[-5], refs[-4:]
    half, cells, shard, tiles, wide = plan.half, plan.cells, plan.shard, plan.tiles, plan.tiles * LANES
    me = place_on("mod")

    def fold(parity, ref):
        for row in range(0, cells, CHUNK):
            here = slice(row, row + CHUNK)
            both, gap = weight_ref[0, parity, here, :], weight_ref[1, parity, here, :]
            for tile in range(tiles):
                at = tile * LANES
                cosine = cos_ref[parity, here, at : at + LANES]
                sine = sin_ref[parity, here, at : at + LANES]
                image_cos = image_ref[parity, here, at : at + LANES]
                image_sin = image_ref[parity, here, wide + at : wide + at + LANES]
                put_split(ref, row, CHUNK, cells, at, gap * cosine + both * image_sin)
                put_split(ref, row, CHUNK, cells, wide + at, gap * sine - both * image_cos)

    def back(parity, table, ref):
        back_ref[parity] = product(table, ref)

    fold(0, even_in_ref)
    fold(1, odd_in_ref)
    back(1, even_ref, even_in_ref)
    back(0, odd_ref, odd_in_ref)
    lane = lax.broadcasted_iota(jnp.int32, (CHUNK, LANES), 1)
    for row in range(0, cells, CHUNK):
        here = slice(row, row + CHUNK)
        grads = []
        for parity in range(2):
            grad = weight_ref[2, parity, here, :]
            for tile in range(tiles):
                at = tile * LANES
                grad += cos_ref[parity, here, at : at + LANES] * back_ref[parity, here, at : at + LANES]
                grad += sin_ref[parity, here, at : at + LANES] * back_ref[parity, here, wide + at : wide + at + LANES]
            grads.append(lane_sum(grad, plan) * 2.0)
        grad_ref[here, :] = jnp.where(lane < plan.width, grads[0], grads[1])
    step, side = place_on("tm"), me % 2
    alone = jnp.where(side == 0, step == 0, step == lax.axis_size("tm") - 1)
    rows = [jnp.where(alone, 0.0, r) for r in (halo_ref[0:1, :], halo_ref[2 * shard - 1 : 2 * shard, :])]
    rows += [jnp.zeros((1, LANES), jnp.float32)] * (SUB - len(rows))
    tail = jnp.concatenate(rows, axis=0)
    def put(out, at, k):
        place = pl.ds(pl.multiple_of((me ^ k) * half, SUB), half)
        out[at : at + half, :] = grad_ref[place, :]
        out[at + half : at + half + SUB, :] = tail

    *even_outs, near_out = outs
    for k in range(0, plan.mods, 2):
        put(even_outs[k // 2], 0, k)
    for k in range(1, plan.mods, 2):
        put(near_out, (k // 2) * (half + SUB), k)
    prior_terms(plan, flow_ref, rim_ref, coef_ref, edge_ref, prior_ref)
    theirs = pl.ds(pl.multiple_of((1 - me % 2) * shard, SUB), shard)
    for f in range(plan.frames // 2):
        start = plan.mods // 2 * (half + SUB) + f * shard
        near_out[start : start + shard, :] = prior_ref[f, theirs, :]


def prior_terms(plan, flow_ref, rim_ref, coef_ref, edge_ref, prior_ref):
    reach = 2 * plan.shard
    row_id = lax.broadcasted_iota(jnp.int32, (reach, LANES), 0)

    def from_last(body, first):
        return jnp.where(row_id == 0, first, pltpu.roll(body, 1, 0))

    for t in range(plan.frames // 2):
        own, rim = flow_ref[t + 1], rim_ref[t : t + 1, :]
        ahead, both = [
            from_last(coef_ref[i] * own, edge_ref[i, SUB - 1 : SUB, :] * rim) for i in (1, 3)
        ]
        prior_ref[t] = flow_ref[t] - (coef_ref[0] * own + ahead + row_behind(coef_ref[2] * own + both))


def sum_kernel(*refs):
    total = refs[0][...]
    for ref in refs[1:-1]:
        total += ref[...]
    refs[-1][...] = jnp.broadcast_to(jnp.sum(total, axis=0, keepdims=True), total.shape)


def seal_kernel(plan, total_ref, *refs):
    size, count = plan.half + SUB, plan.mods // 2 - 1
    own, near_ref, outs = refs[:count], refs[count], refs[count + 1 :]
    for i, out in enumerate(outs):
        out[0:size, :] = own[i][...]
        out[plan.half + 2 : plan.half + 3, :] = total_ref[0:1, :]
        out[size : 2 * size, :] = near_ref[(i + 1) * size : (i + 2) * size, :]


def row_ahead(cells):
    lane = lax.broadcasted_iota(jnp.int32, cells.shape, 1)
    return jnp.where(lane == LANES - 1, 0.0, pltpu.roll(cells, LANES - 1, 1))


def row_behind(cells):
    lane = lax.broadcasted_iota(jnp.int32, cells.shape, 1)
    return jnp.where(lane == 0, 0.0, pltpu.roll(cells, 1, 1))


def shares(codes):
    ahead_x = ((codes & 3).astype(jnp.float32) + 0.5) / 4.0
    ahead_r = ((codes >> 2).astype(jnp.float32) + 0.5) / 4.0
    return (1.0 - ahead_x) * (1.0 - ahead_r), ahead_x * (1.0 - ahead_r), (1.0 - ahead_x) * ahead_r, ahead_x * ahead_r


def prior_kernel(plan, steps, *refs):
    mods, shard, frames = plan.mods, plan.shard, plan.frames
    pieces, refs = refs[: mods - 1], refs[mods - 1 :]
    pair_ref, halo_ref, coef_ref, edge_ref, data_ref, flow_ref, rim_ref, total_ref = refs
    me, step = place_on("mod"), place_on("tm")
    side, base, reach, held = me % 2, me - me % 2, 2 * shard, frames // 2
    first_frame, total_frames = step * frames + side * held, steps * frames
    zero_row = jnp.zeros((1, LANES), jnp.float32)

    alone = jnp.where(side == 0, step == 0, step == steps - 1)
    halo = jnp.where(alone, 0.0, halo_ref[...])
    cells, below, above = [], [], []
    for t in range(held + 2):
        frame = side * held + t - 1
        inside = (frame >= 0) & (frame < frames)
        cells.append(jnp.where(inside, pair_ref[jnp.clip(frame, 0, frames - 1)], halo))
        low, high = zero_row, zero_row
        for k in range(2, mods):
            source = me ^ k
            for f in range(frames):
                at = shard + 2 * f
                here = frame == f
                high = jnp.where((source == base + 2) & here, pieces[k - 1][at : at + 1, :], high)
                low = jnp.where((source == base - 1) & here, pieces[k - 1][at + 1 : at + 2, :], low)
        below.append(low)
        above.append(high)

    row_id = lax.broadcasted_iota(jnp.int32, (reach, LANES), 0)

    def from_next(body, last):
        return jnp.where(row_id == reach - 1, last, pltpu.roll(body, reach - 1, 0))

    coef = [coef_ref[i] for i in range(4)]
    edge = [edge_ref[i, SUB - 1 : SUB, :] for i in range(4)]

    def moved(share, base, ahead):
        return share[0] * base + share[1] * ahead + share[2] * row_ahead(base) + share[3] * row_ahead(ahead)

    flow, flow_edge = [], []
    for t in range(held + 1):
        frame = first_frame + t - 1
        valid = (frame >= 0) & (frame <= total_frames - 2)
        ahead = from_next(cells[t], above[t])
        flow.append(jnp.where(valid, cells[t + 1] - moved(coef, cells[t], ahead), 0.0))
        if t > 0:
            value = below[t + 1] - moved(edge, below[t], cells[t][0:1])
            flow_edge.append(jnp.where(valid & (me > 1), value, 0.0))
    total = data_ref[...]
    for t in range(held):
        square = flow[t + 1] * flow[t + 1]
        for r in range(0, reach, SUB):
            total += square[r : r + SUB]
    for t in range(held + 1):
        flow_ref[t] = flow[t]
    rim_ref[...] = jnp.concatenate(flow_edge + [zero_row] * (SUB - held), axis=0)
    total_ref[...] = total


def add_pieces(plan, me, pieces, hess_ref):
    half, width = plan.half, plan.width
    lane_group = lax.broadcasted_iota(jnp.int32, (half, LANES), 1) // width
    for k, piece, at in pieces:
        source = me ^ k
        frame, group = source // plan.groups, source % plan.groups
        for parity in range(2):
            own = pl.ds(parity, half, stride=2)
            cells = piece[at : at + half, :]
            if plan.copies == 2:
                moved = jnp.where(group == parity, cells, pltpu.roll(cells, width, 1))
            else:
                moved = pltpu.roll(cells, (group * width - parity * width + LANES) % LANES, 1)
            hess_ref[frame, own, :] += jnp.where(lane_group == group, moved, 0.0)


def begin_kernel(plan, own_ref, near_ref, prior_ref, hess_ref):
    shard, start = plan.shard, plan.mods // 2 * (plan.half + SUB)
    me = place_on("mod")
    side, held = me % 2, plan.frames // 2
    mine = pl.ds(pl.multiple_of(side * shard, SUB), shard)
    for f in range(held):
        hess_ref[side * held + f] = prior_ref[f, mine, :]
        hess_ref[(1 - side) * held + f] = near_ref[start + f * shard : start + (f + 1) * shard, :]
    add_pieces(plan, me, [(0, own_ref, 0), (1, near_ref, 0)], hess_ref)


def final_kernel(plan, entries, *refs):
    half, shard = plan.half, plan.shard
    size, pairs = half + SUB, plan.mods // 2
    begun_ref, far, sums = refs[0], refs[1:pairs], refs[pairs : 2 * pairs + 1]
    coef_ref, edge_ref, hess_ref, curvature_ref = refs[2 * pairs + 1 :]
    me = place_on("mod")
    side = me % 2
    pieces = [(2 * i + 2 + p, ref, p * size) for i, ref in enumerate(far) for p in range(2)]
    hess_ref[...] = begun_ref[...]
    add_pieces(plan, me, pieces, hess_ref)
    zero_row = jnp.zeros((1, LANES), jnp.float32)
    total, above, below = zero_row, zero_row, zero_row
    for ref in sums:
        total += ref[0:1, :]
    for ref in far:
        total += ref[half + 2 : half + 3, :]
    for k, piece, at in pieces:
        source, at = me ^ k, at + half
        above = jnp.where((source == me + 1) & (side == 1), piece[at : at + 1, :], above)
        below = jnp.where((source == me - 1) & (side == 0), piece[at + 1 : at + 2, :], below)
    last, top, rim = slice(shard - 1, shard), slice(2 * shard - 1, 2 * shard), slice(SUB - 1, SUB)
    hess_ref[0, last, :] -= coef_ref[1, top, :] * above + coef_ref[3, top, :] * row_ahead(above)
    hess_ref[plan.frames - 1, 0:1, :] -= edge_ref[1, rim, :] * below + row_behind(edge_ref[3, rim, :] * below)
    curvature_ref[0] = jnp.sum(total) / entries


def exchange(arrays, axis):
    count = lax.axis_size(axis)
    return [arrays[0]] + [
        lax.ppermute(arrays[k], axis, [(i, i ^ k) for i in range(count)]) for k in range(1, count)
    ]


def per_device(phase, direction, pupil_mask, mod_tilts, wind_codes, noise_weight):
    frames, shard, rows = phase.shape
    mods, steps = lax.axis_size("mod"), lax.axis_size("tm")
    plan = Plan(frames, shard, rows, mod_tilts.shape[0], mods)
    total_frames = frames * steps
    cells, wide = plan.cells, plan.tiles * LANES
    tables = [jnp.asarray(t) for t in roof_tables(plan)]
    pupil_mask, wind_codes, noise_weight, *tables = [
        pltpu.with_memory_space_constraint(array, pltpu.HBM)
        for array in (pupil_mask, wind_codes, noise_weight, *tables)
    ]

    def f32(*shape):
        return jax.ShapeDtypeStruct(shape, jnp.float32)

    def bf16(*shape):
        return jax.ShapeDtypeStruct(shape, jnp.bfloat16)

    def scratch(shape):
        return pltpu.VMEM(shape.shape, shape.dtype)

    def call(kernel, name, outs, in_specs, out_specs=None, scratch_shapes=(), aliases=None, work=0.02):
        return pl.pallas_call(
            kernel,
            out_shape=outs,
            in_specs=in_specs,
            out_specs=out_specs or [VMEM] * len(outs),
            scratch_shapes=list(scratch_shapes),
            input_output_aliases=aliases or {},
            compiler_params=params(),
            cost_estimate=pl.CostEstimate(
                flops=int(work * 1.1e9), bytes_accessed=int(work * 3.6e6), transcendentals=0
            ),
            name=name,
        )

    rows_in = shard + plan.extra
    tilts = jnp.broadcast_to(mod_tilts.astype(jnp.float32)[:, None], (plan.points, LANES))
    tilts = call(tilt_kernel, "tilts", [f32(plan.points, LANES)], [VMEM], work=0.8)(tilts)[0]
    *packed, direction_near = call(
        functools.partial(pack_kernel, plan),
        "pack",
        [f32(rows_in + (frames * shard if k == 1 else 0), LANES) for k in range(mods)] + [f32(*phase.shape)],
        [VMEM] * 3,
        work=0.3,
    )(tilts, phase, direction)
    pieces = exchange(packed, "mod")

    table = bf16(*tables[0].shape)
    mask, noise, coef, edge, even, odd, even_back, odd_back = call(
        functools.partial(prep_kernel, plan),
        "prepare",
        [f32(2, cells, LANES), f32(2, 2, cells, LANES), f32(4, 2 * shard, LANES), f32(4, SUB, LANES)]
        + [table] * 4,
        [VMEM] + [HBM] * 7,
        scratch_shapes=[
            pltpu.VMEM(pupil_mask.shape, jnp.int32),
            pltpu.VMEM(noise_weight.shape[1:], jnp.float32),
            pltpu.VMEM((2 * shard + SUB, LANES), jnp.int32),
            pltpu.SemaphoreType.DMA((8,)),
        ],
        work=1.5,
    )(packed[0], pupil_mask, noise_weight, wind_codes, *tables)

    pair, edge_frame = call(
        functools.partial(relay_kernel, plan),
        "relay",
        [f32(frames, 2 * shard, LANES), f32(2 * shard, LANES)],
        [VMEM] * 3,
        work=0.05,
    )(direction_near, pieces[1], edge)
    ends = [(t * mods + m, (t + 1) * mods + m - 1) for t in range(steps - 1) for m in range(1, mods, 2)]
    lone = [m for m in range(0, mods, 2)] + [(steps - 1) * mods + m for m in range(1, mods, 2)]
    if mods % 4 == 0:
        ends += [(a, a ^ 2) for a in lone if a & 2]
    else:
        ends += list(zip(lone[: mods // 2], lone[mods // 2 :]))
    halo = lax.ppermute(edge_frame, ("tm", "mod"), ends + [(b, a) for a, b in ends])

    cosine, sine, image, weights, data_total = call(
        functools.partial(forward_kernel, plan),
        "forward",
        [f32(2, cells, wide), f32(2, cells, wide), f32(2, cells, 4 * wide), f32(3, 2, cells, LANES), f32(SUB, LANES)],
        [VMEM] * (mods + 4),
        scratch_shapes=[
            scratch(s)
            for s in (f32(2, cells, LANES),) * 2 + (bf16(2 * cells, 4 * wide),) * 2
        ],
        work=2.8,
    )(*pieces, mask, noise, even, odd)

    flow, rim, total = call(
        functools.partial(prior_kernel, plan, steps),
        "prior",
        [f32(frames // 2 + 1, 2 * shard, LANES), f32(SUB, LANES), f32(SUB, LANES)],
        [VMEM] * (mods + 4),
        work=0.4,
    )(*pieces[1:], pair, halo, coef, edge, data_total)
    totals = [
        lax.ppermute(total, "tm", [(i, (i + k) % steps) for i in range(steps)]) for k in range(1, steps)
    ]

    size, pairs = plan.half + SUB, mods // 2
    *sent, near, prior = call(
        functools.partial(backward_kernel, plan),
        "backward",
        [f32(size, LANES)] * pairs
        + [f32(pairs * size + frames // 2 * shard, LANES), f32(frames // 2, 2 * shard, LANES)],
        [VMEM] * 11,
        scratch_shapes=[
            scratch(s)
            for s in (f32(cells, LANES),) + (bf16(2 * cells, 2 * wide),) * 2 + (f32(2, cells, 2 * wide),)
        ],
        work=0.8,
    )(cosine, sine, image, weights, even_back, odd_back, halo, flow, rim, coef, edge)

    def swap(array, k):
        return lax.ppermute(array, "mod", [(i, i ^ k) for i in range(mods)])

    near = swap(near, 1)
    total = call(sum_kernel, "sum", [f32(SUB, LANES)], [VMEM] * steps, work=3.0)(*totals, total)[0]
    joined = call(
        functools.partial(seal_kernel, plan),
        "seal",
        [f32(2 * size, LANES)] * (pairs - 1),
        [VMEM] * (pairs + 1),
    )(total, *sent[1:], near)
    far = [swap(array, 2 * k + 2) for k, array in enumerate(joined)]
    sums = [total] + [swap(total, k) for k in range(1, mods, 2)]

    begun = call(functools.partial(begin_kernel, plan), "begin", [f32(*phase.shape)], [VMEM] * 3, work=0.2)(
        sent[0], near, prior
    )[0]
    hess_vec, curvature = call(
        functools.partial(final_kernel, plan, float(total_frames * plan.pupil * rows)),
        "join",
        [f32(*phase.shape), f32(1)],
        [VMEM] * (2 * pairs + 3),
        out_specs=[VMEM, SMEM],
        work=0.8,
    )(begun, *far, *sums, coef, edge)
    return hess_vec, curvature


def solution(mesh):
    return jax.shard_map(
        per_device,
        mesh=mesh,
        in_specs=(
            P(("grp", "tm"), "mod", None),
            P(("grp", "tm"), "mod", None),
            P(),
            P("mod"),
            P("grp", None),
            P(("grp", "tm"), None, None),
        ),
        out_specs=(P(("grp", "tm"), "mod", None), P("grp")),
        check_vma=False,
    )
```

```python
import functools

import jax
import jax.numpy as jnp
import ml_dtypes
import numpy as np
from jax import lax
from jax.experimental import pallas as pl
from jax.experimental.pallas import tpu as pltpu
from jax.sharding import PartitionSpec as P

LANES = 128
SUB = 8
CHUNK = 32
VMEM = pl.BlockSpec(memory_space=pltpu.VMEM)
SMEM = pl.BlockSpec(memory_space=pltpu.SMEM)
HBM = pl.BlockSpec(memory_space=pltpu.HBM)


def params():
    return pltpu.CompilerParams(vmem_limit_bytes=48 * 1024 * 1024)


class Plan:
    def __init__(self, frames, shard, rows, points, mods):
        self.frames, self.shard, self.rows, self.mods = frames, shard, rows, mods
        self.points = points
        self.pupil = shard * mods
        self.length = 2 * self.pupil
        assert rows == LANES and mods % frames == 0 and frames % 2 == 0 and mods % 2 == 0
        self.groups = mods // frames
        self.width = rows // self.groups
        assert 2 * self.width <= LANES
        self.copies = LANES // self.width
        self.total_points = points * mods
        assert self.total_points % self.copies == 0
        self.tiles = self.total_points // self.copies
        self.half = shard // 2
        self.cells = self.pupil // 2
        self.extra = -(-(points + 2 * frames) // SUB) * SUB


def roof_tables(plan):
    cells, length = plan.cells, plan.length
    index = np.arange(cells)
    turned = (index + cells // 2) % cells

    def kernel(gap):
        return 2.0 / length / np.cos(2.0 * np.pi * gap / length)

    even = kernel(2 * turned[:, None] - (2 * index[None, :] + 1))
    odd = kernel(2 * turned[:, None] + 1 - 2 * index[None, :])

    def split(table):
        high = table.astype(ml_dtypes.bfloat16)
        low = (table - high.astype(np.float64)).astype(ml_dtypes.bfloat16)
        return np.concatenate([high, low], axis=0)

    return split(even), split(odd), split(even.T), split(odd.T)


def spread(cells, plan, first):
    lane = lax.broadcasted_iota(jnp.int32, cells.shape, 1)
    width = plan.width
    if 2 * width == LANES:
        other = pltpu.roll(cells, width, 1)
        keep = (lane < width) if first == 0 else (lane >= width)
        return jnp.where(keep, cells, other)
    if first:
        cells = pltpu.roll(cells, LANES - first, 1)
    cells = jnp.where(lane < width, cells, 0.0)
    step = width
    while step < LANES:
        cells = cells + pltpu.roll(cells, step, 1)
        step *= 2
    return cells


def lane_sum(cells, plan):
    step = plan.width
    while step < LANES:
        cells = cells + pltpu.roll(cells, step, 1)
        step *= 2
    return cells


def place_on(axis):
    return lax.axis_index(axis)


def place_on(axis):
    return lax.axis_index(axis)


def tilt_kernel(tilt_ref, out_ref):
    out_ref[...] = tilt_ref[...]


def pack_kernel(plan, tilt_ref, phase_ref, direction_ref, *refs):
    outs, near_ref = refs[: plan.mods], refs[plan.mods]
    me = place_on("mod")
    width, half, shard, frames = plan.width, plan.half, plan.shard, plan.frames
    lane = lax.broadcasted_iota(jnp.int32, (half, LANES), 1)
    for k, out in enumerate(outs):
        dest = me ^ k
        frame, group = dest // plan.groups, dest % plan.groups
        back = (LANES - group * width) % LANES
        ahead = (LANES + width - group * width) % LANES
        for parity in range(2):
            own = pl.ds(parity, half, stride=2)
            one, two = phase_ref[frame, own, :], direction_ref[frame, own, :]
            if plan.copies == 2:
                kept = jnp.where(group == 0, one, two)
                moved = pltpu.roll(jnp.where(group == 0, two, one), width, 1)
                low = (lane < width) == (group == 0)
                mixed = jnp.where(low, kept, moved)
            else:
                mixed = jnp.where(lane < width, pltpu.roll(one, back, 1), pltpu.roll(two, ahead, 1))
            out[parity * half : (parity + 1) * half, :] = mixed
        rows = []
        for f in range(frames):
            rows += [direction_ref[f, 0:1, :], direction_ref[f, shard - 1 : shard, :]]
        rows += [tilt_ref[p : p + 1, :] for p in range(plan.points)]
        rows += [jnp.zeros((1, LANES), jnp.float32)] * (plan.extra - len(rows))
        out[shard : shard + plan.extra, :] = jnp.concatenate(rows, axis=0)
    for f in range(frames):
        start = shard + plan.extra + f * shard
        outs[1][start : start + shard, :] = direction_ref[f]
        near_ref[f] = direction_ref[f]


def relay_kernel(plan, own_ref, piece_ref, after_ref, pair_ref, send_ref):
    shard, frames = plan.shard, plan.frames
    side = place_on("mod") % 2
    for f in range(frames):
        start = shard + plan.extra + f * shard
        pair_ref[f, pl.ds(pl.multiple_of(side * shard, SUB), shard), :] = own_ref[f]
        pair_ref[f, pl.ds(pl.multiple_of((1 - side) * shard, SUB), shard), :] = piece_ref[start : start + shard, :]
    send_ref[...] = pair_ref[side * (frames - 1)]


def prep_kernel(plan, seed_ref, mask_hbm, noise_hbm, codes_hbm, *refs):
    tables_hbm, refs = refs[:4], refs[4:]
    mask_out, noise_out, coef_out, edge_out, *tables, mask_ref, noise_ref, codes_ref, sems = refs
    me = place_on("mod")
    shard, cells, quarter_line = plan.shard, plan.cells, plan.pupil // 2
    frame, group = me // plan.groups, me % plan.groups
    group_back = (LANES - group * plan.width) % LANES
    reach = 2 * shard
    begin = pl.multiple_of((me // 2) * reach, SUB)
    before = pl.multiple_of(jnp.maximum(begin - SUB, 0), SUB)
    pairs = [
        (mask_hbm, mask_ref),
        (noise_hbm.at[frame], noise_ref),
        (codes_hbm.at[pl.ds(before, SUB)], codes_ref.at[0:SUB]),
        (codes_hbm.at[pl.ds(begin, reach)], codes_ref.at[SUB : SUB + reach]),
        *zip(tables_hbm, tables),
    ]
    loads = [pltpu.make_async_copy(source, target, sems.at[i]) for i, (source, target) in enumerate(pairs)]
    for load in loads:
        load.start()

    lane_group = lax.broadcasted_iota(jnp.int32, (CHUNK, LANES), 1) // plan.width

    def own_rows(cells_in):
        if plan.copies == 2:
            return jnp.where(lane_group == group, cells_in, pltpu.roll(cells_in, plan.width, 1))
        return spread(pltpu.roll(cells_in, group_back, 1), plan, 0)

    loads[0].wait()
    for parity in range(2):
        for row in range(0, cells, CHUNK):
            picked = mask_ref[pl.ds(2 * row + parity, CHUNK, stride=2), :].astype(jnp.float32)
            mask_out[parity, row : row + CHUNK, :] = own_rows(picked)
    loads[1].wait()
    for parity in range(2):
        for row in range(0, cells, CHUNK):
            low_half = row < cells // 2
            inner = 2 * (row % (cells // 2)) + parity
            for side, block in enumerate((2, 0) if low_half else (1, 3)):
                picked = noise_ref[pl.ds(block * quarter_line + inner, CHUNK, stride=2), :]
                noise_out[side, parity, row : row + CHUNK, :] = own_rows(picked)
    loads[2].wait()
    loads[3].wait()
    for i, share in enumerate(shares(codes_ref[SUB : SUB + reach, :])):
        coef_out[i] = share
    for i, share in enumerate(shares(codes_ref[0:SUB, :])):
        edge_out[i] = jnp.where(me > 1, share, 0.0)
    for load in loads[4:]:
        load.wait()


def wave(turns):
    quarters = jnp.round(turns * 4.0)
    angle = (turns - quarters * 0.25) * (2.0 * np.pi)
    square = angle * angle
    sin_part = ((-1.9515295891e-4 * square + 8.3321608736e-3) * square - 1.6666654611e-1) * square * angle + angle
    cos_part = (
        (2.443315711809948e-5 * square - 1.388731625493765e-3) * square + 4.166664568298827e-2
    ) * (square * square) + (1.0 - 0.5 * square)
    count = quarters.astype(jnp.int32)
    odd = (count & 1) != 0
    cosine = jnp.where(odd, sin_part, cos_part)
    sine = jnp.where(odd, cos_part, sin_part)
    cosine = jnp.where(((count + 1) & 2) != 0, -cosine, cosine)
    sine = jnp.where((count & 2) != 0, -sine, sine)
    return cosine, sine


def product(table_ref, ref):
    cells = ref.shape[0] // 2
    first = jnp.dot(table_ref[...], ref[:cells], preferred_element_type=jnp.float32)
    second = jnp.dot(table_ref[:cells], ref[cells:], preferred_element_type=jnp.float32)
    return first[:cells] + first[cells:] + second


def put_split(ref, row, rows, cells, column, value):
    high = value.astype(jnp.bfloat16)
    low = (value - high.astype(jnp.float32)).astype(jnp.bfloat16)
    where = slice(column, column + LANES)
    ref[row : row + rows, where] = high
    ref[cells + row : cells + row + rows, where] = low


def forward_kernel(plan, *refs):
    mods, half, cells = plan.mods, plan.half, plan.cells
    tiles, wide = plan.tiles, plan.tiles * LANES
    pieces = refs[:mods]
    mask_ref, noise_ref, even_ref, odd_ref = refs[mods : mods + 4]
    cos_ref, sin_ref, image_ref, weight_ref, total_ref = refs[mods + 4 : mods + 9]
    turn_ref, dir_ref, even_in_ref, odd_in_ref = refs[mods + 9 :]
    me = place_on("mod")
    lane_row = lax.broadcasted_iota(jnp.int32, (1, LANES), 1)

    for k, piece in enumerate(pieces):
        place = pl.ds(pl.multiple_of((me ^ k) * half, SUB), half)
        for parity in range(2):
            cells_in = piece[parity * half : (parity + 1) * half, :]
            turn_ref[parity, place, :] = spread(cells_in, plan, 0) * (0.5 / np.pi)
            dir_ref[parity, place, :] = spread(cells_in, plan, plan.width)

    tilt_rows = [jnp.zeros((1, LANES), jnp.float32)] * tiles
    for k, piece in enumerate(pieces):
        for p in range(plan.points):
            tile, slot = divmod(k * plan.points + p, plan.copies)
            at = plan.shard + 2 * plan.frames + p
            row = piece[at : at + 1, :]
            tilt_rows[tile] = jnp.where(lane_row // plan.width == slot, row, tilt_rows[tile])

    def tilted(tile, spots):
        tilt = spots.astype(jnp.float32) / plan.length * tilt_rows[tile]
        return wave(tilt - jnp.round(tilt))

    steps = [tilted(tile, jnp.full((1, LANES), 2 * CHUNK, jnp.int32)) for tile in range(tiles)]
    spots = lax.broadcasted_iota(jnp.int32, (CHUNK, LANES), 0) * 2 + plan.pupil // 2

    def fields(parity, ref):
        tilts = [tilted(tile, spots + parity) for tile in range(tiles)]
        for row in range(0, cells, CHUNK):
            here = slice(row, row + CHUNK)
            mask = mask_ref[parity, here, :]
            push = dir_ref[parity, here, :]
            turns = turn_ref[parity, here, :]
            flat_cos, flat_sin = wave(turns)
            flat_cos, flat_sin = flat_cos * mask, flat_sin * mask
            for tile in range(tiles):
                tilt_cos, tilt_sin = tilts[tile]
                cosine = flat_cos * tilt_cos - flat_sin * tilt_sin
                sine = flat_sin * tilt_cos + flat_cos * tilt_sin
                step_cos, step_sin = steps[tile]
                tilts[tile] = (
                    tilt_cos * step_cos - tilt_sin * step_sin,
                    tilt_sin * step_cos + tilt_cos * step_sin,
                )
                at = tile * LANES
                cos_ref[parity, here, at : at + LANES] = cosine
                sin_ref[parity, here, at : at + LANES] = sine
                put_split(ref, row, CHUNK, cells, at, cosine)
                put_split(ref, row, CHUNK, cells, wide + at, sine)
                put_split(ref, row, CHUNK, cells, 2 * wide + at, -sine * push)
                put_split(ref, row, CHUNK, cells, 3 * wide + at, cosine * push)

    def signals(parity, total):
        for row in range(0, cells, CHUNK):
            here = slice(row, row + CHUNK)
            push = dir_ref[parity, here, :]
            even_sum = odd_sum = shift = 0.0
            for tile in range(tiles):
                at = tile * LANES
                cosine = cos_ref[parity, here, at : at + LANES]
                sine = sin_ref[parity, here, at : at + LANES]
                image_cos, image_sin, push_real, push_imag = [
                    image_ref[parity, here, q * wide + at : q * wide + at + LANES] for q in range(4)
                ]
                even_sum += image_sin * push_imag + image_cos * push_real
                odd_sum += cosine * (push_imag - push * image_cos) - sine * (push_real + push * image_sin)
                shift += cosine * image_cos + sine * image_sin
            even_sum = lane_sum(even_sum, plan) * 2.0
            odd_sum = lane_sum(odd_sum, plan)
            signal_after, signal_before = even_sum + odd_sum, even_sum - odd_sum
            weighted_after = noise_ref[0, parity, here, :] * signal_after
            weighted_before = noise_ref[1, parity, here, :] * signal_before
            squares = weighted_after * signal_after + weighted_before * signal_before
            for r in range(0, CHUNK, SUB):
                total += squares[r : r + SUB]
            gap = (weighted_after - weighted_before) * 0.5
            weight_ref[0, parity, here, :] = weighted_after + weighted_before
            weight_ref[1, parity, here, :] = gap
            weight_ref[2, parity, here, :] = -gap * shift
        return total

    def image(parity, table, ref):
        image_ref[parity] = product(table, ref)

    fields(0, even_in_ref)
    fields(1, odd_in_ref)
    image(1, odd_ref, even_in_ref)
    image(0, even_ref, odd_in_ref)
    total = signals(1, jnp.zeros((SUB, LANES), jnp.float32))
    total = signals(0, total)
    total_ref[...] = total / plan.copies


def backward_kernel(plan, *refs):
    cos_ref, sin_ref, image_ref, weight_ref, even_ref, odd_ref, halo_ref, flow_ref, rim_ref, coef_ref, edge_ref = refs[:11]
    outs, prior_ref, (grad_ref, even_in_ref, odd_in_ref, back_ref) = refs[11:-5], refs[-5], refs[-4:]
    half, cells, shard, tiles, wide = plan.half, plan.cells, plan.shard, plan.tiles, plan.tiles * LANES
    me = place_on("mod")

    def fold(parity, ref):
        for row in range(0, cells, CHUNK):
            here = slice(row, row + CHUNK)
            both, gap = weight_ref[0, parity, here, :], weight_ref[1, parity, here, :]
            for tile in range(tiles):
                at = tile * LANES
                cosine = cos_ref[parity, here, at : at + LANES]
                sine = sin_ref[parity, here, at : at + LANES]
                image_cos = image_ref[parity, here, at : at + LANES]
                image_sin = image_ref[parity, here, wide + at : wide + at + LANES]
                put_split(ref, row, CHUNK, cells, at, gap * cosine + both * image_sin)
                put_split(ref, row, CHUNK, cells, wide + at, gap * sine - both * image_cos)

    def back(parity, table, ref):
        back_ref[parity] = product(table, ref)

    fold(0, even_in_ref)
    fold(1, odd_in_ref)
    back(1, even_ref, even_in_ref)
    back(0, odd_ref, odd_in_ref)
    lane = lax.broadcasted_iota(jnp.int32, (CHUNK, LANES), 1)
    for row in range(0, cells, CHUNK):
        here = slice(row, row + CHUNK)
        grads = []
        for parity in range(2):
            grad = weight_ref[2, parity, here, :]
            for tile in range(tiles):
                at = tile * LANES
                grad += cos_ref[parity, here, at : at + LANES] * back_ref[parity, here, at : at + LANES]
                grad += sin_ref[parity, here, at : at + LANES] * back_ref[parity, here, wide + at : wide + at + LANES]
            grads.append(lane_sum(grad, plan) * 2.0)
        grad_ref[here, :] = jnp.where(lane < plan.width, grads[0], grads[1])
    step, side = place_on("tm"), me % 2
    alone = jnp.where(side == 0, step == 0, step == lax.axis_size("tm") - 1)
    rows = [jnp.where(alone, 0.0, r) for r in (halo_ref[0:1, :], halo_ref[2 * shard - 1 : 2 * shard, :])]
    rows += [jnp.zeros((1, LANES), jnp.float32)] * (SUB - len(rows))
    tail = jnp.concatenate(rows, axis=0)
    def put(out, at, k):
        place = pl.ds(pl.multiple_of((me ^ k) * half, SUB), half)
        out[at : at + half, :] = grad_ref[place, :]
        out[at + half : at + half + SUB, :] = tail

    *even_outs, near_out = outs
    for k in range(0, plan.mods, 2):
        put(even_outs[k // 2], 0, k)
    for k in range(1, plan.mods, 2):
        put(near_out, (k // 2) * (half + SUB), k)
    prior_terms(plan, flow_ref, rim_ref, coef_ref, edge_ref, prior_ref)
    theirs = pl.ds(pl.multiple_of((1 - me % 2) * shard, SUB), shard)
    for f in range(plan.frames // 2):
        start = plan.mods // 2 * (half + SUB) + f * shard
        near_out[start : start + shard, :] = prior_ref[f, theirs, :]


def prior_terms(plan, flow_ref, rim_ref, coef_ref, edge_ref, prior_ref):
    reach = 2 * plan.shard
    row_id = lax.broadcasted_iota(jnp.int32, (reach, LANES), 0)

    def from_last(body, first):
        return jnp.where(row_id == 0, first, pltpu.roll(body, 1, 0))

    for t in range(plan.frames // 2):
        own, rim = flow_ref[t + 1], rim_ref[t : t + 1, :]
        ahead, both = [
            from_last(coef_ref[i] * own, edge_ref[i, SUB - 1 : SUB, :] * rim) for i in (1, 3)
        ]
        prior_ref[t] = flow_ref[t] - (coef_ref[0] * own + ahead + row_behind(coef_ref[2] * own + both))


def sum_kernel(*refs):
    total = refs[0][...]
    for ref in refs[1:-1]:
        total += ref[...]
    refs[-1][...] = jnp.broadcast_to(jnp.sum(total, axis=0, keepdims=True), total.shape)


def seal_kernel(plan, total_ref, *refs):
    size, count = plan.half + SUB, plan.mods // 2 - 1
    own, near_ref, outs = refs[:count], refs[count], refs[count + 1 :]
    for i, out in enumerate(outs):
        out[0:size, :] = own[i][...]
        out[plan.half + 2 : plan.half + 3, :] = total_ref[0:1, :]
        out[size : 2 * size, :] = near_ref[(i + 1) * size : (i + 2) * size, :]


def row_ahead(cells):
    lane = lax.broadcasted_iota(jnp.int32, cells.shape, 1)
    return jnp.where(lane == LANES - 1, 0.0, pltpu.roll(cells, LANES - 1, 1))


def row_behind(cells):
    lane = lax.broadcasted_iota(jnp.int32, cells.shape, 1)
    return jnp.where(lane == 0, 0.0, pltpu.roll(cells, 1, 1))


def shares(codes):
    ahead_x = ((codes & 3).astype(jnp.float32) + 0.5) / 4.0
    ahead_r = ((codes >> 2).astype(jnp.float32) + 0.5) / 4.0
    return (1.0 - ahead_x) * (1.0 - ahead_r), ahead_x * (1.0 - ahead_r), (1.0 - ahead_x) * ahead_r, ahead_x * ahead_r


def prior_kernel(plan, steps, *refs):
    mods, shard, frames = plan.mods, plan.shard, plan.frames
    pieces, refs = refs[: mods - 1], refs[mods - 1 :]
    pair_ref, halo_ref, coef_ref, edge_ref, data_ref, flow_ref, rim_ref, total_ref = refs
    me, step = place_on("mod"), place_on("tm")
    side, base, reach, held = me % 2, me - me % 2, 2 * shard, frames // 2
    first_frame, total_frames = step * frames + side * held, steps * frames
    zero_row = jnp.zeros((1, LANES), jnp.float32)

    alone = jnp.where(side == 0, step == 0, step == steps - 1)
    halo = jnp.where(alone, 0.0, halo_ref[...])
    cells, below, above = [], [], []
    for t in range(held + 2):
        frame = side * held + t - 1
        inside = (frame >= 0) & (frame < frames)
        cells.append(jnp.where(inside, pair_ref[jnp.clip(frame, 0, frames - 1)], halo))
        low, high = zero_row, zero_row
        for k in range(2, mods):
            source = me ^ k
            for f in range(frames):
                at = shard + 2 * f
                here = frame == f
                high = jnp.where((source == base + 2) & here, pieces[k - 1][at : at + 1, :], high)
                low = jnp.where((source == base - 1) & here, pieces[k - 1][at + 1 : at + 2, :], low)
        below.append(low)
        above.append(high)

    row_id = lax.broadcasted_iota(jnp.int32, (reach, LANES), 0)

    def from_next(body, last):
        return jnp.where(row_id == reach - 1, last, pltpu.roll(body, reach - 1, 0))

    coef = [coef_ref[i] for i in range(4)]
    edge = [edge_ref[i, SUB - 1 : SUB, :] for i in range(4)]

    def moved(share, base, ahead):
        return share[0] * base + share[1] * ahead + share[2] * row_ahead(base) + share[3] * row_ahead(ahead)

    flow, flow_edge = [], []
    for t in range(held + 1):
        frame = first_frame + t - 1
        valid = (frame >= 0) & (frame <= total_frames - 2)
        ahead = from_next(cells[t], above[t])
        flow.append(jnp.where(valid, cells[t + 1] - moved(coef, cells[t], ahead), 0.0))
        if t > 0:
            value = below[t + 1] - moved(edge, below[t], cells[t][0:1])
            flow_edge.append(jnp.where(valid & (me > 1), value, 0.0))
    total = data_ref[...]
    for t in range(held):
        square = flow[t + 1] * flow[t + 1]
        for r in range(0, reach, SUB):
            total += square[r : r + SUB]
    for t in range(held + 1):
        flow_ref[t] = flow[t]
    rim_ref[...] = jnp.concatenate(flow_edge + [zero_row] * (SUB - held), axis=0)
    total_ref[...] = total


def add_pieces(plan, me, pieces, hess_ref):
    half, width = plan.half, plan.width
    lane_group = lax.broadcasted_iota(jnp.int32, (half, LANES), 1) // width
    for k, piece, at in pieces:
        source = me ^ k
        frame, group = source // plan.groups, source % plan.groups
        for parity in range(2):
            own = pl.ds(parity, half, stride=2)
            cells = piece[at : at + half, :]
            if plan.copies == 2:
                moved = jnp.where(group == parity, cells, pltpu.roll(cells, width, 1))
            else:
                moved = pltpu.roll(cells, (group * width - parity * width + LANES) % LANES, 1)
            hess_ref[frame, own, :] += jnp.where(lane_group == group, moved, 0.0)


def begin_kernel(plan, own_ref, near_ref, prior_ref, hess_ref):
    shard, start = plan.shard, plan.mods // 2 * (plan.half + SUB)
    me = place_on("mod")
    side, held = me % 2, plan.frames // 2
    mine = pl.ds(pl.multiple_of(side * shard, SUB), shard)
    for f in range(held):
        hess_ref[side * held + f] = prior_ref[f, mine, :]
        hess_ref[(1 - side) * held + f] = near_ref[start + f * shard : start + (f + 1) * shard, :]
    add_pieces(plan, me, [(0, own_ref, 0), (1, near_ref, 0)], hess_ref)


def final_kernel(plan, entries, *refs):
    half, shard = plan.half, plan.shard
    size, pairs = half + SUB, plan.mods // 2
    begun_ref, far, sums = refs[0], refs[1:pairs], refs[pairs : 2 * pairs + 1]
    coef_ref, edge_ref, hess_ref, curvature_ref = refs[2 * pairs + 1 :]
    me = place_on("mod")
    side = me % 2
    pieces = [(2 * i + 2 + p, ref, p * size) for i, ref in enumerate(far) for p in range(2)]
    hess_ref[...] = begun_ref[...]
    add_pieces(plan, me, pieces, hess_ref)
    zero_row = jnp.zeros((1, LANES), jnp.float32)
    total, above, below = zero_row, zero_row, zero_row
    for ref in sums:
        total += ref[0:1, :]
    for ref in far:
        total += ref[half + 2 : half + 3, :]
    for k, piece, at in pieces:
        source, at = me ^ k, at + half
        above = jnp.where((source == me + 1) & (side == 1), piece[at : at + 1, :], above)
        below = jnp.where((source == me - 1) & (side == 0), piece[at + 1 : at + 2, :], below)
    last, top, rim = slice(shard - 1, shard), slice(2 * shard - 1, 2 * shard), slice(SUB - 1, SUB)
    hess_ref[0, last, :] -= coef_ref[1, top, :] * above + coef_ref[3, top, :] * row_ahead(above)
    hess_ref[plan.frames - 1, 0:1, :] -= edge_ref[1, rim, :] * below + row_behind(edge_ref[3, rim, :] * below)
    curvature_ref[0] = jnp.sum(total) / entries


def exchange(arrays, axis):
    count = lax.axis_size(axis)
    return [arrays[0]] + [
        lax.ppermute(arrays[k], axis, [(i, i ^ k) for i in range(count)]) for k in range(1, count)
    ]


def per_device(phase, direction, pupil_mask, mod_tilts, wind_codes, noise_weight):
    frames, shard, rows = phase.shape
    mods, steps = lax.axis_size("mod"), lax.axis_size("tm")
    plan = Plan(frames, shard, rows, mod_tilts.shape[0], mods)
    total_frames = frames * steps
    cells, wide = plan.cells, plan.tiles * LANES
    tables = [jnp.asarray(t) for t in roof_tables(plan)]
    pupil_mask, wind_codes, noise_weight, *tables = [
        pltpu.with_memory_space_constraint(array, pltpu.HBM)
        for array in (pupil_mask, wind_codes, noise_weight, *tables)
    ]

    def f32(*shape):
        return jax.ShapeDtypeStruct(shape, jnp.float32)

    def bf16(*shape):
        return jax.ShapeDtypeStruct(shape, jnp.bfloat16)

    def scratch(shape):
        return pltpu.VMEM(shape.shape, shape.dtype)

    def call(kernel, name, outs, in_specs, out_specs=None, scratch_shapes=(), aliases=None, work=0.02):
        return pl.pallas_call(
            kernel,
            out_shape=outs,
            in_specs=in_specs,
            out_specs=out_specs or [VMEM] * len(outs),
            scratch_shapes=list(scratch_shapes),
            input_output_aliases=aliases or {},
            compiler_params=params(),
            cost_estimate=pl.CostEstimate(
                flops=int(work * 1.1e9), bytes_accessed=int(work * 3.6e6), transcendentals=0
            ),
            name=name,
        )

    rows_in = shard + plan.extra
    tilts = jnp.broadcast_to(mod_tilts.astype(jnp.float32)[:, None], (plan.points, LANES))
    tilts = call(tilt_kernel, "tilts", [f32(plan.points, LANES)], [VMEM], work=0.8)(tilts)[0]
    *packed, direction_near = call(
        functools.partial(pack_kernel, plan),
        "pack",
        [f32(rows_in + (frames * shard if k == 1 else 0), LANES) for k in range(mods)] + [f32(*phase.shape)],
        [VMEM] * 3,
        work=0.3,
    )(tilts, phase, direction)
    pieces = exchange(packed, "mod")

    table = bf16(*tables[0].shape)
    mask, noise, coef, edge, even, odd, even_back, odd_back = call(
        functools.partial(prep_kernel, plan),
        "prepare",
        [f32(2, cells, LANES), f32(2, 2, cells, LANES), f32(4, 2 * shard, LANES), f32(4, SUB, LANES)]
        + [table] * 4,
        [VMEM] + [HBM] * 7,
        scratch_shapes=[
            pltpu.VMEM(pupil_mask.shape, jnp.int32),
            pltpu.VMEM(noise_weight.shape[1:], jnp.float32),
            pltpu.VMEM((2 * shard + SUB, LANES), jnp.int32),
            pltpu.SemaphoreType.DMA((8,)),
        ],
        work=1.5,
    )(packed[0], pupil_mask, noise_weight, wind_codes, *tables)

    pair, edge_frame = call(
        functools.partial(relay_kernel, plan),
        "relay",
        [f32(frames, 2 * shard, LANES), f32(2 * shard, LANES)],
        [VMEM] * 3,
        work=0.05,
    )(direction_near, pieces[1], edge)
    ends = [(t * mods + m, (t + 1) * mods + m - 1) for t in range(steps - 1) for m in range(1, mods, 2)]
    lone = [m for m in range(0, mods, 2)] + [(steps - 1) * mods + m for m in range(1, mods, 2)]
    if mods % 4 == 0:
        ends += [(a, a ^ 2) for a in lone if a & 2]
    else:
        ends += list(zip(lone[: mods // 2], lone[mods // 2 :]))
    halo = lax.ppermute(edge_frame, ("tm", "mod"), ends + [(b, a) for a, b in ends])

    cosine, sine, image, weights, data_total = call(
        functools.partial(forward_kernel, plan),
        "forward",
        [f32(2, cells, wide), f32(2, cells, wide), f32(2, cells, 4 * wide), f32(3, 2, cells, LANES), f32(SUB, LANES)],
        [VMEM] * (mods + 4),
        scratch_shapes=[
            scratch(s)
            for s in (f32(2, cells, LANES),) * 2 + (bf16(2 * cells, 4 * wide),) * 2
        ],
        work=2.8,
    )(*pieces, mask, noise, even, odd)

    flow, rim, total = call(
        functools.partial(prior_kernel, plan, steps),
        "prior",
        [f32(frames // 2 + 1, 2 * shard, LANES), f32(SUB, LANES), f32(SUB, LANES)],
        [VMEM] * (mods + 4),
        work=0.4,
    )(*pieces[1:], pair, halo, coef, edge, data_total)
    totals = [
        lax.ppermute(total, "tm", [(i, (i + k) % steps) for i in range(steps)]) for k in range(1, steps)
    ]

    size, pairs = plan.half + SUB, mods // 2
    *sent, near, prior = call(
        functools.partial(backward_kernel, plan),
        "backward",
        [f32(size, LANES)] * pairs
        + [f32(pairs * size + frames // 2 * shard, LANES), f32(frames // 2, 2 * shard, LANES)],
        [VMEM] * 11,
        scratch_shapes=[
            scratch(s)
            for s in (f32(cells, LANES),) + (bf16(2 * cells, 2 * wide),) * 2 + (f32(2, cells, 2 * wide),)
        ],
        work=0.8,
    )(cosine, sine, image, weights, even_back, odd_back, halo, flow, rim, coef, edge)

    def swap(array, k):
        return lax.ppermute(array, "mod", [(i, i ^ k) for i in range(mods)])

    near = swap(near, 1)
    total = call(sum_kernel, "sum", [f32(SUB, LANES)], [VMEM] * steps, work=3.0)(*totals, total)[0]
    joined = call(
        functools.partial(seal_kernel, plan),
        "seal",
        [f32(2 * size, LANES)] * (pairs - 1),
        [VMEM] * (pairs + 1),
    )(total, *sent[1:], near)
    far = [swap(array, 2 * k + 2) for k, array in enumerate(joined)]
    sums = [total] + [swap(total, k) for k in range(1, mods, 2)]

    begun = call(functools.partial(begin_kernel, plan), "begin", [f32(*phase.shape)], [VMEM] * 3, work=0.2)(
        sent[0], near, prior
    )[0]
    hess_vec, curvature = call(
        functools.partial(final_kernel, plan, float(total_frames * plan.pupil * rows)),
        "join",
        [f32(*phase.shape), f32(1)],
        [VMEM] * (2 * pairs + 3),
        out_specs=[VMEM, SMEM],
        work=0.8,
    )(begun, *far, *sums, coef, edge)
    return hess_vec, curvature


def solution(mesh):
    return jax.shard_map(
        per_device,
        mesh=mesh,
        in_specs=(
            P(("grp", "tm"), "mod", None),
            P(("grp", "tm"), "mod", None),
            P(),
            P("mod"),
            P("grp", None),
            P(("grp", "tm"), None, None),
        ),
        out_specs=(P(("grp", "tm"), "mod", None), P("grp")),
        check_vma=False,
    )
```
